32 devices in a mesh: img: 8 (over z, y), seq: 4 (over x, core).
Axes of the slice: x: 2, y: 2, z: 4, core: 2. Of those that a mesh axis runs over, the one named last changes fastest.
Arguments:
- tokens: bfloat16 [24, 1056, 768], P('img', 'seq'), may hold values from -6 to 6
- cotangent: bfloat16 [24, 1056, 768], P('img', 'seq'), may hold values from -6 to 6
- images_held: int32 [8], P('img'), may hold values from 2 to 3, as said below
- piece_rows: int32 [4], replicated, may hold values from 260 to 264, as said below
- norm_gain: bfloat16 [768], P('img'), may hold values from 0.5 to 1.5
- norm_shift: bfloat16 [768], P('img'), may hold values from -4 to 4
- qkv_weight: bfloat16 [768, 2304], P('img'), may hold values from -0.21875 to 0.21875
- qkv_bias: bfloat16 [1536], P('img'), may hold values from -0.75 to 0.75
- out_weight: bfloat16 [768, 768], P('img'), may hold values from -6 to 6
- out_bias: bfloat16 [768], P('img'), may hold values from -4 to 4
- mlp_gain: bfloat16 [768], P('img'), may hold values from 0.5 to 1.5
- mlp_shift: bfloat16 [768], P('img'), may hold values from -4 to 4
- up_weight: bfloat16 [768, 3072], P('img'), may hold values from -0.21875 to 0.21875
- up_bias: bfloat16 [3072], P('img'), may hold values from -4 to 4
- down_weight: bfloat16 [3072, 768], P('img'), may hold values from -0.109375 to 0.109375
- down_bias: bfloat16 [768], P('img'), may hold values from -4 to 4
Outputs:
- layer_out: bfloat16 [24, 1056, 768], P('img', 'seq')
- tokens_grad: float32 [24, 1056, 768], P('img', 'seq')
- grad_norm_gain: float32 [768], P('img')
- grad_norm_shift: float32 [768], P('img')
- grad_qkv_weight: float32 [768, 2304], P('img')
- grad_qkv_bias: float32 [1536], P('img')
- grad_out_weight: float32 [768, 768], P('img')
- grad_out_bias: float32 [768], P('img')
- grad_mlp_gain: float32 [768], P('img')
- grad_mlp_shift: float32 [768], P('img')
- grad_up_weight: float32 [768, 3072], P('img')
- grad_up_bias: float32 [3072], P('img')
- grad_down_weight: float32 [3072, 768], P('img')
- grad_down_bias: float32 [768], P('img')
The draws below stay inside these ranges and needn't reach their ends.
Inputs may be any that keep to these rules, and one draw needn't show every extreme that they name: `images_held`: every group holds 2 or 3 images; some group holds 3 and some group holds 2. `piece_rows`: one piece is full.
All inputs are finite; a program needn't handle non-finite values.
Results may differ from the reference program's by a relative error of at most 0.013.
Values may be sent and summed in bfloat16 or wider, within the bound.
No kernel may reach another device: no remote copies, remote signals or barrier semaphores. Data moves between devices by JAX's collectives and lax.ppermute only.
A program may use at most 192 MiB of HBM per device.

```python
from functools import partial
import jax
import jax.numpy as jnp
from jax import lax

D = 768
HEADS = 12
HEAD_DIM = 64
FF = 3072
SLOTS = 3
PIECE = 264
IMAGE_SLOTS = 24
SEQ_ROWS = 1056
N_IMG = 8
N_SEQ = 4


def draw_images_held(key, part):
    key = jax.random.fold_in(key, 11)
    first_key, second_key = jax.random.split(key)
    held_count = jax.random.randint(first_key, (N_IMG,), 2, 4)
    shuffled = jax.random.permutation(second_key, N_IMG)
    held_count = held_count.at[shuffled[0]].set(3).at[shuffled[1]].set(2)
    return held_count.astype(jnp.int32)


def draw_piece_rows(key, part):
    key = jax.random.fold_in(key, 23)
    first_key, second_key = jax.random.split(key)
    short_most = max(2, PIECE // 64)
    piece_fill = PIECE - jax.random.randint(first_key, (N_SEQ,), 0, short_most + 1)
    full_piece = jax.random.randint(second_key, (), 0, N_SEQ)
    piece_fill = jnp.where(jnp.arange(N_SEQ) == full_piece, PIECE, piece_fill)
    return piece_fill.astype(jnp.int32)


def block_scale(key, dims, pieces, smallest, top_value):
    def one(position, shards_of):
        draws = jax.random.uniform(jax.random.fold_in(jax.random.fold_in(key, 6), position), (shards_of,), jnp.float32, smallest / len(pieces), top_value / len(pieces))
        return jnp.repeat(jnp.exp(draws), dims[position] // shards_of).reshape((-1,) + (1,) * (len(dims) - position - 1))

    gain = one(*pieces[0])
    for cut in pieces[1:]:
        gain = gain * one(*cut)
    return gain


def noise(rng, dims, scale, most, cuts=(), dtype=jnp.bfloat16):
    values = scale * jax.random.normal(rng, dims, jnp.float32)
    if cuts:
        values = values * block_scale(rng, dims, cuts, -0.22, 0.18)
    return jnp.clip(values, -most, most).astype(dtype)


def setup_inputs(seed: int = 0) -> dict:
    streams_of = jax.random.split(jax.random.key(seed), 17)
    return {
        "tokens": noise(streams_of[0], (IMAGE_SLOTS, SEQ_ROWS, D), 1.0, 6.0, ((0, 8), (1, 4))),
        "cotangent": noise(streams_of[1], (IMAGE_SLOTS, SEQ_ROWS, D), 1.0, 6.0, ((0, 8), (1, 4))),
        "images_held": draw_images_held(jax.random.fold_in(streams_of[16], 71), 0),
        "piece_rows": draw_piece_rows(jax.random.fold_in(streams_of[16], 71), 0),
        "norm_gain": jnp.clip(1.0 + 0.1 * jax.random.normal(streams_of[4], (D,), jnp.float32), 0.5, 1.5).astype(jnp.bfloat16),
        "norm_shift": noise(streams_of[5], (D,), 0.3, 4.0, ((0, 8),)),
        "qkv_weight": noise(streams_of[6], (D, 3 * D), D ** -0.5, 0.21875, ((0, 8),)),
        "qkv_bias": noise(streams_of[7], (2 * D,), 0.05, 0.75, ((0, 8),)),
        "out_weight": noise(streams_of[8], (D, D), (max(1, D // SEQ_ROWS)) ** -0.5, 6.0, ((0, 8),)),
        "out_bias": noise(streams_of[9], (D,), 0.3, 4.0, ((0, 8),)),
        "mlp_gain": jnp.clip(1.0 + 0.1 * jax.random.normal(streams_of[10], (D,), jnp.float32), 0.5, 1.5).astype(jnp.bfloat16),
        "mlp_shift": noise(streams_of[11], (D,), 0.3, 4.0, ((0, 8),)),
        "up_weight": noise(streams_of[12], (D, FF), D ** -0.5, 0.21875, ((0, 8),)),
        "up_bias": noise(streams_of[13], (FF,), 0.3, 4.0, ((0, 8),)),
        "down_weight": noise(streams_of[14], (FF, D), FF ** -0.5, 0.109375, ((0, 8),)),
        "down_bias": noise(streams_of[15], (D,), 0.3, 4.0, ((0, 8),)),
    }


EPS = 1e-06
NEG = -1e+30

@jax.custom_vjp
def low(v):
    return lax.optimization_barrier(v.astype(jnp.bfloat16)).astype(jnp.float32)

@jax.custom_vjp
def low_back(v):
    return v

def low_keep(v):
    return (low(v), None)

def low_pass(kept, grad):
    return (grad,)

def back_keep(v):
    return (v, None)

def back_low(kept, grad):
    return (low(grad),)
low.defvjp(low_keep, low_pass)
low_back.defvjp(back_keep, back_low)

def product(left_side, right_side):
    return jnp.einsum('...d,de->...e', left_side, right_side, precision=lax.Precision.HIGHEST)

def layer_norm(features, gain_vec, shift_vec):
    row_mean = lax.optimization_barrier(jnp.mean(features, axis=-1, keepdims=True))
    centred = features - row_mean
    spread = lax.optimization_barrier(jnp.mean(centred * centred, axis=-1, keepdims=True))
    return centred * lax.rsqrt(spread + EPS) * gain_vec + shift_vec

def full_bias(pair_bias):
    paired = pair_bias.reshape(HEADS, 2, HEAD_DIM)
    zero_keys = jnp.zeros((HEADS, 1, HEAD_DIM), jnp.float32)
    return jnp.concatenate([paired[:, :1], zero_keys, paired[:, 1:]], axis=1).reshape(3 * D)

def attend(slot_block, key_valid):
    queries = slot_block[:, :, 0]
    key_rows = slot_block[:, :, 1]
    values = slot_block[:, :, 2]
    scores = jnp.einsum('qhd,khd->hqk', queries, key_rows, precision=lax.Precision.HIGHEST) * HEAD_DIM ** (-0.5)
    scores = low_back(scores)
    scores = jnp.where(key_valid[None, None, :], scores, NEG)
    attn_probs = low(jax.nn.softmax(scores, axis=-1))
    attended = jnp.einsum('hqk,khd->qhd', attn_probs, values, precision=lax.Precision.HIGHEST)
    return low_back(low(attended))

def forward(params, block_tokens, row_mask, key_valid):
    norm_gain, norm_shift, qkv_weight, qkv_bias, out_weight, out_bias, mlp_gain, mlp_shift, up_weight, up_bias, down_weight, down_bias = params
    slot_count = block_tokens.shape[0]
    seq_rows = block_tokens.shape[1]
    normed = low(layer_norm(block_tokens, norm_gain, norm_shift))
    qkv_rows = low_back(low(product(normed, qkv_weight) + full_bias(qkv_bias)))
    qkv_rows = qkv_rows.reshape(slot_count, seq_rows, HEADS, 3, HEAD_DIM)
    attended = lax.map(jax.checkpoint(partial(attend, key_valid=key_valid)), qkv_rows)
    attended = attended.reshape(slot_count, seq_rows, D)
    branch = low_back(product(attended, out_weight) + out_bias)
    residual = block_tokens + branch
    normed_mlp = low(layer_norm(residual, mlp_gain, mlp_shift))
    hidden_pre = low_back(product(normed_mlp, up_weight) + up_bias)
    activated = low(jax.nn.gelu(hidden_pre, approximate=False))
    output = residual + product(activated, down_weight) + down_bias
    return output * row_mask[..., None]

def reference(tokens, cotangent, images_held, piece_rows, norm_gain, norm_shift, qkv_weight, qkv_bias, out_weight, out_bias, mlp_gain, mlp_shift, up_weight, up_bias, down_weight, down_bias):
    params = tuple((weight.astype(jnp.float32) for weight in (norm_gain, norm_shift, qkv_weight, qkv_bias, out_weight, out_bias, mlp_gain, mlp_shift, up_weight, up_bias, down_weight, down_bias)))
    seq_rows = N_SEQ * PIECE
    key_valid = (jnp.arange(PIECE)[None, :] < piece_rows[:, None]).reshape(seq_rows)
    groups = tokens.reshape(N_IMG, SLOTS, seq_rows, D)
    group_cots = cotangent.reshape(N_IMG, SLOTS, seq_rows, D)

    def group_step(totals, group_items):
        group_tokens, group_cot, held_count = group_items
        live_slots = jnp.arange(SLOTS) < held_count
        row_mask = (live_slots[:, None] & key_valid[None, :]).astype(jnp.float32)

        def apply_layer(layer_params, layer_input):
            return forward(layer_params, layer_input, row_mask, key_valid)
        outputs, pullback = jax.vjp(apply_layer, params, group_tokens.astype(jnp.float32))
        param_grads, input_grad = pullback(group_cot.astype(jnp.float32))
        totals = jax.tree.map(jnp.add, totals, param_grads)
        return (totals, (outputs.astype(jnp.bfloat16), input_grad))
    start_totals = jax.tree.map(jnp.zeros_like, params)
    totals, (outputs, input_grads) = lax.scan(group_step, start_totals, (groups, group_cots, images_held))
    layer_out = outputs.reshape(IMAGE_SLOTS, seq_rows, D)
    tokens_grad = input_grads.reshape(IMAGE_SLOTS, seq_rows, D)
    return (layer_out, tokens_grad, totals[0], totals[1], totals[2], totals[3], totals[4], totals[5], totals[6], totals[7], totals[8], totals[9], totals[10], totals[11])
```

```python
from functools import partial

import jax
import jax.numpy as jnp
from jax import lax
from jax.sharding import PartitionSpec as P

D = 768
HEADS = 12
HEAD_DIM = 64


EPS = 1e-06
NEG = -1e30


def layer_norm(features, gain_vec, shift_vec):
    row_mean = jnp.mean(features, axis=-1, keepdims=True)
    centred = features - row_mean
    spread = jnp.mean(centred * centred, axis=-1, keepdims=True)
    return centred * lax.rsqrt(spread + EPS) * gain_vec + shift_vec

def xor_send(block, axis, bits):
    n = lax.axis_size(axis)
    return lax.ppermute(block, axis, [(i, i ^ bits) for i in range(n)])


def img_shape():
    n = lax.axis_size("img")
    return n // 2, 2


def ring_perm():
    outer, inner = img_shape()
    return [
        (z * inner + y, ((z + 1) % outer) * inner + y) for z in range(outer) for y in range(inner)
    ]


def small_axis():
    return lax.axis_size("img") <= 16


def pair_up(block, bits):
    other = xor_send(block, "img", bits)
    first = (lax.axis_index("img") & bits) == 0
    return jnp.where(first, jnp.stack([block, other]), jnp.stack([other, block]))


def ring_gather(block):
    outer, inner = img_shape()
    z = lax.axis_index("img") // inner
    gathered = jnp.zeros((outer,) + block.shape, block.dtype)
    moving = block
    for step in range(outer):
        owner = (z + outer - step) % outer
        gathered = lax.dynamic_update_slice_in_dim(gathered, moving[None], owner, 0)
        if step < outer - 1:
            moving = lax.ppermute(moving, "img", ring_perm())
    return gathered


def gather_img(block, inner_first=True):
    n = lax.axis_size("img")
    if not small_axis():
        return lax.all_gather(block, "img", axis=0)
    if inner_first:
        return ring_gather(pair_up(block, 1)).reshape((n,) + block.shape)
    both = pair_up(ring_gather(block), 1)
    return jnp.swapaxes(both, 0, 1).reshape((n,) + block.shape)


def ring_reduce(parts):
    outer, inner = img_shape()
    z = lax.axis_index("img") // inner

    def part(step):
        return lax.dynamic_index_in_dim(parts, (z + 2 * outer - step) % outer, 0, keepdims=False)

    total = part(1)
    for step in range(1, outer):
        arrived = lax.ppermute(total.astype(jnp.bfloat16), "img", ring_perm())
        total = arrived.astype(jnp.float32) + part(step + 1).astype(jnp.float32)
    return total


def pair_reduce(parts):
    me = lax.axis_index("img") & 1
    keep = lax.dynamic_index_in_dim(parts, me, 0, keepdims=False)
    send = lax.dynamic_index_in_dim(parts, 1 - me, 0, keepdims=False)
    arrived = xor_send(send.astype(jnp.bfloat16), "img", 1)
    return keep.astype(jnp.float32) + arrived.astype(jnp.float32)


def reduce_img(parts, inner_first=True):
    if not small_axis():
        return lax.psum_scatter(
            parts.astype(jnp.bfloat16), "img", scatter_dimension=0, tiled=False
        ).astype(jnp.float32)
    outer, inner = img_shape()
    split = parts.reshape((outer, inner) + parts.shape[1:])
    if inner_first:
        return ring_reduce(pair_reduce(jnp.swapaxes(split, 0, 1)))
    return pair_reduce(ring_reduce(split))


def all_sum(vector):
    axes = (("seq", 1), ("seq", 2)) + tuple(
        ("img", 1 << k) for k in range(lax.axis_size("img").bit_length() - 1)
    )
    for axis, bits in axes:
        vector = vector + xor_send(vector, axis, bits)
    return vector


def halves(mine, axis):
    first = (lax.axis_index("seq") & 1) == 0
    other = xor_send(mine, "seq", 1)
    return jnp.where(
        first,
        jnp.concatenate([mine, other], axis),
        jnp.concatenate([other, mine], axis),
    )


def half_of(block, axis, which):
    size = block.shape[axis] // 2
    return lax.dynamic_slice_in_dim(block, which * size, size, axis)


def finish_halves(total, axis):
    low = total.astype(jnp.bfloat16)
    low = (low.astype(jnp.float32) + xor_send(low, "seq", 2).astype(jnp.float32)).astype(
        jnp.bfloat16
    )
    return halves(low, axis).astype(jnp.float32)


def half_reduce(grad, axis):
    me = lax.axis_index("seq") & 1
    arrived = xor_send(half_of(grad, axis, 1 - me).astype(jnp.bfloat16), "seq", 1)
    return half_of(grad, axis, me).astype(jnp.float32) + arrived.astype(jnp.float32)


def attend_forward(qkv_rows, key_valid, score_scale):
    heads_here = qkv_rows.shape[1] // (3 * HEAD_DIM)
    cols = qkv_rows.reshape(-1, heads_here, 3, HEAD_DIM)
    scores = (
        jnp.einsum("qhd,khd->hqk", cols[:, :, 0], cols[:, :, 1], preferred_element_type=jnp.float32)
        * score_scale
    )
    scores = jnp.where(key_valid[None, None, :], scores, NEG)
    probs = jax.nn.softmax(scores, axis=-1).astype(jnp.bfloat16)
    attended = jnp.einsum("hqk,khd->qhd", probs, cols[:, :, 2], preferred_element_type=jnp.float32)
    return attended.astype(jnp.bfloat16).reshape(qkv_rows.shape[0], -1)


def attend_backward(qkv_rows, grad_attended, key_valid, score_scale):
    heads_here = qkv_rows.shape[1] // (3 * HEAD_DIM)
    cols = qkv_rows.reshape(-1, heads_here, 3, HEAD_DIM)
    grads = grad_attended.reshape(-1, heads_here, HEAD_DIM)
    scores = (
        jnp.einsum("qhd,khd->hqk", cols[:, :, 0], cols[:, :, 1], preferred_element_type=jnp.float32)
        * score_scale
    )
    scores = jnp.where(key_valid[None, None, :], scores, NEG)
    probs = jax.nn.softmax(scores, axis=-1)
    grad_probs = jnp.einsum("qhd,khd->hqk", grads, cols[:, :, 2], preferred_element_type=jnp.float32)
    inner = jnp.sum(probs * grad_probs, axis=-1, keepdims=True)
    grad_scores = (probs * (grad_probs - inner)).astype(jnp.bfloat16)
    grad_q = score_scale * jnp.einsum(
        "hqk,khd->qhd", grad_scores, cols[:, :, 1], preferred_element_type=jnp.float32
    )
    grad_k = score_scale * jnp.einsum(
        "hqk,qhd->khd", grad_scores, cols[:, :, 0], preferred_element_type=jnp.float32
    )
    grad_v = jnp.einsum(
        "hqk,qhd->khd", probs.astype(jnp.bfloat16), grads, preferred_element_type=jnp.float32
    )
    return jnp.stack([grad_q, grad_k, grad_v], axis=2).astype(jnp.bfloat16).reshape(qkv_rows.shape)


def local(
    tokens,
    cotangent,
    images_held,
    piece_rows,
    norm_gain,
    norm_shift,
    qkv_weight,
    qkv_bias,
    out_weight,
    out_bias,
    mlp_gain,
    mlp_shift,
    up_weight,
    up_bias,
    down_weight,
    down_bias,
):
    slot_count, piece_size, model_width = tokens.shape
    n_seq = lax.axis_size("seq")
    n_img = lax.axis_size("img")
    me = lax.axis_index("seq")
    own_img = lax.axis_index("img")
    row_count = slot_count * piece_size
    heads_here = HEADS // n_seq
    group = 3 * D // n_seq
    shard = D // n_img
    score_scale = HEAD_DIM ** (-0.5)

    pieces = me ^ jnp.arange(n_seq)
    rows_of = piece_rows[pieces]
    key_valid = (jnp.arange(piece_size)[None, :] < rows_of[:, None]).reshape(n_seq * piece_size)
    own_valid = key_valid[:piece_size]
    live_slots = jnp.arange(slot_count) < images_held[0]
    valid_rows = (live_slots[:, None] & own_valid[None, :]).reshape(row_count)

    slot_tokens = []
    for slot in range(slot_count):
        own = tokens[slot]
        pair = xor_send(own, "seq", 1)
        across = xor_send(own, "seq", 2)
        slot_tokens.append([own, pair, across, xor_send(across, "seq", 1)])
    small = jnp.concatenate(
        [norm_gain, norm_shift, out_bias, mlp_gain, mlp_shift, down_bias, qkv_bias, up_bias]
    )
    small_rows = -(-small.shape[0] // group)
    small_rows = -(-small_rows // 16) * 16
    small = jnp.pad(small, (0, small_rows * group - small.shape[0])).reshape(small_rows, group)
    my_columns = lax.dynamic_slice_in_dim(qkv_weight, me * group, group, 1)
    first_set = gather_img(jnp.concatenate([my_columns, small], axis=0))
    qkv_cols = first_set[:, :shard].reshape(model_width, group)
    params = first_set[:, shard:].reshape(n_img, -1).astype(jnp.float32)

    def param(start, width):
        return params[:, start * shard : (start + width) * shard].reshape(-1)

    gain_first, shift_first, bias_out = param(0, 1), param(1, 1), param(2, 1)
    gain_second, shift_second, bias_down = param(3, 1), param(4, 1), param(5, 1)
    pair_bias, bias_up = param(6, 2), param(8, 4)
    paired = lax.dynamic_slice_in_dim(
        pair_bias.reshape(HEADS, 2, HEAD_DIM), me * heads_here, heads_here, 0
    )
    bias_qkv = jnp.concatenate(
        [paired[:, :1], jnp.zeros((heads_here, 1, HEAD_DIM), jnp.float32), paired[:, 1:]], axis=1
    ).reshape(group)

    pair_me = me & 1
    half_up = gather_img(
        jnp.concatenate([half_of(up_weight, 1, pair_me), half_of(out_weight, 1, pair_me)], axis=1),
        inner_first=False,
    ).reshape(model_width, -1)
    half_down = gather_img(half_of(down_weight, 1, pair_me)).reshape(-1, model_width // 2)
    ff = up_weight.shape[1]
    up_full = halves(half_up[:, : ff // 2], 1)
    out_full = halves(half_up[:, ff // 2 :], 1)
    down_full = halves(half_down, 1)

    inputs = tokens.reshape(row_count, model_width).astype(jnp.float32)
    slot_normed, slot_qkv, slot_attended = [], [], []
    for slot in range(slot_count):
        rows = jnp.concatenate(slot_tokens[slot], axis=0).astype(jnp.float32)
        normed = layer_norm(rows, gain_first, shift_first).astype(jnp.bfloat16)
        qkv_rows = (
            jnp.dot(normed, qkv_cols, preferred_element_type=jnp.float32) + bias_qkv
        ).astype(jnp.bfloat16)
        attended = attend_forward(qkv_rows, key_valid, score_scale).reshape(
            n_seq, piece_size, -1
        )
        slot_normed.append(normed)
        slot_qkv.append(qkv_rows)
        slot_attended.append(
            [attended[0]] + [xor_send(attended[r], "seq", r) for r in range(1, n_seq)]
        )

    group_width = heads_here * HEAD_DIM
    out_rel = [
        lax.dynamic_slice_in_dim(out_full, (me ^ r) * group_width, group_width, 0)
        for r in range(n_seq)
    ]
    out_rel = jnp.concatenate(out_rel, axis=0)
    attended_tokens = jnp.concatenate(
        [jnp.concatenate(parts, axis=1) for parts in slot_attended], axis=0
    )
    residual = (
        inputs + jnp.dot(attended_tokens, out_rel, preferred_element_type=jnp.float32) + bias_out
    )

    normed_mlp = layer_norm(residual, gain_second, shift_second).astype(jnp.bfloat16)
    hidden_pre = jnp.dot(normed_mlp, up_full, preferred_element_type=jnp.float32) + bias_up
    gelu_out, gelu_back = jax.vjp(partial(jax.nn.gelu, approximate=False), hidden_pre)
    activated = gelu_out.astype(jnp.bfloat16)
    output = residual + jnp.dot(activated, down_full, preferred_element_type=jnp.float32) + bias_down
    layer_out = (
        jnp.where(valid_rows[:, None], output, 0.0)
        .astype(jnp.bfloat16)
        .reshape(slot_count, piece_size, model_width)
    )
    grad_out = jnp.where(
        valid_rows[:, None], cotangent.reshape(row_count, model_width), jnp.zeros((), jnp.bfloat16)
    )
    grad_act = jnp.einsum("rd,fd->rf", grad_out, down_full, preferred_element_type=jnp.float32)
    grad_hidden = gelu_back(grad_act)[0].astype(jnp.bfloat16)
    grad_norm_in = jnp.einsum("rf,df->rd", grad_hidden, up_full, preferred_element_type=jnp.float32)
    second_norm, second_back = jax.vjp(layer_norm, residual, gain_second, shift_second)
    grad_resid_norm, grad_mlp_gain, grad_mlp_shift = second_back(grad_norm_in)
    grad_residual = grad_out.astype(jnp.float32) + grad_resid_norm
    grad_branch = grad_residual.astype(jnp.bfloat16)
    grad_attended = jnp.einsum(
        "re,de->rd", grad_branch, out_rel, preferred_element_type=jnp.float32
    ).astype(jnp.bfloat16)
    grad_attended = grad_attended.reshape(slot_count, piece_size, n_seq, group_width)
    slot_grads = []
    for slot in range(slot_count):
        slot_grads.append(
            jnp.concatenate(
                [grad_attended[slot, :, 0]]
                + [xor_send(grad_attended[slot, :, r], "seq", r) for r in range(1, n_seq)],
                axis=0,
            )
        )

    grad_down_weight = jnp.einsum(
        "rf,rd->fd", activated, grad_out, preferred_element_type=jnp.float32
    )
    grad_up_weight = jnp.einsum(
        "rd,rf->df", normed_mlp, grad_hidden, preferred_element_type=jnp.float32
    )
    grad_out_rel = jnp.einsum(
        "rd,re->de", attended_tokens, grad_branch, preferred_element_type=jnp.float32
    ).reshape(n_seq, group_width, model_width)
    grad_out_weight = jnp.concatenate(
        [lax.dynamic_index_in_dim(grad_out_rel, me ^ r, 0, keepdims=False) for r in range(n_seq)],
        axis=0,
    )
    part_up = half_reduce(grad_up_weight, 1)
    part_out = half_reduce(grad_out_weight, 1)
    part_down = half_reduce(grad_down_weight, 1)
    own_up = reduce_img(
        jnp.concatenate([part_up, part_out], axis=1).reshape(n_img, shard, -1), inner_first=False
    )
    own_down = reduce_img(part_down.reshape(n_img, ff // n_img, -1))
    share_up = finish_halves(own_up[:, : ff // 2], 1)
    share_out = finish_halves(own_up[:, ff // 2 :], 1)
    share_down = finish_halves(own_down, 1)

    grad_down_bias = jnp.sum(grad_out.astype(jnp.float32), axis=0)
    grad_up_bias = jnp.sum(grad_hidden.astype(jnp.float32), axis=0)
    grad_out_bias = jnp.sum(grad_branch.astype(jnp.float32), axis=0)

    grad_columns = jnp.zeros((model_width, group), jnp.float32)
    bias_sums = jnp.zeros((group,), jnp.float32)
    own_sums = []
    for slot in range(slot_count):
        grad_qkv = attend_backward(slot_qkv[slot], slot_grads[slot], key_valid, score_scale)
        partial_in = jnp.einsum(
            "re,de->rd", grad_qkv, qkv_cols, preferred_element_type=jnp.float32
        ).reshape(n_seq, piece_size, model_width)
        low = partial_in.astype(jnp.bfloat16)
        pair = xor_send(low[1], "seq", 1).astype(jnp.float32)
        across = xor_send(low[3], "seq", 1).astype(jnp.float32)
        across = xor_send((partial_in[2] + across).astype(jnp.bfloat16), "seq", 2)
        own_sums.append(partial_in[0] + pair + across.astype(jnp.float32))
        grad_columns += jnp.einsum(
            "rd,re->de", slot_normed[slot], grad_qkv, preferred_element_type=jnp.float32
        )
        bias_sums += jnp.sum(grad_qkv.astype(jnp.float32), axis=0)
    grad_norm_first = jnp.concatenate(own_sums, axis=0)
    first_norm, first_back = jax.vjp(layer_norm, inputs, gain_first, shift_first)
    grad_inputs_norm, grad_norm_gain, grad_norm_shift = first_back(grad_norm_first)
    tokens_grad = (grad_residual + grad_inputs_norm).reshape(slot_count, piece_size, model_width)

    own_columns = reduce_img(grad_columns.reshape(n_img, shard, group)).astype(jnp.bfloat16)
    by_sender = [own_columns] + [xor_send(own_columns, "seq", r) for r in range(1, n_seq)]
    by_sender = jnp.stack(by_sender)
    share_qkv = jnp.concatenate(
        [lax.dynamic_index_in_dim(by_sender, me ^ g, 0, keepdims=False) for g in range(n_seq)],
        axis=1,
    ).astype(jnp.float32)

    bias_sums = bias_sums.reshape(heads_here, 3, HEAD_DIM)
    grad_pairs = jnp.concatenate([bias_sums[:, :1], bias_sums[:, 2:]], axis=1).reshape(-1)
    grad_pairs = lax.dynamic_update_slice_in_dim(
        jnp.zeros((2 * D,), jnp.float32), grad_pairs, me * grad_pairs.shape[0], 0
    )
    vectors = [
        grad_norm_gain,
        grad_norm_shift,
        grad_pairs,
        grad_out_bias,
        grad_mlp_gain,
        grad_mlp_shift,
        grad_up_bias,
        grad_down_bias,
    ]
    totals = all_sum(jnp.concatenate([v.reshape(n_img, -1) for v in vectors], axis=1))
    mine = lax.dynamic_index_in_dim(totals, own_img, 0, keepdims=False)
    shares, at = [], 0
    for v in vectors:
        size = v.shape[0] // n_img
        shares.append(mine[at : at + size])
        at += size
    return (
        layer_out,
        tokens_grad,
        shares[0],
        shares[1],
        share_qkv,
        shares[2],
        share_out,
        shares[3],
        shares[4],
        shares[5],
        share_up,
        shares[6],
        share_down,
        shares[7],
    )


def solution(mesh):
    placed = (
        P("img", "seq", None),
        P("img", "seq", None),
        P("img"),
        P(),
        P("img"),
        P("img"),
        P("img", None),
        P("img"),
        P("img", None),
        P("img"),
        P("img"),
        P("img"),
        P("img", None),
        P("img"),
        P("img", None),
        P("img"),
    )
    return jax.shard_map(
        local,
        mesh=mesh,
        in_specs=placed,
        out_specs=(
            P("img", "seq", None),
            P("img", "seq", None),
            P("img"),
            P("img"),
            P("img", None),
            P("img"),
            P("img", None),
            P("img"),
            P("img"),
            P("img"),
            P("img", None),
            P("img"),
            P("img", None),
            P("img"),
        ),
        check_vma=False,
    )
```

```python
from functools import partial

import jax
import jax.numpy as jnp
import numpy as np
from jax import lax
from jax.experimental import pallas as pl
from jax.experimental.pallas import tpu as pltpu
from jax.sharding import PartitionSpec as P

D = 768
HEADS = 12
HEAD_DIM = 64
EPS = 1e-06
NEG = -1e30
LANES = 128
F32 = jnp.float32
BF16 = jnp.bfloat16
VMEM_BYTES = 60 * 1024 * 1024


def mm(left, right, left_dim=1, right_dim=0):
    return lax.dot_general(
        left, right, (((left_dim,), (right_dim,)), ((), ())), preferred_element_type=F32
    )


def normalize(features):
    row_mean = jnp.mean(features, axis=-1, keepdims=True)
    centred = features - row_mean
    spread = jnp.mean(centred * centred, axis=-1, keepdims=True)
    factor = lax.rsqrt(spread + EPS)
    return centred * factor, factor


def round_up(size, unit):
    return -(-size // unit) * unit


def head_columns(heads, parts):
    place = np.zeros((heads * parts, LANES, heads * parts * HEAD_DIM), np.float32)
    for b in range(heads * parts):
        for d in range(HEAD_DIM):
            place[b, d, b * HEAD_DIM + d] = 1.0
    return jnp.asarray(place, BF16)


def query_block(rows):
    for size in range(min(rows, 400) // 16 * 16, 15, -16):
        if rows % size == 0:
            return size
    return rows


def forward_kernel(n_seq, heads, n_after, *refs):
    tokens, refs = refs[:n_seq], refs[:n_seq] + refs[n_seq + n_after :]
    gain, shift, weight, bias, key_mask, place = refs[n_seq : n_seq + 6]
    normed_out, qkv_out, attended_out, rows, attended = refs[n_seq + 6 :]
    piece = tokens[0].shape[0]
    total = n_seq * piece
    for r in range(n_seq):
        unit, _ = normalize(tokens[r][...].astype(F32))
        rows[r * piece : (r + 1) * piece, :] = unit * gain[...] + shift[...]
    normed = rows[...].astype(BF16)
    normed_out[...] = normed
    block = query_block(total)
    pad = qkv_out.shape[1] - total
    for h in range(heads):
        parts = []
        for t in range(3):
            b = 3 * h + t
            part = mm(normed, weight[b]) + bias[b]
            if t == 1:
                part = part + key_mask[...]
            part = part.astype(BF16)
            qkv_out[b, :total] = part
            if pad:
                qkv_out[b, total:] = jnp.zeros((pad, LANES), BF16)
            parts.append(part)
        queries, keys, values = parts
        for at in range(0, total, block):
            scores = mm(queries[at : at + block], keys, 1, 1)
            peak = jnp.max(scores, axis=-1, keepdims=True)
            terms = jnp.exp(scores - peak).astype(BF16)
            weighted = mm(terms, values)
            result = (weighted / weighted[:, HEAD_DIM : HEAD_DIM + 1]).astype(BF16)
            placed = mm(result, place[h])
            if h:
                placed = placed + attended[at : at + block, :]
            attended[at : at + block, :] = placed
    for r in range(n_seq):
        attended_out[r] = attended[r * piece : (r + 1) * piece, :].astype(BF16)


def after_specs(after):
    return [pl.BlockSpec(memory_space=pl.ANY)] * len(after)


def whole_specs(count):
    return [pl.BlockSpec(memory_space=pltpu.VMEM)] * count


def slot_forward(pieces, gain, shift, weight, bias, key_mask, after=()):
    n_seq = len(pieces)
    piece, width = pieces[0].shape
    heads = weight.shape[0] // 3
    total = n_seq * piece
    padded = round_up(total, LANES)
    return pl.pallas_call(
        partial(forward_kernel, n_seq, heads, len(after)),
        in_specs=whole_specs(n_seq) + after_specs(after) + whole_specs(6),
        out_shape=(
            jax.ShapeDtypeStruct((total, width), BF16),
            jax.ShapeDtypeStruct((3 * heads, padded, LANES), BF16),
            jax.ShapeDtypeStruct((n_seq, piece, heads * HEAD_DIM), BF16),
        ),
        scratch_shapes=[
            pltpu.VMEM((total, width), F32),
            pltpu.VMEM((total, heads * HEAD_DIM), F32),
        ],
        compiler_params=pltpu.CompilerParams(vmem_limit_bytes=VMEM_BYTES),
        cost_estimate=pl.CostEstimate(
            flops=20 * 10**9, bytes_accessed=12 * 10**6, transcendentals=heads * total * total
        ),
        name="slot_forward",
    )(*pieces, *after, gain, shift, weight, bias, key_mask, head_columns(heads, 1))


def backward_kernel(n_seq, heads, n_after, *refs):
    grads, refs = refs[:n_seq], refs[:n_seq] + refs[n_seq + n_after :]
    qkv, place, spread = refs[n_seq : n_seq + 3]
    grad_out, rows, total_grad = refs[n_seq + 3 :]
    piece = grads[0].shape[0]
    total = n_seq * piece
    padded = qkv.shape[1]
    for r in range(n_seq):
        rows[r * piece : (r + 1) * piece, :] = grads[r][...].astype(F32)
    if padded > total:
        rows[total:, :] = jnp.zeros((padded - total, rows.shape[1]), F32)
    grad_rows = rows[...].astype(BF16)
    block = 3 * LANES if padded % (3 * LANES) == 0 else LANES
    for h in range(heads):
        grad_head = mm(grad_rows, place[h], 1, 1).astype(BF16)
        queries = qkv[3 * h]
        keys = qkv[3 * h + 1, :total]
        values = qkv[3 * h + 2, :total]
        keys_t = jnp.transpose(qkv[3 * h + 1])[:, :total]
        grad_keys = jnp.zeros((total, LANES), F32)
        grad_values = jnp.zeros((total, LANES), F32)
        grad_queries = []
        for at in range(0, padded, block):
            query_part = queries[at : at + block]
            grad_part = grad_head[at : at + block]
            scores = mm(keys, query_part, 1, 1)
            peak = jnp.max(scores, axis=0, keepdims=True)
            terms = jnp.exp(scores - peak)
            probs = terms * (1.0 / jnp.sum(terms, axis=0, keepdims=True))
            grad_probs = mm(values, grad_part, 1, 1)
            inner = jnp.sum(probs * grad_probs, axis=0, keepdims=True)
            grad_scores = (probs * (grad_probs - inner)).astype(BF16)
            grad_values = grad_values + mm(probs.astype(BF16), grad_part)
            grad_keys = grad_keys + mm(grad_scores, query_part)
            grad_queries.append(jnp.transpose(mm(keys_t, grad_scores)))
        grad_queries = jnp.concatenate(grad_queries, axis=0)[:total] * (HEAD_DIM**-0.5)
        for t, part in enumerate((grad_queries, grad_keys, grad_values)):
            placed = mm(part.astype(BF16), spread[3 * h + t])
            if h or t:
                placed = placed + total_grad[...]
            total_grad[...] = placed
    grad_out[...] = total_grad[...].astype(BF16)


def slot_backward(grads, qkv, after=()):
    n_seq = len(grads)
    piece, width = grads[0].shape
    heads = qkv.shape[0] // 3
    total = n_seq * piece
    return pl.pallas_call(
        partial(backward_kernel, n_seq, heads, len(after)),
        in_specs=whole_specs(n_seq) + after_specs(after) + whole_specs(3),
        out_shape=jax.ShapeDtypeStruct((total, 3 * width), BF16),
        scratch_shapes=[
            pltpu.VMEM((qkv.shape[1], width), F32),
            pltpu.VMEM((total, 3 * width), F32),
        ],
        compiler_params=pltpu.CompilerParams(vmem_limit_bytes=VMEM_BYTES),
        cost_estimate=pl.CostEstimate(
            flops=28 * 10**9, bytes_accessed=8 * 10**6, transcendentals=heads * total * total
        ),
        name="slot_backward",
    )(*grads, *after, qkv, head_columns(heads, 1), head_columns(heads, 3))


def mlp_kernel(
    tokens, attended, cotangent, valid, out_weight, bias_out, gain, shift, bias_down, up_own,
    up_other, bias_up, down_own, down_other, layer_out, grad_residual, grad_attended,
    grad_out_weight, vectors, grad_up_own, grad_up_other, grad_up_bias, grad_down_own,
    grad_down_other, staged, residual, output, grad_norm, normed, normed_t, grad_out, heads_in,
):
    step = pl.program_id(0)
    slots, piece, width = tokens.shape
    groups = attended.shape[0]
    rows = slots * piece
    padded = residual.shape[0]

    def stage(source):
        for s in range(slots):
            staged[s * piece : (s + 1) * piece, : source.shape[-1]] = source[s].astype(F32)

    @pl.when(step == 0)
    def _():
        if padded > rows:
            staged[rows:, :] = jnp.zeros((padded - rows, width), F32)
        for r in range(groups):
            stage(attended.at[r])
            heads_in[r] = staged[:, : attended.shape[-1]].astype(BF16)
        stage(cotangent)
        grad_out[...] = (staged[...] * valid[...]).astype(BF16)
        stage(tokens)
        total = staged[...] + bias_out[...]
        for r in range(groups):
            total = total + mm(heads_in[r], out_weight[r])
        residual[...] = total
        unit, _ = normalize(total)
        normed_here = (unit * gain[...] + shift[...]).astype(BF16)
        normed[...] = normed_here
        normed_t[...] = jnp.transpose(normed_here)
        output[...] = total + bias_down[...]
        grad_norm[...] = jnp.zeros_like(grad_norm)

    first = step < pl.num_programs(0) // 2
    up = jnp.where(first, up_own[...], up_other[...])
    down = jnp.where(first, down_own[...], down_other[...])
    hidden = mm(normed[...], up) + bias_up[...]
    share = 0.5 * (1.0 + lax.erf(hidden * np.float32(np.sqrt(0.5))))
    density = jnp.exp(-0.5 * hidden * hidden) * np.float32(1.0 / np.sqrt(2.0 * np.pi))
    activated = (hidden * share).astype(BF16)
    grad_hidden = (mm(grad_out[...], down, 1, 1) * (share + hidden * density)).astype(BF16)
    output[...] += mm(activated, down)
    grad_norm[...] += mm(grad_hidden, up, 1, 1)
    grad_up = mm(normed_t[...], grad_hidden).astype(BF16)
    grad_down = mm(activated, grad_out[...], 0, 0).astype(BF16)

    @pl.when(first)
    def _():
        grad_up_own[...] = grad_up
        grad_down_own[...] = grad_down

    @pl.when(jnp.logical_not(first))
    def _():
        grad_up_other[...] = grad_up
        grad_down_other[...] = grad_down

    grad_up_bias[...] = jnp.sum(grad_hidden.astype(F32), axis=0, keepdims=True)

    @pl.when(step == pl.num_programs(0) - 1)
    def _():
        staged[...] = output[...] * valid[...]
        for s in range(slots):
            layer_out[s] = staged[s * piece : (s + 1) * piece, :].astype(BF16)
        grad_low = grad_out[...].astype(F32)
        unit, factor = normalize(residual[...])
        back = grad_norm[...]
        scaled = back * gain[...]
        mean_scaled = jnp.mean(scaled, axis=-1, keepdims=True)
        mean_product = jnp.mean(scaled * unit, axis=-1, keepdims=True)
        total = grad_low + factor * (scaled - mean_scaled - unit * mean_product)
        staged[...] = total
        for s in range(slots):
            grad_residual[s] = staged[s * piece : (s + 1) * piece, :]
        branch = total.astype(BF16)
        vectors[0:1, :] = jnp.sum(back * unit, axis=0, keepdims=True)
        vectors[1:2, :] = jnp.sum(back, axis=0, keepdims=True)
        vectors[2:3, :] = jnp.sum(branch.astype(F32), axis=0, keepdims=True)
        vectors[3:4, :] = jnp.sum(grad_low, axis=0, keepdims=True)
        vectors[4:8, :] = jnp.zeros((4, width), F32)
        for r in range(groups):
            grad_out_weight[r] = mm(heads_in[r], branch, 0, 0).astype(BF16)
            staged[:, : attended.shape[-1]] = mm(branch, out_weight[r], 1, 1)
            for s in range(slots):
                grad_attended[r, s] = staged[
                    s * piece : (s + 1) * piece, : attended.shape[-1]
                ].astype(BF16)


def feed_forward(
    tokens, attended, cotangent, valid, out_weight, bias_out, gain, shift, bias_down, up_own,
    up_other, bias_up, down_own, down_other,
):
    slots, piece, width = tokens.shape
    groups, head_width = attended.shape[0], attended.shape[-1]
    ff = 2 * up_own.shape[1]
    chunk = 384
    half = ff // 2 // chunk
    padded = round_up(slots * piece, 16)
    whole = lambda shape: pl.BlockSpec(
        shape, lambda i: (0,) * len(shape), pipeline_mode=pl.Buffered(1)
    )
    own = lambda i: jnp.minimum(i, half - 1)
    other = lambda i: jnp.maximum(i - half, 0)
    by_columns = [pl.BlockSpec((width, chunk), lambda i, at=at: (0, at(i))) for at in (own, other)]
    by_rows = [pl.BlockSpec((chunk, width), lambda i, at=at: (at(i), 0)) for at in (own, other)]
    bias_block = pl.BlockSpec((1, chunk), lambda i: (0, i))
    row = whole((1, width))
    return pl.pallas_call(
        mlp_kernel,
        grid=(ff // chunk,),
        in_specs=[
            whole(tokens.shape),
            whole(attended.shape),
            whole(cotangent.shape),
            whole((padded, 1)),
            whole(out_weight.shape),
            row,
            row,
            row,
            row,
            *by_columns,
            bias_block,
            *by_rows,
        ],
        out_specs=[
            whole(tokens.shape),
            whole(tokens.shape),
            whole(attended.shape),
            whole(out_weight.shape),
            whole((8, width)),
            *by_columns,
            bias_block,
            *by_rows,
        ],
        out_shape=[
            jax.ShapeDtypeStruct(tokens.shape, BF16),
            jax.ShapeDtypeStruct(tokens.shape, F32),
            jax.ShapeDtypeStruct(attended.shape, BF16),
            jax.ShapeDtypeStruct(out_weight.shape, BF16),
            jax.ShapeDtypeStruct((8, width), F32),
            jax.ShapeDtypeStruct(up_own.shape, BF16),
            jax.ShapeDtypeStruct(up_own.shape, BF16),
            jax.ShapeDtypeStruct((1, ff), F32),
            jax.ShapeDtypeStruct(down_own.shape, BF16),
            jax.ShapeDtypeStruct(down_own.shape, BF16),
        ],
        scratch_shapes=[
            pltpu.VMEM((padded, width), F32),
            pltpu.VMEM((padded, width), F32),
            pltpu.VMEM((padded, width), F32),
            pltpu.VMEM((padded, width), F32),
            pltpu.VMEM((padded, width), BF16),
            pltpu.VMEM((width, padded), BF16),
            pltpu.VMEM((padded, width), BF16),
            pltpu.VMEM((groups, padded, head_width), BF16),
        ],
        compiler_params=pltpu.CompilerParams(
            vmem_limit_bytes=VMEM_BYTES, dimension_semantics=("arbitrary",)
        ),
        cost_estimate=pl.CostEstimate(
            flops=55 * 10**9, bytes_accessed=40 * 10**6, transcendentals=2 * padded * ff
        ),
        name="feed_forward",
    )(
        tokens, attended, cotangent, valid, out_weight, bias_out, gain, shift, bias_down, up_own,
        up_other, bias_up, down_own, down_other,
    )


def xor_send(block, axis, bits):
    n = lax.axis_size(axis)
    return lax.ppermute(block, axis, [(i, i ^ bits) for i in range(n)])


INNER = 2


def outer_send(block, shift):
    outer = lax.axis_size("img") // INNER
    return lax.ppermute(
        block,
        "img",
        [
            (z * INNER + y, ((z + shift) % outer) * INNER + y)
            for z in range(outer)
            for y in range(INNER)
        ],
    )


def few_devices():
    return lax.axis_size("img") <= 16


def place_outer(block, arrived):
    outer = lax.axis_size("img") // INNER
    z = lax.axis_index("img") // INNER
    placed = jnp.zeros((outer,) + block.shape, block.dtype)
    for k, part in enumerate([block] + arrived):
        placed = lax.dynamic_update_slice_in_dim(placed, part[None], (z + outer - k) % outer, 0)
    return placed


def gather_inner(placed):
    other = xor_send(placed, "img", 1)
    first = (lax.axis_index("img") & 1) == 0
    both = jnp.stack([jnp.where(first, placed, other), jnp.where(first, other, placed)], axis=1)
    return both.reshape((-1,) + placed.shape[1:])


def start_gather(block):
    if not few_devices():
        return lax.all_gather(block, "img", axis=0), None
    outer = lax.axis_size("img") // INNER
    return block, [outer_send(block, k) for k in range(1, outer)]


def end_gather(block, arrived):
    if arrived is None:
        return block
    return gather_inner(place_outer(block, arrived))


def reduce_inner(parts):
    outer = lax.axis_size("img") // INNER
    split = parts.reshape((outer, INNER) + parts.shape[1:])
    me = lax.axis_index("img") % INNER
    send = lax.dynamic_index_in_dim(split, 1 - me, 1, keepdims=False)
    keep = lax.dynamic_index_in_dim(split, me, 1, keepdims=False)
    return keep.astype(F32) + xor_send(send, "img", 1).astype(F32)


def reduce_outer(sums):
    outer = sums.shape[0]
    z = lax.axis_index("img") // INNER
    total = lax.dynamic_index_in_dim(sums, z, 0, keepdims=False)
    for k in range(1, outer):
        send = lax.dynamic_index_in_dim(sums, (z + k) % outer, 0, keepdims=False)
        total = total + outer_send(send.astype(BF16), k).astype(F32)
    return total


def scatter_img(parts):
    return lax.psum_scatter(parts, "img", scatter_dimension=0, tiled=False).astype(F32)


def sum_vectors(parts):
    arrived = [xor_send(parts, "seq", r) for r in range(1, 4)]
    parts = (parts + arrived[0]) + (arrived[1] + arrived[2])
    if not few_devices():
        return lax.psum_scatter(parts, "img", scatter_dimension=0, tiled=False)
    outer = lax.axis_size("img") // INNER
    img = lax.axis_index("img")
    z, y = img // INNER, img % INNER
    split = parts.reshape(outer, INNER, -1)
    mine = lax.dynamic_index_in_dim(split, z, 0, keepdims=False)
    for k in range(1, outer):
        mine = mine + outer_send(
            lax.dynamic_index_in_dim(split, (z + k) % outer, 0, keepdims=False), k
        )
    send = lax.dynamic_index_in_dim(mine, 1 - y, 0, keepdims=False)
    return lax.dynamic_index_in_dim(mine, y, 0, keepdims=False) + xor_send(send, "img", 1)


def in_pair_order(own, other, axis):
    first = (lax.axis_index("seq") & 1) == 0
    return jnp.where(
        first, jnp.concatenate([own, other], axis), jnp.concatenate([other, own], axis)
    )


def half_of(block, axis, which):
    size = block.shape[axis] // 2
    return lax.dynamic_slice_in_dim(block, which * size, size, axis)


def over_pieces(total):
    low = total.astype(BF16)
    low = (low.astype(F32) + xor_send(low, "seq", 2).astype(F32)).astype(BF16)
    return low, xor_send(low, "seq", 1)


def local(
    tokens,
    cotangent,
    images_held,
    piece_rows,
    norm_gain,
    norm_shift,
    qkv_weight,
    qkv_bias,
    out_weight,
    out_bias,
    mlp_gain,
    mlp_shift,
    up_weight,
    up_bias,
    down_weight,
    down_bias,
):
    slot_count, piece_size, model_width = tokens.shape
    n_seq = lax.axis_size("seq")
    n_img = lax.axis_size("img")
    me = lax.axis_index("seq")
    pair_me = me & 1
    own_img = lax.axis_index("img")
    row_count = slot_count * piece_size
    heads_here = HEADS // n_seq
    group = 3 * D // n_seq
    group_width = heads_here * HEAD_DIM
    shard = D // n_img
    ff = up_weight.shape[1]
    ff_half = ff // n_img // 2
    blocks = 3 * heads_here

    rows_of = piece_rows[me ^ jnp.arange(n_seq)]
    key_valid = (jnp.arange(piece_size)[None, :] < rows_of[:, None]).reshape(n_seq * piece_size)
    live_slots = jnp.arange(slot_count) < images_held[0]
    valid_rows = (live_slots[:, None] & key_valid[None, :piece_size]).reshape(row_count)
    valid_rows = jnp.pad(valid_rows, (0, round_up(row_count, 16) - row_count))
    valid_rows = valid_rows.astype(F32)[:, None]
    key_mask = jnp.where(
        key_valid[:, None] | (jnp.arange(LANES) != HEAD_DIM)[None, :], 0.0, NEG
    ).astype(F32)

    small = jnp.concatenate(
        [norm_gain, norm_shift, out_bias, mlp_gain, mlp_shift, down_bias, qkv_bias, up_bias]
    )
    small_rows = round_up(-(-small.shape[0] // group), 16)
    small = jnp.pad(small, (0, small_rows * group - small.shape[0])).reshape(small_rows, group)
    my_columns = lax.dynamic_slice_in_dim(qkv_weight, me * group, group, 1)
    first_part, first_arrived = start_gather(jnp.concatenate([my_columns, small], axis=0))

    slot_tokens = []
    for slot in range(slot_count):
        own = tokens[slot]
        pair = xor_send(own, "seq", 1)
        across = xor_send(own, "seq", 2)
        slot_tokens.append([own, pair, across, xor_send(across, "seq", 1)])
    down_own = lax.all_gather(half_of(down_weight, 0, pair_me), "img", axis=0)
    down_own = down_own.reshape(-1, model_width)

    first_set = end_gather(first_part, first_arrived)
    qkv_cols = first_set[:, :shard].reshape(model_width, group)
    params = first_set[:, shard:].reshape(n_img, -1).astype(F32)

    def param(start, width):
        return params[:, start * shard : (start + width) * shard].reshape(-1)

    gain_first, shift_first, bias_out = param(0, 1)[None], param(1, 1)[None], param(2, 1)[None]
    gain_second, shift_second, bias_down = param(3, 1)[None], param(4, 1)[None], param(5, 1)[None]
    pair_bias, bias_up = param(6, 2), param(8, 4).reshape(n_img, 2, ff_half)
    bias_up = jnp.concatenate(
        [
            lax.dynamic_index_in_dim(bias_up, which, 1, keepdims=False).reshape(1, -1)
            for which in (pair_me, 1 - pair_me)
        ],
        axis=1,
    )

    scale = np.ones((blocks, 1, 1), np.float32)
    scale[0::3] = HEAD_DIM**-0.5
    ones = np.zeros((blocks, 1, LANES), np.float32)
    ones[0::3, 0, HEAD_DIM] = 1.0
    ones[2::3, 0, HEAD_DIM] = 1.0
    lanes = ((0, 0), (0, 0), (0, LANES - HEAD_DIM))
    head_weight = jnp.swapaxes(qkv_cols.reshape(model_width, blocks, HEAD_DIM), 0, 1)
    head_weight = jnp.pad(head_weight * scale.astype(BF16), lanes)
    paired = lax.dynamic_slice_in_dim(
        pair_bias.reshape(HEADS, 2, HEAD_DIM), me * heads_here, heads_here, 0
    )
    head_bias = jnp.concatenate(
        [paired[:, :1], jnp.zeros((heads_here, 1, HEAD_DIM), F32), paired[:, 1:]], axis=1
    ).reshape(blocks, 1, HEAD_DIM)
    head_bias = jnp.pad(head_bias * scale, lanes) + ones

    my_up = lax.dynamic_index_in_dim(
        up_weight.reshape(shard, n_img, 2, ff_half), pair_me, 2, keepdims=False
    ).reshape(shard, -1)
    second_part, second_arrived = start_gather(
        jnp.concatenate([my_up, half_of(out_weight, 1, pair_me)], axis=1)
    )

    slot_normed, slot_qkv, slot_attended = [], [], []
    for slot in range(slot_count):
        after = ()
        if slot == 1 and second_arrived is not None:
            after = tuple(second_arrived)
        normed, qkv_rows, attended = slot_forward(
            slot_tokens[slot], gain_first, shift_first, head_weight, head_bias, key_mask, after
        )
        slot_normed.append(normed)
        slot_qkv.append(qkv_rows)
        slot_attended.append(
            [attended[0]] + [xor_send(attended[r], "seq", r) for r in range(1, n_seq)]
        )
    second_set = end_gather(second_part, second_arrived).reshape(model_width, -1)
    up_own, out_own = second_set[:, : ff // 2], second_set[:, ff // 2 :]
    up_other = xor_send(up_own, "seq", 1)
    down_other = xor_send(down_own, "seq", 1)
    out_full = in_pair_order(out_own, xor_send(out_own, "seq", 1), 1)
    out_full = out_full.reshape(n_seq, group_width, model_width)
    out_groups = jnp.stack(
        [lax.dynamic_index_in_dim(out_full, me ^ r, 0, keepdims=False) for r in range(n_seq)]
    )
    attended_groups = jnp.stack(
        [jnp.stack([parts[r] for parts in slot_attended]) for r in range(n_seq)]
    )

    (
        layer_out,
        grad_residual,
        grad_attended,
        grad_out_groups,
        vectors,
        grad_up_own,
        grad_up_other,
        grad_up_bias,
        grad_down_own,
        grad_down_other,
    ) = feed_forward(
        tokens,
        attended_groups,
        cotangent,
        valid_rows,
        out_groups,
        bias_out,
        gain_second,
        shift_second,
        bias_down,
        up_own,
        up_other,
        bias_up,
        down_own,
        down_other,
    )

    slot_grads = []
    for slot in range(slot_count):
        slot_grads.append(
            [grad_attended[0, slot]]
            + [xor_send(grad_attended[r, slot], "seq", r) for r in range(1, n_seq)]
        )

    down_sum = grad_down_own.astype(F32) + xor_send(grad_down_other, "seq", 1).astype(F32)
    own_down = scatter_img(down_sum.astype(BF16).reshape(n_img, ff_half, model_width))
    up_sum = grad_up_own.astype(F32) + xor_send(grad_up_other, "seq", 1).astype(F32)
    grad_out_weight = jnp.concatenate(
        [lax.dynamic_index_in_dim(grad_out_groups, me ^ r, 0, keepdims=False) for r in range(n_seq)],
        axis=0,
    )
    out_sum = half_of(grad_out_weight, 1, pair_me).astype(F32) + xor_send(
        half_of(grad_out_weight, 1, 1 - pair_me), "seq", 1
    ).astype(F32)
    second_grads = jnp.concatenate([up_sum, out_sum], axis=1).astype(BF16)
    second_grads = second_grads.reshape(n_img, shard, -1)
    stages = [(), (), ()]
    if few_devices():
        sums = reduce_inner(second_grads)
        own_second = reduce_outer(sums)
        stages = [(), (sums,), (own_second,)]
    else:
        own_second = scatter_img(second_grads)

    grad_columns = jnp.zeros((model_width, group), F32)
    bias_sums = jnp.zeros((group,), F32)
    own_sums = []
    for slot in range(slot_count):
        grad_qkv = slot_backward(slot_grads[slot], slot_qkv[slot], stages[min(slot, 2)])
        partial_in = mm(grad_qkv, qkv_cols, 1, 1).reshape(n_seq, piece_size, model_width)
        low = partial_in.astype(BF16)
        pair = xor_send(low[1], "seq", 1).astype(F32)
        across = xor_send(low[3], "seq", 1).astype(F32)
        across = xor_send((partial_in[2] + across).astype(BF16), "seq", 2)
        own_sums.append(partial_in[0] + pair + across.astype(F32))
        grad_columns += mm(slot_normed[slot], grad_qkv, 0, 0)
        bias_sums += jnp.sum(grad_qkv.astype(F32), axis=0)
    columns = grad_columns.astype(BF16).reshape(n_img, shard, group)
    if few_devices():
        own_columns = reduce_outer(reduce_inner(columns))
    else:
        own_columns = scatter_img(columns)
    own_columns = own_columns.astype(BF16)

    grad_norm_first = jnp.concatenate(own_sums, axis=0)
    unit, factor = normalize(tokens.reshape(row_count, model_width).astype(F32))
    scaled = grad_norm_first * gain_first
    mean_scaled = jnp.mean(scaled, axis=-1, keepdims=True)
    mean_product = jnp.mean(scaled * unit, axis=-1, keepdims=True)
    grad_inputs = factor * (scaled - mean_scaled - unit * mean_product)
    tokens_grad = grad_residual + grad_inputs.reshape(grad_residual.shape)
    grad_norm_gain = jnp.sum(grad_norm_first * unit, axis=0)
    grad_norm_shift = jnp.sum(grad_norm_first, axis=0)

    by_sender = jnp.stack(
        [own_columns] + [xor_send(own_columns, "seq", r) for r in range(1, n_seq)]
    )
    share_qkv = jnp.concatenate(
        [lax.dynamic_index_in_dim(by_sender, me ^ g, 0, keepdims=False) for g in range(n_seq)],
        axis=1,
    ).astype(F32)
    second_low, second_other = over_pieces(own_second)
    up_low = second_low[:, : ff // 2].reshape(shard, n_img, 1, ff_half)
    up_there = second_other[:, : ff // 2].reshape(shard, n_img, 1, ff_half)
    share_up = in_pair_order(up_low, up_there, 2).reshape(shard, ff).astype(F32)
    share_out = in_pair_order(second_low[:, ff // 2 :], second_other[:, ff // 2 :], 1).astype(F32)
    share_down = in_pair_order(*over_pieces(own_down), 0).astype(F32)

    bias_sums = bias_sums.reshape(heads_here, 3, HEAD_DIM)
    grad_pairs = jnp.concatenate([bias_sums[:, :1], bias_sums[:, 2:]], axis=1).reshape(-1)
    grad_pairs = lax.dynamic_update_slice_in_dim(
        jnp.zeros((2 * D,), F32), grad_pairs, me * grad_pairs.shape[0], 0
    )
    up_halves = grad_up_bias.reshape(2, n_img, 1, ff_half)
    grad_up_bias = in_pair_order(up_halves[0], up_halves[1], 1).reshape(-1)
    all_vectors = [
        grad_norm_gain,
        grad_norm_shift,
        grad_pairs,
        vectors[2],
        vectors[0],
        vectors[1],
        grad_up_bias,
        vectors[3],
    ]
    mine = sum_vectors(jnp.concatenate([v.reshape(n_img, -1) for v in all_vectors], axis=1))
    shares, at = [], 0
    for v in all_vectors:
        size = v.shape[0] // n_img
        shares.append(mine[at : at + size])
        at += size
    return (
        layer_out,
        tokens_grad,
        shares[0],
        shares[1],
        share_qkv,
        shares[2],
        share_out,
        shares[3],
        shares[4],
        shares[5],
        share_up,
        shares[6],
        share_down,
        shares[7],
    )


def solution(mesh):
    placed = (
        P("img", "seq", None),
        P("img", "seq", None),
        P("img"),
        P(),
        P("img"),
        P("img"),
        P("img", None),
        P("img"),
        P("img", None),
        P("img"),
        P("img"),
        P("img"),
        P("img", None),
        P("img"),
        P("img", None),
        P("img"),
    )
    return jax.shard_map(
        local,
        mesh=mesh,
        in_specs=placed,
        out_specs=(
            P("img", "seq", None),
            P("img", "seq", None),
            P("img"),
            P("img"),
            P("img", None),
            P("img"),
            P("img", None),
            P("img"),
            P("img"),
            P("img"),
            P("img", None),
            P("img"),
            P("img", None),
            P("img"),
        ),
        check_vma=False,
    )
```

```python
from functools import partial

import jax
import jax.numpy as jnp
import numpy as np
from jax import lax
from jax.experimental import pallas as pl
from jax.experimental.pallas import tpu as pltpu
from jax.sharding import PartitionSpec as P

D = 768
HEADS = 12
HEAD_DIM = 64
EPS = 1e-06
NEG = -1e30
LANES = 128
F32 = jnp.float32
BF16 = jnp.bfloat16
VMEM_BYTES = 60 * 1024 * 1024


def mm(left, right, left_dim=1, right_dim=0):
    return lax.dot_general(
        left, right, (((left_dim,), (right_dim,)), ((), ())), preferred_element_type=F32
    )


def normalize(features):
    row_mean = jnp.mean(features, axis=-1, keepdims=True)
    centred = features - row_mean
    spread = jnp.mean(centred * centred, axis=-1, keepdims=True)
    factor = lax.rsqrt(spread + EPS)
    return centred * factor, factor


def round_up(size, unit):
    return -(-size // unit) * unit


def head_columns(heads, parts):
    place = np.zeros((heads * parts, LANES, heads * parts * HEAD_DIM), np.float32)
    for b in range(heads * parts):
        for d in range(HEAD_DIM):
            place[b, d, b * HEAD_DIM + d] = 1.0
    return jnp.asarray(place, BF16)


def lane_columns(heads):
    pick = np.zeros((3 * heads, LANES, LANES), np.float32)
    ones = np.zeros((3 * heads, 1, LANES), np.float32)
    for b in range(3 * heads):
        start = b * HEAD_DIM % LANES
        for d in range(HEAD_DIM):
            pick[b, start + d, d] = HEAD_DIM**-0.5 if b % 3 == 0 else 1.0
        if b % 3 != 1:
            ones[b, 0, HEAD_DIM] = 1.0
    return jnp.asarray(pick, BF16), jnp.asarray(ones, F32)


def query_block(rows):
    for size in range(min(rows, 400) // 16 * 16, 15, -16):
        if rows % size == 0:
            return size
    return rows


def after_specs(after):
    return [pl.BlockSpec(memory_space=pl.ANY)] * len(after)


def whole_specs(count):
    return [pl.BlockSpec(memory_space=pltpu.VMEM)] * count


def forward_kernel(n_seq, heads, n_after, *refs):
    tokens, refs = refs[:n_seq], refs[n_seq + n_after :]
    gain, shift, weight, bias, key_mask, pick, ones, place = refs[:8]
    normed_out, qkv_out, attended_out, rows, attended = refs[8:]
    piece = tokens[0].shape[0]
    total = n_seq * piece
    for r in range(n_seq):
        unit, _ = normalize(tokens[r][...].astype(F32))
        rows[r * piece : (r + 1) * piece, :] = unit * gain[...] + shift[...]
    normed = rows[...].astype(BF16)
    normed_out[...] = normed
    qkv = (mm(normed, weight[...]) + bias[...]).astype(BF16)
    width = qkv.shape[1]
    block = query_block(total)
    pad = qkv_out.shape[1] - total
    parts = []
    for b in range(3 * heads):
        start = b * HEAD_DIM // LANES * LANES
        size = min(LANES, width - start)
        part = mm(qkv[:, start : start + size], pick[b, :size]) + ones[b]
        if b % 3 == 1:
            part = part + key_mask[...]
        part = part.astype(BF16)
        qkv_out[b, :total] = part
        if pad:
            qkv_out[b, total:] = jnp.zeros((pad, LANES), BF16)
        parts.append(part)

    tasks = [(at, h) for at in range(0, total, block) for h in range(heads)]

    def score(task):
        at, h = task
        return mm(parts[3 * h][at : at + block], parts[3 * h + 1], 1, 1)

    scores = score(tasks[0])
    placed = None
    for index, (at, h) in enumerate(tasks):
        following = score(tasks[index + 1]) if index + 1 < len(tasks) else None
        peak = jnp.max(scores, axis=-1, keepdims=True)
        terms = jnp.exp(scores - peak).astype(BF16)
        weighted = mm(terms, parts[3 * h + 2])
        result = (weighted / weighted[:, HEAD_DIM : HEAD_DIM + 1]).astype(BF16)
        here = mm(result, place[h])
        placed = here if h == 0 else placed + here
        if h == heads - 1:
            attended[at : at + block, :] = placed
        scores = following
    for r in range(n_seq):
        attended_out[r] = attended[r * piece : (r + 1) * piece, :].astype(BF16)


def slot_forward(pieces, gain, shift, weight, bias, key_mask, after=()):
    n_seq = len(pieces)
    piece, width = pieces[0].shape
    heads = weight.shape[1] // (3 * HEAD_DIM)
    total = n_seq * piece
    padded = round_up(total, LANES)
    return pl.pallas_call(
        partial(forward_kernel, n_seq, heads, len(after)),
        in_specs=whole_specs(n_seq) + after_specs(after) + whole_specs(8),
        out_shape=(
            jax.ShapeDtypeStruct((total, width), BF16),
            jax.ShapeDtypeStruct((3 * heads, padded, LANES), BF16),
            jax.ShapeDtypeStruct((n_seq, piece, heads * HEAD_DIM), BF16),
        ),
        scratch_shapes=[
            pltpu.VMEM((total, width), F32),
            pltpu.VMEM((total, heads * HEAD_DIM), F32),
        ],
        compiler_params=pltpu.CompilerParams(vmem_limit_bytes=VMEM_BYTES),
        cost_estimate=pl.CostEstimate(
            flops=20 * 10**9, bytes_accessed=12 * 10**6, transcendentals=heads * total * total
        ),
        name="slot_forward",
    )(
        *pieces, *after, gain, shift, weight, bias, key_mask, *lane_columns(heads),
        head_columns(heads, 1),
    )


def backward_kernel(n_seq, heads, n_after, *refs):
    grads, refs = refs[:n_seq], refs[n_seq + n_after :]
    tokens, refs = refs[:n_seq], refs[n_seq:]
    qkv, normed, weight, before, place, spread = refs[:6]
    outs, refs = refs[6 : 6 + n_seq], refs[6 + n_seq :]
    grad_weight, vectors, grad_bias, rows, wide = refs
    piece = grads[0].shape[0]
    total = n_seq * piece
    padded = qkv.shape[1]
    for r in range(n_seq):
        rows[r * piece : (r + 1) * piece, :] = grads[r][...].astype(F32)
    if padded > total:
        rows[total:, :] = jnp.zeros((padded - total, rows.shape[1]), F32)
    grad_rows = rows[...].astype(BF16)
    grad_heads = [mm(grad_rows, place[h], 1, 1).astype(BF16) for h in range(heads)]
    block = 4 * LANES
    tasks = [(h, at) for h in range(heads) for at in range(0, padded, block)]

    def products(task):
        h, at = task
        end = min(at + block, padded)
        scores = mm(qkv[3 * h + 1, :total], qkv[3 * h, at:end], 1, 1)
        return scores, mm(qkv[3 * h + 2, :total], grad_heads[h][at:end], 1, 1)

    current = products(tasks[0])
    grad_qkv = None
    for index, (h, at) in enumerate(tasks):
        following = products(tasks[index + 1]) if index + 1 < len(tasks) else None
        if at == 0:
            keys_t = jnp.transpose(qkv[3 * h + 1])[:, :total]
            grad_keys = jnp.zeros((total, LANES), F32)
            grad_values = jnp.zeros((total, LANES), F32)
            grad_queries = []
        end = min(at + block, padded)
        scores, grad_probs = current
        peak = jnp.max(scores, axis=0, keepdims=True)
        terms = jnp.exp(scores - peak)
        probs = terms * (1.0 / jnp.sum(terms, axis=0, keepdims=True))
        inner = jnp.sum(probs * grad_probs, axis=0, keepdims=True)
        grad_scores = (probs * (grad_probs - inner)).astype(BF16)
        grad_values = grad_values + mm(probs.astype(BF16), grad_heads[h][at:end])
        grad_keys = grad_keys + mm(grad_scores, qkv[3 * h, at:end])
        grad_queries.append(jnp.transpose(mm(keys_t, grad_scores)))
        if end == padded:
            queries = jnp.concatenate(grad_queries, axis=0)[:total] * (HEAD_DIM**-0.5)
            for t, part in enumerate((queries, grad_keys, grad_values)):
                placed = mm(part.astype(BF16), spread[3 * h + t])
                grad_qkv = placed if grad_qkv is None else grad_qkv + placed
        current = following
    grad_low = grad_qkv.astype(BF16)
    grad_bias[...] = jnp.broadcast_to(
        jnp.sum(grad_low.astype(F32), axis=0, keepdims=True), grad_bias.shape
    )
    grad_weight[...] = before[...] + mm(normed[...], grad_low, 0, 0)
    wide[...] = mm(grad_low, weight[...], 1, 1)
    by_unit = jnp.zeros((1, wide.shape[1]), F32)
    by_one = jnp.zeros((1, wide.shape[1]), F32)
    for r in range(n_seq):
        share = wide[r * piece : (r + 1) * piece, :]
        unit, _ = normalize(tokens[r][...].astype(F32))
        by_unit = by_unit + jnp.sum(share * unit, axis=0, keepdims=True)
        by_one = by_one + jnp.sum(share, axis=0, keepdims=True)
        outs[r][...] = share.astype(outs[r].dtype)
    vectors[...] = jnp.zeros(vectors.shape, F32)
    vectors[0:1, :] = by_unit
    vectors[1:2, :] = by_one


def slot_backward(grads, tokens, qkv, normed, weight, before, after=()):
    n_seq = len(grads)
    piece, width = grads[0].shape
    heads = qkv.shape[0] // 3
    total = n_seq * piece
    model = normed.shape[1]
    share = lambda r: jax.ShapeDtypeStruct((piece, model), BF16 if r & 1 else F32)
    return pl.pallas_call(
        partial(backward_kernel, n_seq, heads, len(after)),
        in_specs=whole_specs(n_seq) + after_specs(after) + whole_specs(n_seq + 6),
        out_shape=(
            *(share(r) for r in range(n_seq)),
            jax.ShapeDtypeStruct((model, 3 * width), F32),
            jax.ShapeDtypeStruct((8, model), F32),
            jax.ShapeDtypeStruct((8, 3 * width), F32),
        ),
        scratch_shapes=[
            pltpu.VMEM((qkv.shape[1], width), F32),
            pltpu.VMEM((total, model), F32),
        ],
        compiler_params=pltpu.CompilerParams(vmem_limit_bytes=VMEM_BYTES),
        cost_estimate=pl.CostEstimate(
            flops=28 * 10**9, bytes_accessed=12 * 10**6, transcendentals=heads * total * total
        ),
        name="slot_backward",
    )(
        *grads, *after, *tokens, qkv, normed, weight, before, head_columns(heads, 1),
        head_columns(heads, 3),
    )


def copy_kernel(count, n_after, *refs):
    for source, target in zip(refs[:count], refs[count + n_after :]):
        target[...] = source[...]


def once_there(arrays, after):
    if not after:
        return arrays
    return pl.pallas_call(
        partial(copy_kernel, len(arrays), len(after)),
        in_specs=whole_specs(len(arrays)) + after_specs(after),
        out_shape=tuple(jax.ShapeDtypeStruct(a.shape, a.dtype) for a in arrays),
        name="once_there",
    )(*arrays, *after)


def mlp_kernel(
    tokens, attended, cotangent, valid, out_weight, bias_out, gain, shift, bias_down, up_own,
    up_other, bias_up, down_own, down_other, layer_out, grad_residual, grad_attended,
    grad_out_weight, vectors, grad_up_own, grad_up_other, grad_up_bias, grad_down_own,
    grad_down_other, staged, residual, output, grad_norm, normed, normed_t, grad_out, heads_in,
):
    step = pl.program_id(0)
    slots, piece, width = tokens.shape
    groups = attended.shape[0]
    rows = slots * piece
    padded = residual.shape[0]

    def stage(source):
        for s in range(slots):
            staged[s * piece : (s + 1) * piece, : source.shape[-1]] = source[s].astype(F32)

    @pl.when(step == 0)
    def _():
        if padded > rows:
            staged[rows:, :] = jnp.zeros((padded - rows, width), F32)
        for r in range(groups):
            stage(attended.at[r])
            heads_in[r] = staged[:, : attended.shape[-1]].astype(BF16)
        stage(cotangent)
        grad_out[...] = (staged[...] * valid[...]).astype(BF16)
        stage(tokens)
        total = staged[...] + bias_out[...]
        for r in range(groups):
            total = total + mm(heads_in[r], out_weight[r])
        residual[...] = total
        unit, _ = normalize(total)
        normed_here = (unit * gain[...] + shift[...]).astype(BF16)
        normed[...] = normed_here
        normed_t[...] = jnp.transpose(normed_here)
        output[...] = total + bias_down[...]
        grad_norm[...] = jnp.zeros_like(grad_norm)

    first = step < pl.num_programs(0) // 2
    up = jnp.where(first, up_own[...], up_other[...])
    down = jnp.where(first, down_own[...], down_other[...])
    hidden = mm(normed[...], up) + bias_up[...]
    share = 0.5 * (1.0 + lax.erf(hidden * np.float32(np.sqrt(0.5))))
    density = jnp.exp(-0.5 * hidden * hidden) * np.float32(1.0 / np.sqrt(2.0 * np.pi))
    activated = (hidden * share).astype(BF16)
    grad_hidden = (mm(grad_out[...], down, 1, 1) * (share + hidden * density)).astype(BF16)
    output[...] += mm(activated, down)
    grad_norm[...] += mm(grad_hidden, up, 1, 1)
    grad_up = mm(normed_t[...], grad_hidden).astype(BF16)
    grad_down = mm(activated, grad_out[...], 0, 0).astype(BF16)

    @pl.when(first)
    def _():
        grad_up_own[...] = grad_up
        grad_down_own[...] = grad_down

    @pl.when(jnp.logical_not(first))
    def _():
        grad_up_other[...] = grad_up
        grad_down_other[...] = grad_down

    grad_up_bias[...] = jnp.sum(grad_hidden.astype(F32), axis=0, keepdims=True)

    @pl.when(step == pl.num_programs(0) - 1)
    def _():
        staged[...] = output[...] * valid[...]
        for s in range(slots):
            layer_out[s] = staged[s * piece : (s + 1) * piece, :].astype(BF16)
        grad_low = grad_out[...].astype(F32)
        unit, factor = normalize(residual[...])
        back = grad_norm[...]
        scaled = back * gain[...]
        mean_scaled = jnp.mean(scaled, axis=-1, keepdims=True)
        mean_product = jnp.mean(scaled * unit, axis=-1, keepdims=True)
        total = grad_low + factor * (scaled - mean_scaled - unit * mean_product)
        staged[...] = total
        for s in range(slots):
            grad_residual[s] = staged[s * piece : (s + 1) * piece, :]
        branch = total.astype(BF16)
        vectors[0:1, :] = jnp.sum(back * unit, axis=0, keepdims=True)
        vectors[1:2, :] = jnp.sum(back, axis=0, keepdims=True)
        vectors[2:3, :] = jnp.sum(branch.astype(F32), axis=0, keepdims=True)
        vectors[3:4, :] = jnp.sum(grad_low, axis=0, keepdims=True)
        vectors[4:8, :] = jnp.zeros((4, width), F32)
        for r in range(groups):
            grad_out_weight[r] = mm(heads_in[r], branch, 0, 0).astype(BF16)
            staged[:, : attended.shape[-1]] = mm(branch, out_weight[r], 1, 1)
            for s in range(slots):
                grad_attended[r, s] = staged[
                    s * piece : (s + 1) * piece, : attended.shape[-1]
                ].astype(BF16)


def feed_forward(
    tokens, attended, cotangent, valid, out_weight, bias_out, gain, shift, bias_down, up_own,
    up_other, bias_up, down_own, down_other,
):
    slots, piece, width = tokens.shape
    groups, head_width = attended.shape[0], attended.shape[-1]
    ff = 2 * up_own.shape[1]
    chunk = 384
    half = ff // 2 // chunk
    padded = round_up(slots * piece, 16)
    whole = lambda shape: pl.BlockSpec(
        shape, lambda i: (0,) * len(shape), pipeline_mode=pl.Buffered(1)
    )
    own = lambda i: jnp.minimum(i, half - 1)
    other = lambda i: jnp.maximum(i - half, 0)
    by_columns = [pl.BlockSpec((width, chunk), lambda i, at=at: (0, at(i))) for at in (own, other)]
    by_rows = [pl.BlockSpec((chunk, width), lambda i, at=at: (at(i), 0)) for at in (own, other)]
    bias_block = pl.BlockSpec((1, chunk), lambda i: (0, i))
    row = whole((1, width))
    return pl.pallas_call(
        mlp_kernel,
        grid=(ff // chunk,),
        in_specs=[
            whole(tokens.shape),
            whole(attended.shape),
            whole(cotangent.shape),
            whole((padded, 1)),
            whole(out_weight.shape),
            row,
            row,
            row,
            row,
            *by_columns,
            bias_block,
            *by_rows,
        ],
        out_specs=[
            whole(tokens.shape),
            whole(tokens.shape),
            whole(attended.shape),
            whole(out_weight.shape),
            whole((8, width)),
            *by_columns,
            bias_block,
            *by_rows,
        ],
        out_shape=[
            jax.ShapeDtypeStruct(tokens.shape, BF16),
            jax.ShapeDtypeStruct(tokens.shape, F32),
            jax.ShapeDtypeStruct(attended.shape, BF16),
            jax.ShapeDtypeStruct(out_weight.shape, BF16),
            jax.ShapeDtypeStruct((8, width), F32),
            jax.ShapeDtypeStruct(up_own.shape, BF16),
            jax.ShapeDtypeStruct(up_own.shape, BF16),
            jax.ShapeDtypeStruct((1, ff), F32),
            jax.ShapeDtypeStruct(down_own.shape, BF16),
            jax.ShapeDtypeStruct(down_own.shape, BF16),
        ],
        scratch_shapes=[
            pltpu.VMEM((padded, width), F32),
            pltpu.VMEM((padded, width), F32),
            pltpu.VMEM((padded, width), F32),
            pltpu.VMEM((padded, width), F32),
            pltpu.VMEM((padded, width), BF16),
            pltpu.VMEM((width, padded), BF16),
            pltpu.VMEM((padded, width), BF16),
            pltpu.VMEM((groups, padded, head_width), BF16),
        ],
        compiler_params=pltpu.CompilerParams(
            vmem_limit_bytes=VMEM_BYTES, dimension_semantics=("arbitrary",)
        ),
        cost_estimate=pl.CostEstimate(
            flops=55 * 10**9, bytes_accessed=40 * 10**6, transcendentals=2 * padded * ff
        ),
        name="feed_forward",
    )(
        tokens, attended, cotangent, valid, out_weight, bias_out, gain, shift, bias_down, up_own,
        up_other, bias_up, down_own, down_other,
    )


def xor_send(block, axis, bits):
    n = lax.axis_size(axis)
    return lax.ppermute(block, axis, [(i, i ^ bits) for i in range(n)])


INNER = 2


def outer_send(block, shift):
    outer = lax.axis_size("img") // INNER
    return lax.ppermute(
        block,
        "img",
        [
            (z * INNER + y, ((z + shift) % outer) * INNER + y)
            for z in range(outer)
            for y in range(INNER)
        ],
    )


def few_devices():
    return lax.axis_size("img") <= 16


def place_outer(block, arrived):
    outer = lax.axis_size("img") // INNER
    z = lax.axis_index("img") // INNER
    placed = jnp.zeros((outer,) + block.shape, block.dtype)
    for k, part in enumerate([block] + arrived):
        placed = lax.dynamic_update_slice_in_dim(placed, part[None], (z + outer - k) % outer, 0)
    return placed


def gather_inner(placed):
    other = xor_send(placed, "img", 1)
    first = (lax.axis_index("img") & 1) == 0
    both = jnp.stack([jnp.where(first, placed, other), jnp.where(first, other, placed)], axis=1)
    return both.reshape((-1,) + placed.shape[1:])


def start_gather(block):
    if not few_devices():
        return lax.all_gather(block, "img", axis=0), None
    outer = lax.axis_size("img") // INNER
    return block, [outer_send(block, k) for k in range(1, outer)]


def end_gather(block, arrived):
    if arrived is None:
        return block
    return gather_inner(place_outer(block, arrived))


def reduce_inner(parts):
    outer = lax.axis_size("img") // INNER
    split = parts.reshape((outer, INNER) + parts.shape[1:])
    me = lax.axis_index("img") % INNER
    send = lax.dynamic_index_in_dim(split, 1 - me, 1, keepdims=False)
    keep = lax.dynamic_index_in_dim(split, me, 1, keepdims=False)
    return keep.astype(F32) + xor_send(send, "img", 1).astype(F32)


def reduce_outer(sums):
    outer = sums.shape[0]
    z = lax.axis_index("img") // INNER
    total = lax.dynamic_index_in_dim(sums, z, 0, keepdims=False)
    for k in range(1, outer):
        send = lax.dynamic_index_in_dim(sums, (z + k) % outer, 0, keepdims=False)
        total = total + outer_send(send.astype(BF16), k).astype(F32)
    return total


def scatter_img(parts):
    return lax.psum_scatter(parts, "img", scatter_dimension=0, tiled=False).astype(F32)


def sum_vectors(parts):
    arrived = [xor_send(parts, "seq", r) for r in range(1, 4)]
    parts = (parts + arrived[0]) + (arrived[1] + arrived[2])
    if not few_devices():
        return lax.psum_scatter(parts, "img", scatter_dimension=0, tiled=False)
    outer = lax.axis_size("img") // INNER
    img = lax.axis_index("img")
    z, y = img // INNER, img % INNER
    split = parts.reshape(outer, INNER, -1)
    mine = lax.dynamic_index_in_dim(split, z, 0, keepdims=False)
    for k in range(1, outer):
        mine = mine + outer_send(
            lax.dynamic_index_in_dim(split, (z + k) % outer, 0, keepdims=False), k
        )
    send = lax.dynamic_index_in_dim(mine, 1 - y, 0, keepdims=False)
    return lax.dynamic_index_in_dim(mine, y, 0, keepdims=False) + xor_send(send, "img", 1)


def in_pair_order(own, other, axis):
    first = (lax.axis_index("seq") & 1) == 0
    return jnp.where(
        first, jnp.concatenate([own, other], axis), jnp.concatenate([other, own], axis)
    )


def half_of(block, axis, which):
    size = block.shape[axis] // 2
    return lax.dynamic_slice_in_dim(block, which * size, size, axis)


def over_pieces(total):
    low = total.astype(BF16)
    low = (low.astype(F32) + xor_send(low, "seq", 2).astype(F32)).astype(BF16)
    return low, xor_send(low, "seq", 1)


def local(
    tokens,
    cotangent,
    images_held,
    piece_rows,
    norm_gain,
    norm_shift,
    qkv_weight,
    qkv_bias,
    out_weight,
    out_bias,
    mlp_gain,
    mlp_shift,
    up_weight,
    up_bias,
    down_weight,
    down_bias,
):
    slot_count, piece_size, model_width = tokens.shape
    n_seq = lax.axis_size("seq")
    n_img = lax.axis_size("img")
    me = lax.axis_index("seq")
    pair_me = me & 1
    own_img = lax.axis_index("img")
    row_count = slot_count * piece_size
    heads_here = HEADS // n_seq
    group = 3 * D // n_seq
    group_width = heads_here * HEAD_DIM
    shard = D // n_img
    ff = up_weight.shape[1]
    ff_half = ff // n_img // 2
    blocks = 3 * heads_here

    rows_of = piece_rows[me ^ jnp.arange(n_seq)]
    key_valid = (jnp.arange(piece_size)[None, :] < rows_of[:, None]).reshape(n_seq * piece_size)
    live_slots = jnp.arange(slot_count) < images_held[0]
    valid_rows = (live_slots[:, None] & key_valid[None, :piece_size]).reshape(row_count)
    valid_rows = jnp.pad(valid_rows, (0, round_up(row_count, 16) - row_count))
    valid_rows = valid_rows.astype(F32)[:, None]
    key_mask = jnp.where(
        key_valid[:, None] | (jnp.arange(LANES) != HEAD_DIM)[None, :], 0.0, NEG
    ).astype(F32)

    small = jnp.concatenate(
        [norm_gain, norm_shift, out_bias, mlp_gain, mlp_shift, down_bias, qkv_bias, up_bias]
    )
    small_rows = round_up(-(-small.shape[0] // group), 16)
    small = jnp.pad(small, (0, small_rows * group - small.shape[0])).reshape(small_rows, group)
    my_columns = lax.dynamic_slice_in_dim(qkv_weight, me * group, group, 1)
    first_part, first_arrived = start_gather(jnp.concatenate([my_columns, small], axis=0))

    slot_tokens = []
    for slot in range(slot_count):
        own = tokens[slot]
        pair = xor_send(own, "seq", 1)
        across = xor_send(own, "seq", 2)
        slot_tokens.append([own, pair, across, xor_send(across, "seq", 1)])

    my_up = lax.dynamic_index_in_dim(
        up_weight.reshape(shard, n_img, 2, ff_half), pair_me, 2, keepdims=False
    ).reshape(shard, -1)
    my_down, my_second = once_there(
        (
            half_of(down_weight, 0, pair_me),
            jnp.concatenate([my_up, half_of(out_weight, 1, pair_me)], axis=1),
        ),
        tuple(first_arrived or ()),
    )
    down_own = lax.all_gather(my_down, "img", axis=0).reshape(-1, model_width)
    second_part, second_arrived = start_gather(my_second)

    first_set = end_gather(first_part, first_arrived)
    qkv_cols = first_set[:, :shard].reshape(model_width, group)
    params = first_set[:, shard:].reshape(n_img, -1).astype(F32)

    def param(start, width):
        return params[:, start * shard : (start + width) * shard].reshape(-1)

    gain_first, shift_first, bias_out = param(0, 1)[None], param(1, 1)[None], param(2, 1)[None]
    gain_second, shift_second, bias_down = param(3, 1)[None], param(4, 1)[None], param(5, 1)[None]
    pair_bias, bias_up = param(6, 2), param(8, 4).reshape(n_img, 2, ff_half)
    bias_up = jnp.concatenate(
        [
            lax.dynamic_index_in_dim(bias_up, which, 1, keepdims=False).reshape(1, -1)
            for which in (pair_me, 1 - pair_me)
        ],
        axis=1,
    )

    paired = lax.dynamic_slice_in_dim(
        pair_bias.reshape(HEADS, 2, HEAD_DIM), me * heads_here, heads_here, 0
    )
    head_bias = jnp.concatenate(
        [paired[:, :1], jnp.zeros((heads_here, 1, HEAD_DIM), F32), paired[:, 1:]], axis=1
    ).reshape(1, group)

    slot_normed, slot_qkv, slot_attended = [], [], []
    for slot in range(slot_count):
        after = ()
        if slot == 1 and second_arrived is not None:
            after = tuple(second_arrived)
        normed, qkv_rows, attended = slot_forward(
            slot_tokens[slot], gain_first, shift_first, qkv_cols, head_bias, key_mask, after
        )
        slot_normed.append(normed)
        slot_qkv.append(qkv_rows)
        slot_attended.append(
            [attended[0]] + [xor_send(attended[r], "seq", r) for r in range(1, n_seq)]
        )
    second_set = end_gather(second_part, second_arrived).reshape(model_width, -1)
    up_own, out_own = second_set[:, : ff // 2], second_set[:, ff // 2 :]
    up_other = xor_send(up_own, "seq", 1)
    down_other = xor_send(down_own, "seq", 1)
    out_full = in_pair_order(out_own, xor_send(out_own, "seq", 1), 1)
    out_full = out_full.reshape(n_seq, group_width, model_width)
    out_groups = jnp.stack(
        [lax.dynamic_index_in_dim(out_full, me ^ r, 0, keepdims=False) for r in range(n_seq)]
    )
    attended_groups = jnp.stack(
        [jnp.stack([parts[r] for parts in slot_attended]) for r in range(n_seq)]
    )

    (
        layer_out,
        grad_residual,
        grad_attended,
        grad_out_groups,
        vectors,
        grad_up_own,
        grad_up_other,
        grad_up_bias,
        grad_down_own,
        grad_down_other,
    ) = feed_forward(
        tokens,
        attended_groups,
        cotangent,
        valid_rows,
        out_groups,
        bias_out,
        gain_second,
        shift_second,
        bias_down,
        up_own,
        up_other,
        bias_up,
        down_own,
        down_other,
    )

    slot_grads = []
    for slot in range(slot_count):
        slot_grads.append(
            [grad_attended[0, slot]]
            + [xor_send(grad_attended[r, slot], "seq", r) for r in range(1, n_seq)]
        )

    down_sum = grad_down_own.astype(F32) + xor_send(grad_down_other, "seq", 1).astype(F32)
    own_down = scatter_img(down_sum.astype(BF16).reshape(n_img, ff_half, model_width))
    up_sum = grad_up_own.astype(F32) + xor_send(grad_up_other, "seq", 1).astype(F32)
    grad_out_weight = jnp.concatenate(
        [lax.dynamic_index_in_dim(grad_out_groups, me ^ r, 0, keepdims=False) for r in range(n_seq)],
        axis=0,
    )
    out_sum = half_of(grad_out_weight, 1, pair_me).astype(F32) + xor_send(
        half_of(grad_out_weight, 1, 1 - pair_me), "seq", 1
    ).astype(F32)
    second_grads = jnp.concatenate([up_sum, out_sum], axis=1).astype(BF16)
    second_grads = second_grads.reshape(n_img, shard, -1)
    stages = [(), (), ()]
    if few_devices():
        sums = reduce_inner(second_grads)
        own_second = reduce_outer(sums)
        stages = [(), (), (sums,)]
    else:
        own_second = scatter_img(second_grads)

    grad_columns = jnp.zeros((model_width, group), F32)
    bias_sums = jnp.zeros((group,), F32)
    norm_sums = jnp.zeros((8, model_width), F32)
    own_sums = []
    for slot in range(slot_count):
        *shares, grad_columns, slot_norm, slot_bias = slot_backward(
            slot_grads[slot],
            slot_tokens[slot],
            slot_qkv[slot],
            slot_normed[slot],
            qkv_cols,
            grad_columns,
            stages[min(slot, 2)],
        )
        norm_sums += slot_norm
        bias_sums += slot_bias[0]
        pair = xor_send(shares[1], "seq", 1).astype(F32)
        across = xor_send(shares[3], "seq", 1).astype(F32)
        across = xor_send((shares[2] + across).astype(BF16), "seq", 2)
        own_sums.append(shares[0] + pair + across.astype(F32))
    columns = grad_columns.astype(BF16).reshape(n_img, shard, group)
    if few_devices():
        own_columns = reduce_outer(reduce_inner(columns))
    else:
        own_columns = scatter_img(columns)
    own_columns = own_columns.astype(BF16)

    grad_norm_first = jnp.concatenate(own_sums, axis=0)
    unit, factor = normalize(tokens.reshape(row_count, model_width).astype(F32))
    scaled = grad_norm_first * gain_first
    mean_scaled = jnp.mean(scaled, axis=-1, keepdims=True)
    mean_product = jnp.mean(scaled * unit, axis=-1, keepdims=True)
    grad_inputs = factor * (scaled - mean_scaled - unit * mean_product)
    tokens_grad = grad_residual + grad_inputs.reshape(grad_residual.shape)

    by_sender = jnp.stack(
        [own_columns] + [xor_send(own_columns, "seq", r) for r in range(1, n_seq)]
    )
    share_qkv = jnp.concatenate(
        [lax.dynamic_index_in_dim(by_sender, me ^ g, 0, keepdims=False) for g in range(n_seq)],
        axis=1,
    ).astype(F32)
    second_low, second_other = over_pieces(own_second)
    up_low = second_low[:, : ff // 2].reshape(shard, n_img, 1, ff_half)
    up_there = second_other[:, : ff // 2].reshape(shard, n_img, 1, ff_half)
    share_up = in_pair_order(up_low, up_there, 2).reshape(shard, ff).astype(F32)
    share_out = in_pair_order(second_low[:, ff // 2 :], second_other[:, ff // 2 :], 1).astype(F32)
    share_down = in_pair_order(*over_pieces(own_down), 0).astype(F32)

    bias_sums = bias_sums.reshape(heads_here, 3, HEAD_DIM)
    grad_pairs = jnp.concatenate([bias_sums[:, :1], bias_sums[:, 2:]], axis=1).reshape(-1)
    grad_pairs = lax.dynamic_update_slice_in_dim(
        jnp.zeros((2 * D,), F32), grad_pairs, me * grad_pairs.shape[0], 0
    )
    up_halves = grad_up_bias.reshape(2, n_img, 1, ff_half)
    grad_up_bias = in_pair_order(up_halves[0], up_halves[1], 1).reshape(-1)
    all_vectors = [
        norm_sums[0],
        norm_sums[1],
        grad_pairs,
        vectors[2],
        vectors[0],
        vectors[1],
        grad_up_bias,
        vectors[3],
    ]
    mine = sum_vectors(jnp.concatenate([v.reshape(n_img, -1) for v in all_vectors], axis=1))
    shares, at = [], 0
    for v in all_vectors:
        size = v.shape[0] // n_img
        shares.append(mine[at : at + size])
        at += size
    return (
        layer_out,
        tokens_grad,
        shares[0],
        shares[1],
        share_qkv,
        shares[2],
        share_out,
        shares[3],
        shares[4],
        shares[5],
        share_up,
        shares[6],
        share_down,
        shares[7],
    )


def solution(mesh):
    placed = (
        P("img", "seq", None),
        P("img", "seq", None),
        P("img"),
        P(),
        P("img"),
        P("img"),
        P("img", None),
        P("img"),
        P("img", None),
        P("img"),
        P("img"),
        P("img"),
        P("img", None),
        P("img"),
        P("img", None),
        P("img"),
    )
    return jax.shard_map(
        local,
        mesh=mesh,
        in_specs=placed,
        out_specs=(
            P("img", "seq", None),
            P("img", "seq", None),
            P("img"),
            P("img"),
            P("img", None),
            P("img"),
            P("img", None),
            P("img"),
            P("img"),
            P("img"),
            P("img", None),
            P("img"),
            P("img", None),
            P("img"),
        ),
        check_vma=False,
    )
```

```python
from functools import partial

import jax
import jax.numpy as jnp
import numpy as np
from jax import lax
from jax.experimental import pallas as pl
from jax.experimental.pallas import tpu as pltpu
from jax.sharding import PartitionSpec as P

D = 768
HEADS = 12
HEAD_DIM = 64
EPS = 1e-06
NEG = -1e30
LANES = 128
F32 = jnp.float32
BF16 = jnp.bfloat16
VMEM_BYTES = 60 * 1024 * 1024
def cost(giga_flops):
    return pl.CostEstimate(
        flops=giga_flops * 10**9, bytes_accessed=10**7, transcendentals=10**6
    )


def mm(left, right, left_dim=1, right_dim=0):
    return lax.dot_general(
        left, right, (((left_dim,), (right_dim,)), ((), ())), preferred_element_type=F32
    )


def normalize(features):
    row_mean = jnp.mean(features, axis=-1, keepdims=True)
    centred = features - row_mean
    spread = jnp.mean(centred * centred, axis=-1, keepdims=True)
    factor = lax.rsqrt(spread + EPS)
    return centred * factor, factor


def round_up(size, unit):
    return -(-size // unit) * unit


def head_columns(heads, parts):
    place = np.zeros((heads * parts, LANES, heads * parts * HEAD_DIM), np.float32)
    for b in range(heads * parts):
        for d in range(HEAD_DIM):
            place[b, d, b * HEAD_DIM + d] = 1.0
    return jnp.asarray(place, BF16)


def lane_columns(heads):
    pick = np.zeros((3 * heads, LANES, LANES), np.float32)
    ones = np.zeros((3 * heads, 1, LANES), np.float32)
    for b in range(3 * heads):
        start = b * HEAD_DIM % LANES
        for d in range(HEAD_DIM):
            pick[b, start + d, d] = HEAD_DIM**-0.5 if b % 3 == 0 else 1.0
        if b % 3 != 1:
            ones[b, 0, HEAD_DIM] = 1.0
    return jnp.asarray(pick, BF16), jnp.asarray(ones, F32)


def query_block(rows):
    for size in range(min(rows, 400) // 16 * 16, 15, -16):
        if rows % size == 0:
            return size
    return rows


def after_specs(after):
    return [pl.BlockSpec(memory_space=pl.ANY)] * len(after)


def piece_spec(array, *at):
    rest = array.shape[len(at) :]
    return pl.BlockSpec((None,) * len(at) + rest, lambda i: at + (0,) * len(rest))


def piece_specs(pieces):
    return [piece_spec(*piece) for piece in pieces]


def whole_specs(count):
    return [pl.BlockSpec(memory_space=pltpu.VMEM)] * count


def forward_kernel(n_seq, heads, n_after, *refs):
    tokens, refs = refs[:n_seq], refs[n_seq + n_after :]
    gain, shift, weight, bias, key_mask, pick, ones, place = refs[:8]
    normed_out, qkv_out = refs[8:10]
    attended_out, (rows, attended) = refs[10 : 10 + n_seq], refs[10 + n_seq :]
    piece = tokens[0].shape[0]
    total = n_seq * piece
    for r in range(n_seq):
        unit, _ = normalize(tokens[r][...].astype(F32))
        rows[r * piece : (r + 1) * piece, :] = unit * gain[...] + shift[...]
    normed = rows[...].astype(BF16)
    normed_out[...] = normed
    qkv = (mm(normed, weight[...]) + bias[...]).astype(BF16)
    width = qkv.shape[1]
    block = query_block(total)
    pad = qkv_out.shape[1] - total
    parts = []
    for b in range(3 * heads):
        start = b * HEAD_DIM // LANES * LANES
        size = min(LANES, width - start)
        part = mm(qkv[:, start : start + size], pick[b, :size]) + ones[b]
        if b % 3 == 1:
            part = part + key_mask[...]
        part = part.astype(BF16)
        qkv_out[b, :total] = part
        if pad:
            qkv_out[b, total:] = jnp.zeros((pad, LANES), BF16)
        parts.append(part)

    tasks = [(at, h) for at in range(0, total, block) for h in range(heads)]

    def score(task):
        at, h = task
        return mm(parts[3 * h][at : at + block], parts[3 * h + 1], 1, 1)

    scores = score(tasks[0])
    placed = None
    for index, (at, h) in enumerate(tasks):
        following = score(tasks[index + 1]) if index + 1 < len(tasks) else None
        peak = jnp.max(scores, axis=-1, keepdims=True)
        terms = jnp.exp(scores - peak).astype(BF16)
        weighted = mm(terms, parts[3 * h + 2])
        result = (weighted / weighted[:, HEAD_DIM : HEAD_DIM + 1]).astype(BF16)
        here = mm(result, place[h])
        placed = here if h == 0 else placed + here
        if h == heads - 1:
            attended[at : at + block, :] = placed
        scores = following
    for r in range(n_seq):
        attended_out[r][...] = attended[r * piece : (r + 1) * piece, :].astype(BF16)


def slot_forward(pieces, gain, shift, weight, bias, key_mask, after=()):
    n_seq = len(pieces)
    piece, width = pieces[0][0].shape[-2:]
    heads = weight.shape[1] // (3 * HEAD_DIM)
    total = n_seq * piece
    padded = round_up(total, LANES)
    return pl.pallas_call(
        partial(forward_kernel, n_seq, heads, len(after)),
        grid=(1,),
        in_specs=piece_specs(pieces) + after_specs(after) + whole_specs(8),
        out_shape=(
            jax.ShapeDtypeStruct((total, width), BF16),
            jax.ShapeDtypeStruct((3 * heads, padded, LANES), BF16),
            *[jax.ShapeDtypeStruct((piece, heads * HEAD_DIM), BF16)] * n_seq,
        ),
        scratch_shapes=[
            pltpu.VMEM((total, width), F32),
            pltpu.VMEM((total, heads * HEAD_DIM), F32),
        ],
        compiler_params=pltpu.CompilerParams(vmem_limit_bytes=VMEM_BYTES),
        cost_estimate=cost(14),
        name="slot_forward",
    )(
        *[p[0] for p in pieces], *after, gain, shift, weight, bias, key_mask, *lane_columns(heads),
        head_columns(heads, 1),
    )


def backward_kernel(n_seq, heads, n_after, *refs):
    grads, refs = refs[:n_seq], refs[n_seq + n_after :]
    tokens, refs = refs[:n_seq], refs[n_seq:]
    qkv, normed, weight, before, place, spread = refs[:6]
    own, across, pairs, grad_weight, vectors, grad_bias, rows, wide = refs[6:]
    piece = grads[0].shape[0]
    total = n_seq * piece
    padded = qkv.shape[1]
    for r in range(n_seq):
        rows[r * piece : (r + 1) * piece, :] = grads[r][...].astype(F32)
    if padded > total:
        rows[total:, :] = jnp.zeros((padded - total, rows.shape[1]), F32)
    grad_rows = rows[...].astype(BF16)
    grad_heads = [mm(grad_rows, place[h], 1, 1).astype(BF16) for h in range(heads)]
    block = 4 * LANES
    tasks = [(h, at) for h in range(heads) for at in range(0, padded, block)]

    def products(task):
        h, at = task
        end = min(at + block, padded)
        scores = mm(qkv[3 * h + 1, :total], qkv[3 * h, at:end], 1, 1)
        return scores, mm(qkv[3 * h + 2, :total], grad_heads[h][at:end], 1, 1)

    current = products(tasks[0])
    grad_qkv = None
    for index, (h, at) in enumerate(tasks):
        following = products(tasks[index + 1]) if index + 1 < len(tasks) else None
        if at == 0:
            keys_t = jnp.transpose(qkv[3 * h + 1])[:, :total]
            grad_keys = jnp.zeros((total, LANES), F32)
            grad_values = jnp.zeros((total, LANES), F32)
            grad_queries = []
        end = min(at + block, padded)
        scores, grad_probs = current
        peak = jnp.max(scores, axis=0, keepdims=True)
        terms = jnp.exp(scores - peak)
        probs = terms * (1.0 / jnp.sum(terms, axis=0, keepdims=True))
        inner = jnp.sum(probs * grad_probs, axis=0, keepdims=True)
        grad_scores = (probs * (grad_probs - inner)).astype(BF16)
        grad_values = grad_values + mm(probs.astype(BF16), grad_heads[h][at:end])
        grad_keys = grad_keys + mm(grad_scores, qkv[3 * h, at:end])
        grad_queries.append(jnp.transpose(mm(keys_t, grad_scores)))
        if end == padded:
            queries = jnp.concatenate(grad_queries, axis=0)[:total] * (HEAD_DIM**-0.5)
            for t, part in enumerate((queries, grad_keys, grad_values)):
                placed = mm(part.astype(BF16), spread[3 * h + t])
                grad_qkv = placed if grad_qkv is None else grad_qkv + placed
        current = following
    grad_low = grad_qkv.astype(BF16)
    grad_bias[...] = jnp.broadcast_to(
        jnp.sum(grad_low.astype(F32), axis=0, keepdims=True), grad_bias.shape
    )
    grad_weight[...] = before[...] + mm(normed[...], grad_low, 0, 0)
    wide[...] = mm(grad_low, weight[...], 1, 1)
    by_unit = jnp.zeros((1, wide.shape[1]), F32)
    by_one = jnp.zeros((1, wide.shape[1]), F32)
    for r in range(n_seq):
        share = wide[r * piece : (r + 1) * piece, :]
        unit, _ = normalize(tokens[r][...].astype(F32))
        by_unit = by_unit + jnp.sum(share * unit, axis=0, keepdims=True)
        by_one = by_one + jnp.sum(share, axis=0, keepdims=True)
        if r & 1:
            pairs[r // 2] = share.astype(BF16)
        else:
            (own if r == 0 else across)[...] = share
    vectors[...] = jnp.zeros(vectors.shape, F32)
    vectors[0:1, :] = by_unit
    vectors[1:2, :] = by_one


def slot_backward(grads, tokens, qkv, normed, weight, before, after=()):
    n_seq = len(grads)
    piece, width = grads[0][0].shape[-2:]
    heads = qkv.shape[0] // 3
    total = n_seq * piece
    model = normed.shape[1]
    return pl.pallas_call(
        partial(backward_kernel, n_seq, heads, len(after)),
        grid=(1,),
        in_specs=piece_specs(grads) + after_specs(after) + piece_specs(tokens) + whole_specs(6),
        out_shape=(
            jax.ShapeDtypeStruct((piece, model), F32),
            jax.ShapeDtypeStruct((piece, model), F32),
            jax.ShapeDtypeStruct((n_seq // 2, piece, model), BF16),
            jax.ShapeDtypeStruct((model, 3 * width), F32),
            jax.ShapeDtypeStruct((8, model), F32),
            jax.ShapeDtypeStruct((8, 3 * width), F32),
        ),
        scratch_shapes=[
            pltpu.VMEM((qkv.shape[1], width), F32),
            pltpu.VMEM((total, model), F32),
        ],
        compiler_params=pltpu.CompilerParams(vmem_limit_bytes=VMEM_BYTES),
        cost_estimate=cost(12),
        name="slot_backward",
    )(
        *[g[0] for g in grads], *after, *[t[0] for t in tokens], qkv, normed, weight, before,
        head_columns(heads, 1), head_columns(heads, 3),
    )


def gate_kernel(*refs):
    pass


def once_there(array, after):
    if not after:
        return array
    return pl.pallas_call(
        gate_kernel,
        in_specs=after_specs((array,) + tuple(after)),
        out_specs=pl.BlockSpec(memory_space=pl.ANY),
        out_shape=jax.ShapeDtypeStruct(array.shape, array.dtype),
        input_output_aliases={0: 0},
        name="once_there",
    )(array, *after)


def mlp_kernel(slots, groups, *refs):
    attended, refs = refs[: slots * groups], refs[slots * groups :]
    (
        tokens, cotangent, valid, out_weight, bias_out, gain, shift, bias_down, up_own, up_other,
        bias_up, down_own, down_other, layer_out, grad_residual,
    ) = refs[:15]
    grad_first, refs = refs[15 : 15 + groups], refs[15 + groups :]
    grad_rest, refs = refs[:groups], refs[groups:]
    (
        grad_out_weight, vectors, grad_up_own, grad_up_other, grad_up_bias, grad_down_own,
        grad_down_other, staged, residual, output, grad_norm, normed, normed_t, grad_out, heads_in,
    ) = refs
    step = pl.program_id(0)
    piece, width = tokens.shape[1:]
    head_width = attended[0].shape[-1]
    rows = slots * piece
    padded = residual.shape[0]

    def stage(source):
        for s in range(slots):
            staged[s * piece : (s + 1) * piece, : source.shape[-1]] = source[s].astype(F32)

    @pl.when(step == 0)
    def _():
        if padded > rows:
            staged[rows:, :] = jnp.zeros((padded - rows, width), F32)
        for r in range(groups):
            for s in range(slots):
                staged[s * piece : (s + 1) * piece, :head_width] = attended[r * slots + s][
                    ...
                ].astype(F32)
            heads_in[r] = staged[:, :head_width].astype(BF16)
        stage(cotangent)
        grad_out[...] = (staged[...] * valid[...]).astype(BF16)
        stage(tokens)
        total = staged[...] + bias_out[...]
        for r in range(groups):
            total = total + mm(heads_in[r], out_weight[r])
        residual[...] = total
        unit, _ = normalize(total)
        normed_here = (unit * gain[...] + shift[...]).astype(BF16)
        normed[...] = normed_here
        normed_t[...] = jnp.transpose(normed_here)
        output[...] = total + bias_down[...]
        grad_norm[...] = jnp.zeros_like(grad_norm)

    first = step < pl.num_programs(0) // 2
    up = jnp.where(first, up_own[...], up_other[...])
    down = jnp.where(first, down_own[...], down_other[...])
    hidden = mm(normed[...], up) + bias_up[...]
    share = 0.5 * (1.0 + lax.erf(hidden * np.float32(np.sqrt(0.5))))
    density = jnp.exp(-0.5 * hidden * hidden) * np.float32(1.0 / np.sqrt(2.0 * np.pi))
    activated = (hidden * share).astype(BF16)
    grad_hidden = (mm(grad_out[...], down, 1, 1) * (share + hidden * density)).astype(BF16)
    output[...] += mm(activated, down)
    grad_norm[...] += mm(grad_hidden, up, 1, 1)
    grad_up = mm(normed_t[...], grad_hidden).astype(BF16)
    grad_down = mm(activated, grad_out[...], 0, 0).astype(BF16)

    @pl.when(first)
    def _():
        grad_up_own[...] = grad_up
        grad_down_own[...] = grad_down

    @pl.when(jnp.logical_not(first))
    def _():
        grad_up_other[...] = grad_up
        grad_down_other[...] = grad_down

    grad_up_bias[...] = jnp.sum(grad_hidden.astype(F32), axis=0, keepdims=True)

    @pl.when(step == pl.num_programs(0) - 1)
    def _():
        staged[...] = output[...] * valid[...]
        for s in range(slots):
            layer_out[s] = staged[s * piece : (s + 1) * piece, :].astype(BF16)
        grad_low = grad_out[...].astype(F32)
        unit, factor = normalize(residual[...])
        back = grad_norm[...]
        scaled = back * gain[...]
        mean_scaled = jnp.mean(scaled, axis=-1, keepdims=True)
        mean_product = jnp.mean(scaled * unit, axis=-1, keepdims=True)
        total = grad_low + factor * (scaled - mean_scaled - unit * mean_product)
        staged[...] = total
        for s in range(slots):
            grad_residual[s] = staged[s * piece : (s + 1) * piece, :]
        branch = total.astype(BF16)
        vectors[0:1, :] = jnp.sum(back * unit, axis=0, keepdims=True)
        vectors[1:2, :] = jnp.sum(back, axis=0, keepdims=True)
        vectors[2:3, :] = jnp.sum(branch.astype(F32), axis=0, keepdims=True)
        vectors[3:4, :] = jnp.sum(grad_low, axis=0, keepdims=True)
        vectors[4:8, :] = jnp.zeros((4, width), F32)
        for r in range(groups):
            grad_out_weight[r] = mm(heads_in[r], branch, 0, 0).astype(BF16)
            staged[:, :head_width] = mm(branch, out_weight[r], 1, 1)
            grad_first[r][...] = staged[:piece, :head_width].astype(BF16)
            for s in range(1, slots):
                grad_rest[r][s - 1] = staged[s * piece : (s + 1) * piece, :head_width].astype(BF16)


def feed_forward(
    attended, tokens, cotangent, valid, out_weight, bias_out, gain, shift, bias_down, up_own,
    up_other, bias_up, down_own, down_other,
):
    slots, piece, width = tokens.shape
    groups, head_width = len(attended), attended[0][0].shape[-1]
    first = jax.ShapeDtypeStruct((piece, head_width), BF16)
    others = jax.ShapeDtypeStruct((slots - 1, piece, head_width), BF16)
    ff = 2 * up_own.shape[1]
    chunk = 384
    half = ff // 2 // chunk
    padded = round_up(slots * piece, 16)
    whole = lambda shape: pl.BlockSpec(
        shape, lambda i: (0,) * len(shape), pipeline_mode=pl.Buffered(1)
    )
    own = lambda i: jnp.minimum(i, half - 1)
    other = lambda i: jnp.maximum(i - half, 0)
    by_columns = [pl.BlockSpec((width, chunk), lambda i, at=at: (0, at(i))) for at in (own, other)]
    by_rows = [pl.BlockSpec((chunk, width), lambda i, at=at: (at(i), 0)) for at in (own, other)]
    bias_block = pl.BlockSpec((1, chunk), lambda i: (0, i))
    row = whole((1, width))
    return pl.pallas_call(
        partial(mlp_kernel, slots, groups),
        grid=(ff // chunk,),
        in_specs=[
            *[whole(first.shape)] * (groups * slots),
            whole(tokens.shape),
            whole(cotangent.shape),
            whole((padded, 1)),
            whole(out_weight.shape),
            row,
            row,
            row,
            row,
            *by_columns,
            bias_block,
            *by_rows,
        ],
        out_specs=[
            whole(tokens.shape),
            whole(tokens.shape),
            *[whole(first.shape)] * groups,
            *[whole(others.shape)] * groups,
            whole(out_weight.shape),
            whole((8, width)),
            *by_columns,
            bias_block,
            *by_rows,
        ],
        out_shape=[
            jax.ShapeDtypeStruct(tokens.shape, BF16),
            jax.ShapeDtypeStruct(tokens.shape, F32),
            *[first] * groups,
            *[others] * groups,
            jax.ShapeDtypeStruct(out_weight.shape, BF16),
            jax.ShapeDtypeStruct((8, width), F32),
            jax.ShapeDtypeStruct(up_own.shape, BF16),
            jax.ShapeDtypeStruct(up_own.shape, BF16),
            jax.ShapeDtypeStruct((1, ff), F32),
            jax.ShapeDtypeStruct(down_own.shape, BF16),
            jax.ShapeDtypeStruct(down_own.shape, BF16),
        ],
        scratch_shapes=[
            pltpu.VMEM((padded, width), F32),
            pltpu.VMEM((padded, width), F32),
            pltpu.VMEM((padded, width), F32),
            pltpu.VMEM((padded, width), F32),
            pltpu.VMEM((padded, width), BF16),
            pltpu.VMEM((width, padded), BF16),
            pltpu.VMEM((padded, width), BF16),
            pltpu.VMEM((groups, padded, head_width), BF16),
        ],
        compiler_params=pltpu.CompilerParams(
            vmem_limit_bytes=VMEM_BYTES, dimension_semantics=("arbitrary",)
        ),
        cost_estimate=cost(55),
        name="feed_forward",
    )(
        *[part for group in attended for part in group], tokens, cotangent, valid, out_weight, bias_out, gain, shift, bias_down, up_own,
        up_other, bias_up, down_own, down_other,
    )


def xor_send(block, axis, bits):
    n = lax.axis_size(axis)
    return lax.ppermute(block, axis, [(i, i ^ bits) for i in range(n)])


INNER = 2


def outer_send(block, shift):
    outer = lax.axis_size("img") // INNER
    return lax.ppermute(
        block,
        "img",
        [
            (z * INNER + y, ((z + shift) % outer) * INNER + y)
            for z in range(outer)
            for y in range(INNER)
        ],
    )


def few_devices():
    return lax.axis_size("img") <= 16


def place_outer(block, arrived):
    outer = lax.axis_size("img") // INNER
    z = lax.axis_index("img") // INNER
    placed = jnp.zeros((outer,) + block.shape, block.dtype)
    for k, part in enumerate([block] + arrived):
        placed = lax.dynamic_update_slice_in_dim(placed, part[None], (z + outer - k) % outer, 0)
    return placed


def gather_inner(placed):
    other = xor_send(placed, "img", 1)
    first = (lax.axis_index("img") & 1) == 0
    both = jnp.stack([jnp.where(first, placed, other), jnp.where(first, other, placed)], axis=1)
    return both.reshape((-1,) + placed.shape[1:])


def start_gather(block):
    if not few_devices():
        return lax.all_gather(block, "img", axis=0), None
    outer = lax.axis_size("img") // INNER
    return block, [outer_send(block, k) for k in range(1, outer)]


def end_gather(block, arrived):
    if arrived is None:
        return block
    return gather_inner(place_outer(block, arrived))


def reduce_inner(parts):
    outer = lax.axis_size("img") // INNER
    split = parts.reshape((outer, INNER) + parts.shape[1:])
    me = lax.axis_index("img") % INNER
    send = lax.dynamic_index_in_dim(split, 1 - me, 1, keepdims=False)
    keep = lax.dynamic_index_in_dim(split, me, 1, keepdims=False)
    return keep.astype(F32) + xor_send(send, "img", 1).astype(F32)


def reduce_outer(sums):
    outer = sums.shape[0]
    z = lax.axis_index("img") // INNER
    total = lax.dynamic_index_in_dim(sums, z, 0, keepdims=False)
    for k in range(1, outer):
        send = lax.dynamic_index_in_dim(sums, (z + k) % outer, 0, keepdims=False)
        total = total + outer_send(send.astype(BF16), k).astype(F32)
    return total


def scatter_img(parts):
    return lax.psum_scatter(parts, "img", scatter_dimension=0, tiled=False).astype(F32)


def in_pair_order(own, other, axis):
    first = (lax.axis_index("seq") & 1) == 0
    return jnp.where(
        first, jnp.concatenate([own, other], axis), jnp.concatenate([other, own], axis)
    )


def half_of(block, axis, which):
    size = block.shape[axis] // 2
    return lax.dynamic_slice_in_dim(block, which * size, size, axis)


def over_pieces(total):
    low = total.astype(BF16)
    low = (low.astype(F32) + xor_send(low, "seq", 2).astype(F32)).astype(BF16)
    return low, xor_send(low, "seq", 1)


def local(
    tokens,
    cotangent,
    images_held,
    piece_rows,
    norm_gain,
    norm_shift,
    qkv_weight,
    qkv_bias,
    out_weight,
    out_bias,
    mlp_gain,
    mlp_shift,
    up_weight,
    up_bias,
    down_weight,
    down_bias,
):
    slot_count, piece_size, model_width = tokens.shape
    n_seq = lax.axis_size("seq")
    n_img = lax.axis_size("img")
    me = lax.axis_index("seq")
    pair_me = me & 1
    own_img = lax.axis_index("img")
    row_count = slot_count * piece_size
    heads_here = HEADS // n_seq
    group = 3 * D // n_seq
    group_width = heads_here * HEAD_DIM
    shard = D // n_img
    ff = up_weight.shape[1]
    ff_half = ff // n_img // 2
    blocks = 3 * heads_here

    rows_of = piece_rows[me ^ jnp.arange(n_seq)]
    key_valid = (jnp.arange(piece_size)[None, :] < rows_of[:, None]).reshape(n_seq * piece_size)
    live_slots = jnp.arange(slot_count) < images_held[0]
    valid_rows = (live_slots[:, None] & key_valid[None, :piece_size]).reshape(row_count)
    valid_rows = jnp.pad(valid_rows, (0, round_up(row_count, 16) - row_count))
    valid_rows = valid_rows.astype(F32)[:, None]
    key_mask = jnp.where(
        key_valid[:, None] | (jnp.arange(LANES) != HEAD_DIM)[None, :], 0.0, NEG
    ).astype(F32)

    small = [norm_gain, norm_shift, out_bias, mlp_gain, mlp_shift, down_bias, qkv_bias, up_bias]
    small = [jnp.pad(v[None], ((0, 0), (0, group - v.shape[0]))) for v in small]
    small.append(jnp.zeros((8, group), BF16))
    my_columns = lax.dynamic_slice_in_dim(qkv_weight, me * group, group, 1)
    first_part, first_arrived = start_gather(jnp.concatenate([my_columns] + small, axis=0))

    pair = xor_send(tokens, "seq", 1)
    across = [xor_send(tokens[0], "seq", 2), xor_send(tokens[1:], "seq", 2)]
    diagonal = [xor_send(part, "seq", 1) for part in across]
    slot_tokens = [[(tokens, 0), (pair, 0), (across[0],), (diagonal[0],)]]
    for slot in range(1, slot_count):
        slot_tokens.append(
            [(tokens, slot), (pair, slot), (across[1], slot - 1), (diagonal[1], slot - 1)]
        )

    my_up = lax.dynamic_index_in_dim(
        up_weight.reshape(shard, n_img, 2, ff_half), pair_me, 2, keepdims=False
    ).reshape(shard, -1)
    my_down = once_there(half_of(down_weight, 0, pair_me), tuple(first_arrived or ()))
    down_own = lax.all_gather(my_down, "img", axis=0).reshape(-1, model_width)

    first_set = end_gather(first_part, first_arrived)
    my_second = jnp.concatenate([my_up, half_of(out_weight, 1, pair_me)], axis=1)
    second_part, second_arrived = start_gather(once_there(my_second, (first_set,)))
    qkv_cols = first_set[:, :shard].reshape(model_width, group)
    params = first_set[:, shard:].astype(F32)

    def param(row, width):
        return params[:, row, : width * shard].reshape(-1)

    gain_first, shift_first, bias_out = param(0, 1)[None], param(1, 1)[None], param(2, 1)[None]
    gain_second, shift_second, bias_down = param(3, 1)[None], param(4, 1)[None], param(5, 1)[None]
    pair_bias, bias_up = param(6, 2), param(7, 4).reshape(n_img, 2, ff_half)
    bias_up = jnp.concatenate(
        [
            lax.dynamic_index_in_dim(bias_up, which, 1, keepdims=False).reshape(1, -1)
            for which in (pair_me, 1 - pair_me)
        ],
        axis=1,
    )

    paired = lax.dynamic_slice_in_dim(
        pair_bias.reshape(HEADS, 2, HEAD_DIM), me * heads_here, heads_here, 0
    )
    head_bias = jnp.concatenate(
        [paired[:, :1], jnp.zeros((heads_here, 1, HEAD_DIM), F32), paired[:, 1:]], axis=1
    ).reshape(1, group)

    slot_normed, slot_qkv, slot_attended = [], [], []
    for slot in range(slot_count):
        after = ()
        if slot > 0:
            after = (slot_attended[-1][0],)
        if slot > 1:
            after = after + tuple(slot_attended[-2][1:])
        normed, qkv_rows, *attended = slot_forward(
            slot_tokens[slot], gain_first, shift_first, qkv_cols, head_bias, key_mask, after
        )
        slot_normed.append(normed)
        slot_qkv.append(qkv_rows)
        slot_attended.append(
            [attended[0]] + [xor_send(attended[r], "seq", r) for r in range(1, n_seq)]
        )
    down_own = once_there(down_own, (slot_attended[-1][0],))
    if second_arrived is not None:
        second_arrived = [once_there(part, (slot_attended[1][0],)) for part in second_arrived]
    second_set = end_gather(second_part, second_arrived).reshape(model_width, -1)
    up_own, out_own = second_set[:, : ff // 2], second_set[:, ff // 2 :]
    up_other = xor_send(up_own, "seq", 1)
    down_other = xor_send(down_own, "seq", 1)
    out_full = in_pair_order(out_own, xor_send(out_own, "seq", 1), 1)
    out_full = out_full.reshape(n_seq, group_width, model_width)
    out_groups = jnp.stack(
        [lax.dynamic_index_in_dim(out_full, me ^ r, 0, keepdims=False) for r in range(n_seq)]
    )
    attended_groups = [[parts[r] for parts in slot_attended] for r in range(n_seq)]

    layer_out, grad_residual, *rest = feed_forward(
        attended_groups,
        tokens,
        cotangent,
        valid_rows,
        out_groups,
        bias_out,
        gain_second,
        shift_second,
        bias_down,
        up_own,
        up_other,
        bias_up,
        down_own,
        down_other,
    )
    grad_first, grad_rest, rest = rest[:n_seq], rest[n_seq : 2 * n_seq], rest[2 * n_seq :]
    grad_out_groups, vectors, grad_up_own, grad_up_other = rest[:4]
    grad_up_bias, grad_down_own, grad_down_other = rest[4:]
    for r in range(1, n_seq):
        grad_first[r] = xor_send(grad_first[r], "seq", r)
        grad_rest[r] = xor_send(grad_rest[r], "seq", r)
    slot_grads = [[(part,) for part in grad_first]]
    for slot in range(1, slot_count):
        slot_grads.append([(part, slot - 1) for part in grad_rest])

    down_sum = grad_down_own.astype(F32) + xor_send(grad_down_other, "seq", 1).astype(F32)
    down_sum = down_sum.astype(BF16).reshape(n_img, ff_half, model_width)
    own_down = scatter_img(down_sum)
    up_sum = grad_up_own.astype(F32) + xor_send(grad_up_other, "seq", 1).astype(F32)
    grad_out_weight = jnp.concatenate(
        [lax.dynamic_index_in_dim(grad_out_groups, me ^ r, 0, keepdims=False) for r in range(n_seq)],
        axis=0,
    )
    out_sum = half_of(grad_out_weight, 1, pair_me).astype(F32) + xor_send(
        half_of(grad_out_weight, 1, 1 - pair_me), "seq", 1
    ).astype(F32)
    second_grads = jnp.concatenate([up_sum, out_sum], axis=1).astype(BF16)
    second_grads = second_grads.reshape(n_img, shard, -1)
    stages = [(down_sum, second_grads), (), ()]
    if few_devices():
        sums = reduce_inner(second_grads)
        own_second = reduce_outer(sums)
        stages[1:] = [(sums,), (own_second,)]
    else:
        own_second = scatter_img(second_grads)

    grad_columns = jnp.zeros((model_width, group), F32)
    bias_sums = jnp.zeros((group,), F32)
    norm_sums = jnp.zeros((8, model_width), F32)
    own_sums = []
    for slot in range(slot_count):
        own, across, pairs, grad_columns, slot_norm, slot_bias = slot_backward(
            slot_grads[slot],
            slot_tokens[slot],
            slot_qkv[slot],
            slot_normed[slot],
            qkv_cols,
            grad_columns,
            stages[min(slot, 2)],
        )
        norm_sums += slot_norm
        bias_sums += slot_bias[0]
        pairs = xor_send(pairs, "seq", 1)
        across = xor_send((across + pairs[1].astype(F32)).astype(BF16), "seq", 2)
        own_sums.append(own + pairs[0].astype(F32) + across.astype(F32))
    bias_sums = bias_sums.reshape(heads_here, 3, HEAD_DIM)
    grad_pairs = jnp.concatenate([bias_sums[:, :1], bias_sums[:, 2:]], axis=1).reshape(-1)
    grad_pairs = lax.dynamic_update_slice_in_dim(
        jnp.zeros((2 * D,), F32), grad_pairs, me * grad_pairs.shape[0], 0
    )
    up_halves = grad_up_bias.reshape(2, n_img, 1, ff_half)
    grad_up_bias = in_pair_order(up_halves[0], up_halves[1], 1).reshape(-1)
    all_vectors = [
        norm_sums[0],
        norm_sums[1],
        grad_pairs,
        vectors[2],
        vectors[0],
        vectors[1],
        grad_up_bias,
        vectors[3],
    ]
    extra = jnp.concatenate([v.reshape(n_img, -1) for v in all_vectors], axis=1)
    extra_rows = -(-extra.shape[1] // group)
    extra = jnp.pad(extra, ((0, 0), (0, extra_rows * group - extra.shape[1])))
    extra = jnp.pad(
        extra.reshape(n_img, extra_rows, group), ((0, 0), (0, 16 - extra_rows), (0, 0))
    )
    columns = jnp.concatenate([grad_columns.reshape(n_img, shard, group), extra], axis=1)
    columns = columns.astype(BF16)
    if few_devices():
        own_columns = reduce_outer(once_there(reduce_inner(columns), (pairs,)))
    else:
        own_columns = scatter_img(columns)
    own_columns = own_columns.astype(BF16)

    grad_norm_first = jnp.concatenate(own_sums, axis=0)
    unit, factor = normalize(tokens.reshape(row_count, model_width).astype(F32))
    scaled = grad_norm_first * gain_first
    mean_scaled = jnp.mean(scaled, axis=-1, keepdims=True)
    mean_product = jnp.mean(scaled * unit, axis=-1, keepdims=True)
    grad_inputs = factor * (scaled - mean_scaled - unit * mean_product)
    tokens_grad = grad_residual + grad_inputs.reshape(grad_residual.shape)

    by_sender = jnp.stack(
        [own_columns] + [xor_send(own_columns, "seq", r) for r in range(1, n_seq)]
    )
    by_sender = [
        lax.dynamic_index_in_dim(by_sender, me ^ g, 0, keepdims=False) for g in range(n_seq)
    ]
    share_qkv = jnp.concatenate([part[:shard] for part in by_sender], axis=1).astype(F32)
    mine = sum(part[shard : shard + extra_rows].astype(F32) for part in by_sender).reshape(-1)
    second_low, second_other = over_pieces(own_second)
    up_low = second_low[:, : ff // 2].reshape(shard, n_img, 1, ff_half)
    up_there = second_other[:, : ff // 2].reshape(shard, n_img, 1, ff_half)
    share_up = in_pair_order(up_low, up_there, 2).reshape(shard, ff).astype(F32)
    share_out = in_pair_order(second_low[:, ff // 2 :], second_other[:, ff // 2 :], 1).astype(F32)
    share_down = in_pair_order(*over_pieces(own_down), 0).astype(F32)

    shares, at = [], 0
    for v in all_vectors:
        size = v.shape[0] // n_img
        shares.append(mine[at : at + size])
        at += size
    return (
        layer_out,
        tokens_grad,
        shares[0],
        shares[1],
        share_qkv,
        shares[2],
        share_out,
        shares[3],
        shares[4],
        shares[5],
        share_up,
        shares[6],
        share_down,
        shares[7],
    )


def solution(mesh):
    placed = (
        P("img", "seq", None),
        P("img", "seq", None),
        P("img"),
        P(),
        P("img"),
        P("img"),
        P("img", None),
        P("img"),
        P("img", None),
        P("img"),
        P("img"),
        P("img"),
        P("img", None),
        P("img"),
        P("img", None),
        P("img"),
    )
    return jax.shard_map(
        local,
        mesh=mesh,
        in_specs=placed,
        out_specs=(
            P("img", "seq", None),
            P("img", "seq", None),
            P("img"),
            P("img"),
            P("img", None),
            P("img"),
            P("img", None),
            P("img"),
            P("img"),
            P("img"),
            P("img", None),
            P("img"),
            P("img", None),
            P("img"),
        ),
        check_vma=False,
    )
```

```python
from functools import partial

import jax
import jax.numpy as jnp
import numpy as np
from jax import lax
from jax.experimental import pallas as pl
from jax.experimental.pallas import tpu as pltpu
from jax.sharding import PartitionSpec as P

D = 768
HEADS = 12
HEAD_DIM = 64
EPS = 1e-06
NEG = -1e30
LANES = 128
F32 = jnp.float32
BF16 = jnp.bfloat16
VMEM_BYTES = 60 * 1024 * 1024
def cost(giga_flops):
    return pl.CostEstimate(
        flops=giga_flops * 10**9, bytes_accessed=10**7, transcendentals=10**6
    )


def mm(left, right, left_dim=1, right_dim=0):
    return lax.dot_general(
        left, right, (((left_dim,), (right_dim,)), ((), ())), preferred_element_type=F32
    )


def normalize(features):
    row_mean = jnp.mean(features, axis=-1, keepdims=True)
    centred = features - row_mean
    spread = jnp.mean(centred * centred, axis=-1, keepdims=True)
    factor = lax.rsqrt(spread + EPS)
    return centred * factor, factor


def round_up(size, unit):
    return -(-size // unit) * unit


def head_columns(heads, parts):
    place = np.zeros((heads * parts, LANES, heads * parts * HEAD_DIM), np.float32)
    for b in range(heads * parts):
        for d in range(HEAD_DIM):
            place[b, d, b * HEAD_DIM + d] = 1.0
    return jnp.asarray(place, BF16)


def lane_columns(heads):
    pick = np.zeros((3 * heads, LANES, LANES), np.float32)
    ones = np.zeros((3 * heads, 1, LANES), np.float32)
    for b in range(3 * heads):
        start = b * HEAD_DIM % LANES
        for d in range(HEAD_DIM):
            pick[b, start + d, d] = HEAD_DIM**-0.5 if b % 3 == 0 else 1.0
        if b % 3 != 1:
            ones[b, 0, HEAD_DIM] = 1.0
    return jnp.asarray(pick, BF16), jnp.asarray(ones, F32)


def query_block(rows):
    for size in range(min(rows, 400) // 16 * 16, 15, -16):
        if rows % size == 0:
            return size
    return rows


def after_specs(after):
    return [pl.BlockSpec(memory_space=pl.ANY)] * len(after)


def piece_spec(array, *at):
    rest = array.shape[len(at) :]
    return pl.BlockSpec((None,) * len(at) + rest, lambda i: at + (0,) * len(rest))


def piece_specs(pieces):
    return [piece_spec(*piece) for piece in pieces]


def whole_specs(count):
    return [pl.BlockSpec(memory_space=pltpu.VMEM)] * count


def forward_kernel(n_seq, heads, n_after, *refs):
    tokens, refs = refs[:n_seq], refs[n_seq + n_after :]
    gain, shift, weight, bias, key_mask, pick, ones, place = refs[:8]
    normed_out, qkv_out = refs[8:10]
    attended_out, (rows, attended) = refs[10 : 10 + n_seq], refs[10 + n_seq :]
    piece = tokens[0].shape[0]
    total = n_seq * piece
    for r in range(n_seq):
        unit, _ = normalize(tokens[r][...].astype(F32))
        rows[r * piece : (r + 1) * piece, :] = unit * gain[...] + shift[...]
    normed = rows[...].astype(BF16)
    normed_out[...] = normed
    qkv = (mm(normed, weight[...]) + bias[...]).astype(BF16)
    width = qkv.shape[1]
    block = query_block(total)
    pad = qkv_out.shape[1] - total
    parts = []
    for b in range(3 * heads):
        start = b * HEAD_DIM // LANES * LANES
        size = min(LANES, width - start)
        part = mm(qkv[:, start : start + size], pick[b, :size]) + ones[b]
        if b % 3 == 1:
            part = part + key_mask[...]
        part = part.astype(BF16)
        qkv_out[b, :total] = part
        if pad:
            qkv_out[b, total:] = jnp.zeros((pad, LANES), BF16)
        parts.append(part)

    tasks = [(at, h) for at in range(0, total, block) for h in range(heads)]

    def score(task):
        at, h = task
        return mm(parts[3 * h][at : at + block], parts[3 * h + 1], 1, 1)

    scores = score(tasks[0])
    placed = None
    for index, (at, h) in enumerate(tasks):
        following = score(tasks[index + 1]) if index + 1 < len(tasks) else None
        peak = jnp.max(scores, axis=-1, keepdims=True)
        terms = jnp.exp(scores - peak).astype(BF16)
        weighted = mm(terms, parts[3 * h + 2])
        result = (weighted / weighted[:, HEAD_DIM : HEAD_DIM + 1]).astype(BF16)
        here = mm(result, place[h])
        placed = here if h == 0 else placed + here
        if h == heads - 1:
            attended[at : at + block, :] = placed
        scores = following
    for r in range(n_seq):
        attended_out[r][...] = attended[r * piece : (r + 1) * piece, :].astype(BF16)


def slot_forward(pieces, gain, shift, weight, bias, key_mask, after=()):
    n_seq = len(pieces)
    piece, width = pieces[0][0].shape[-2:]
    heads = weight.shape[1] // (3 * HEAD_DIM)
    total = n_seq * piece
    padded = round_up(total, LANES)
    return pl.pallas_call(
        partial(forward_kernel, n_seq, heads, len(after)),
        grid=(1,),
        in_specs=piece_specs(pieces) + after_specs(after) + whole_specs(8),
        out_shape=(
            jax.ShapeDtypeStruct((total, width), BF16),
            jax.ShapeDtypeStruct((3 * heads, padded, LANES), BF16),
            *[jax.ShapeDtypeStruct((piece, heads * HEAD_DIM), BF16)] * n_seq,
        ),
        scratch_shapes=[
            pltpu.VMEM((total, width), F32),
            pltpu.VMEM((total, heads * HEAD_DIM), F32),
        ],
        compiler_params=pltpu.CompilerParams(vmem_limit_bytes=VMEM_BYTES),
        cost_estimate=cost(14),
        name="slot_forward",
    )(
        *[p[0] for p in pieces], *after, gain, shift, weight, bias, key_mask, *lane_columns(heads),
        head_columns(heads, 1),
    )


def backward_kernel(n_seq, heads, n_after, *refs):
    grads, refs = refs[:n_seq], refs[n_seq + n_after :]
    tokens, refs = refs[:n_seq], refs[n_seq:]
    qkv, normed, weight, before, place, spread = refs[:6]
    own, across, pairs, grad_weight, vectors, grad_bias, rows, wide = refs[6:]
    piece = grads[0].shape[0]
    total = n_seq * piece
    padded = qkv.shape[1]
    for r in range(n_seq):
        rows[r * piece : (r + 1) * piece, :] = grads[r][...].astype(F32)
    if padded > total:
        rows[total:, :] = jnp.zeros((padded - total, rows.shape[1]), F32)
    grad_rows = rows[...].astype(BF16)
    grad_heads = [mm(grad_rows, place[h], 1, 1).astype(BF16) for h in range(heads)]
    block = 4 * LANES
    tasks = [(h, at) for h in range(heads) for at in range(0, padded, block)]

    def products(task):
        h, at = task
        end = min(at + block, padded)
        scores = mm(qkv[3 * h + 1, :total], qkv[3 * h, at:end], 1, 1)
        return scores, mm(qkv[3 * h + 2, :total], grad_heads[h][at:end], 1, 1)

    current = products(tasks[0])
    grad_qkv = None
    for index, (h, at) in enumerate(tasks):
        following = products(tasks[index + 1]) if index + 1 < len(tasks) else None
        if at == 0:
            keys_t = jnp.transpose(qkv[3 * h + 1])[:, :total]
            grad_keys = jnp.zeros((total, LANES), F32)
            grad_values = jnp.zeros((total, LANES), F32)
            grad_queries = []
        end = min(at + block, padded)
        scores, grad_probs = current
        peak = jnp.max(scores, axis=0, keepdims=True)
        terms = jnp.exp(scores - peak)
        probs = terms * (1.0 / jnp.sum(terms, axis=0, keepdims=True))
        inner = jnp.sum(probs * grad_probs, axis=0, keepdims=True)
        grad_scores = (probs * (grad_probs - inner)).astype(BF16)
        grad_values = grad_values + mm(probs.astype(BF16), grad_heads[h][at:end])
        grad_keys = grad_keys + mm(grad_scores, qkv[3 * h, at:end])
        grad_queries.append(jnp.transpose(mm(keys_t, grad_scores)))
        if end == padded:
            queries = jnp.concatenate(grad_queries, axis=0)[:total] * (HEAD_DIM**-0.5)
            for t, part in enumerate((queries, grad_keys, grad_values)):
                placed = mm(part.astype(BF16), spread[3 * h + t])
                grad_qkv = placed if grad_qkv is None else grad_qkv + placed
        current = following
    grad_low = grad_qkv.astype(BF16)
    grad_bias[...] = jnp.broadcast_to(
        jnp.sum(grad_low.astype(F32), axis=0, keepdims=True), grad_bias.shape
    )
    grad_weight[...] = before[...] + mm(normed[...], grad_low, 0, 0)
    wide[...] = mm(grad_low, weight[...], 1, 1)
    by_unit = jnp.zeros((1, wide.shape[1]), F32)
    by_one = jnp.zeros((1, wide.shape[1]), F32)
    for r in range(n_seq):
        share = wide[r * piece : (r + 1) * piece, :]
        unit, _ = normalize(tokens[r][...].astype(F32))
        by_unit = by_unit + jnp.sum(share * unit, axis=0, keepdims=True)
        by_one = by_one + jnp.sum(share, axis=0, keepdims=True)
        if r & 1:
            pairs[r // 2] = share.astype(BF16)
        else:
            (own if r == 0 else across)[...] = share
    vectors[...] = jnp.zeros(vectors.shape, F32)
    vectors[0:1, :] = by_unit
    vectors[1:2, :] = by_one


def slot_backward(grads, tokens, qkv, normed, weight, before, after=()):
    n_seq = len(grads)
    piece, width = grads[0][0].shape[-2:]
    heads = qkv.shape[0] // 3
    total = n_seq * piece
    model = normed.shape[1]
    return pl.pallas_call(
        partial(backward_kernel, n_seq, heads, len(after)),
        grid=(1,),
        in_specs=piece_specs(grads) + after_specs(after) + piece_specs(tokens) + whole_specs(6),
        out_shape=(
            jax.ShapeDtypeStruct((piece, model), F32),
            jax.ShapeDtypeStruct((piece, model), F32),
            jax.ShapeDtypeStruct((n_seq // 2, piece, model), BF16),
            jax.ShapeDtypeStruct((model, 3 * width), F32),
            jax.ShapeDtypeStruct((8, model), F32),
            jax.ShapeDtypeStruct((8, 3 * width), F32),
        ),
        scratch_shapes=[
            pltpu.VMEM((qkv.shape[1], width), F32),
            pltpu.VMEM((total, model), F32),
        ],
        compiler_params=pltpu.CompilerParams(vmem_limit_bytes=VMEM_BYTES),
        cost_estimate=cost(1),
        name="slot_backward",
    )(
        *[g[0] for g in grads], *after, *[t[0] for t in tokens], qkv, normed, weight, before,
        head_columns(heads, 1), head_columns(heads, 3),
    )


def gate_kernel(*refs):
    pass


def once_there(array, after):
    if not after:
        return array
    return pl.pallas_call(
        gate_kernel,
        in_specs=after_specs((array,) + tuple(after)),
        out_specs=pl.BlockSpec(memory_space=pl.ANY),
        out_shape=jax.ShapeDtypeStruct(array.shape, array.dtype),
        input_output_aliases={0: 0},
        name="once_there",
    )(array, *after)


def mlp_kernel(slots, groups, *refs):
    attended, refs = refs[: slots * groups], refs[slots * groups :]
    (
        tokens, cotangent, valid, out_weight, bias_out, gain, shift, bias_down, up_own, up_other,
        bias_up, down_own, down_other, layer_out, grad_residual,
    ) = refs[:15]
    grad_first, refs = refs[15 : 15 + groups], refs[15 + groups :]
    grad_rest, refs = refs[:groups], refs[groups:]
    (
        grad_out_weight, vectors, grad_up_own, grad_up_other, grad_up_bias, grad_down_own,
        grad_down_other, staged, residual, output, grad_norm, normed, normed_t, grad_out, heads_in,
    ) = refs
    step = pl.program_id(0)
    piece, width = tokens.shape[1:]
    head_width = attended[0].shape[-1]
    rows = slots * piece
    padded = residual.shape[0]

    def stage(source):
        for s in range(slots):
            staged[s * piece : (s + 1) * piece, : source.shape[-1]] = source[s].astype(F32)

    @pl.when(step == 0)
    def _():
        if padded > rows:
            staged[rows:, :] = jnp.zeros((padded - rows, width), F32)
        for r in range(groups):
            for s in range(slots):
                staged[s * piece : (s + 1) * piece, :head_width] = attended[r * slots + s][
                    ...
                ].astype(F32)
            heads_in[r] = staged[:, :head_width].astype(BF16)
        stage(cotangent)
        grad_out[...] = (staged[...] * valid[...]).astype(BF16)
        stage(tokens)
        total = staged[...] + bias_out[...]
        for r in range(groups):
            total = total + mm(heads_in[r], out_weight[r])
        residual[...] = total
        unit, _ = normalize(total)
        normed_here = (unit * gain[...] + shift[...]).astype(BF16)
        normed[...] = normed_here
        normed_t[...] = jnp.transpose(normed_here)
        output[...] = total + bias_down[...]
        grad_norm[...] = jnp.zeros_like(grad_norm)

    first = step < pl.num_programs(0) // 2
    up = jnp.where(first, up_own[...], up_other[...])
    down = jnp.where(first, down_own[...], down_other[...])
    hidden = mm(normed[...], up) + bias_up[...]
    share = 0.5 * (1.0 + lax.erf(hidden * np.float32(np.sqrt(0.5))))
    density = jnp.exp(-0.5 * hidden * hidden) * np.float32(1.0 / np.sqrt(2.0 * np.pi))
    activated = (hidden * share).astype(BF16)
    grad_hidden = (mm(grad_out[...], down, 1, 1) * (share + hidden * density)).astype(BF16)
    output[...] += mm(activated, down)
    grad_norm[...] += mm(grad_hidden, up, 1, 1)
    grad_up = mm(normed_t[...], grad_hidden).astype(BF16)
    grad_down = mm(activated, grad_out[...], 0, 0).astype(BF16)

    @pl.when(first)
    def _():
        grad_up_own[...] = grad_up
        grad_down_own[...] = grad_down

    @pl.when(jnp.logical_not(first))
    def _():
        grad_up_other[...] = grad_up
        grad_down_other[...] = grad_down

    grad_up_bias[...] = jnp.sum(grad_hidden.astype(F32), axis=0, keepdims=True)

    @pl.when(step == pl.num_programs(0) - 1)
    def _():
        staged[...] = output[...] * valid[...]
        for s in range(slots):
            layer_out[s] = staged[s * piece : (s + 1) * piece, :].astype(BF16)
        grad_low = grad_out[...].astype(F32)
        unit, factor = normalize(residual[...])
        back = grad_norm[...]
        scaled = back * gain[...]
        mean_scaled = jnp.mean(scaled, axis=-1, keepdims=True)
        mean_product = jnp.mean(scaled * unit, axis=-1, keepdims=True)
        total = grad_low + factor * (scaled - mean_scaled - unit * mean_product)
        staged[...] = total
        for s in range(slots):
            grad_residual[s] = staged[s * piece : (s + 1) * piece, :]
        branch = total.astype(BF16)
        vectors[0:1, :] = jnp.sum(back * unit, axis=0, keepdims=True)
        vectors[1:2, :] = jnp.sum(back, axis=0, keepdims=True)
        vectors[2:3, :] = jnp.sum(branch.astype(F32), axis=0, keepdims=True)
        vectors[3:4, :] = jnp.sum(grad_low, axis=0, keepdims=True)
        vectors[4:8, :] = jnp.zeros((4, width), F32)
        for r in range(groups):
            grad_out_weight[r] = mm(heads_in[r], branch, 0, 0).astype(BF16)
            staged[:, :head_width] = mm(branch, out_weight[r], 1, 1)
            grad_first[r][...] = staged[:piece, :head_width].astype(BF16)
            for s in range(1, slots):
                grad_rest[r][s - 1] = staged[s * piece : (s + 1) * piece, :head_width].astype(BF16)


def feed_forward(
    attended, tokens, cotangent, valid, out_weight, bias_out, gain, shift, bias_down, up_own,
    up_other, bias_up, down_own, down_other,
):
    slots, piece, width = tokens.shape
    groups, head_width = len(attended), attended[0][0].shape[-1]
    first = jax.ShapeDtypeStruct((piece, head_width), BF16)
    others = jax.ShapeDtypeStruct((slots - 1, piece, head_width), BF16)
    ff = 2 * up_own.shape[1]
    chunk = 384
    half = ff // 2 // chunk
    padded = round_up(slots * piece, 16)
    whole = lambda shape: pl.BlockSpec(
        shape, lambda i: (0,) * len(shape), pipeline_mode=pl.Buffered(1)
    )
    own = lambda i: jnp.minimum(i, half - 1)
    other = lambda i: jnp.maximum(i - half, 0)
    by_columns = [pl.BlockSpec((width, chunk), lambda i, at=at: (0, at(i))) for at in (own, other)]
    by_rows = [pl.BlockSpec((chunk, width), lambda i, at=at: (at(i), 0)) for at in (own, other)]
    bias_block = pl.BlockSpec((1, chunk), lambda i: (0, i))
    row = whole((1, width))
    return pl.pallas_call(
        partial(mlp_kernel, slots, groups),
        grid=(ff // chunk,),
        in_specs=[
            *[whole(first.shape)] * (groups * slots),
            whole(tokens.shape),
            whole(cotangent.shape),
            whole((padded, 1)),
            whole(out_weight.shape),
            row,
            row,
            row,
            row,
            *by_columns,
            bias_block,
            *by_rows,
        ],
        out_specs=[
            whole(tokens.shape),
            whole(tokens.shape),
            *[whole(first.shape)] * groups,
            *[whole(others.shape)] * groups,
            whole(out_weight.shape),
            whole((8, width)),
            *by_columns,
            bias_block,
            *by_rows,
        ],
        out_shape=[
            jax.ShapeDtypeStruct(tokens.shape, BF16),
            jax.ShapeDtypeStruct(tokens.shape, F32),
            *[first] * groups,
            *[others] * groups,
            jax.ShapeDtypeStruct(out_weight.shape, BF16),
            jax.ShapeDtypeStruct((8, width), F32),
            jax.ShapeDtypeStruct(up_own.shape, BF16),
            jax.ShapeDtypeStruct(up_own.shape, BF16),
            jax.ShapeDtypeStruct((1, ff), F32),
            jax.ShapeDtypeStruct(down_own.shape, BF16),
            jax.ShapeDtypeStruct(down_own.shape, BF16),
        ],
        scratch_shapes=[
            pltpu.VMEM((padded, width), F32),
            pltpu.VMEM((padded, width), F32),
            pltpu.VMEM((padded, width), F32),
            pltpu.VMEM((padded, width), F32),
            pltpu.VMEM((padded, width), BF16),
            pltpu.VMEM((width, padded), BF16),
            pltpu.VMEM((padded, width), BF16),
            pltpu.VMEM((groups, padded, head_width), BF16),
        ],
        compiler_params=pltpu.CompilerParams(
            vmem_limit_bytes=VMEM_BYTES, dimension_semantics=("arbitrary",)
        ),
        cost_estimate=cost(55),
        name="feed_forward",
    )(
        *[part for group in attended for part in group], tokens, cotangent, valid, out_weight, bias_out, gain, shift, bias_down, up_own,
        up_other, bias_up, down_own, down_other,
    )


def xor_send(block, axis, bits):
    n = lax.axis_size(axis)
    return lax.ppermute(block, axis, [(i, i ^ bits) for i in range(n)])


INNER = 2


def outer_send(block, shift):
    outer = lax.axis_size("img") // INNER
    return lax.ppermute(
        block,
        "img",
        [
            (z * INNER + y, ((z + shift) % outer) * INNER + y)
            for z in range(outer)
            for y in range(INNER)
        ],
    )


def few_devices():
    return lax.axis_size("img") <= 16


def place_outer(block, arrived):
    outer = lax.axis_size("img") // INNER
    z = lax.axis_index("img") // INNER
    placed = jnp.zeros((outer,) + block.shape, block.dtype)
    for k, part in enumerate([block] + arrived):
        placed = lax.dynamic_update_slice_in_dim(placed, part[None], (z + outer - k) % outer, 0)
    return placed


def gather_inner(placed, after=()):
    other = once_there(xor_send(placed, "img", 1), after)
    first = (lax.axis_index("img") & 1) == 0
    both = jnp.stack([jnp.where(first, placed, other), jnp.where(first, other, placed)], axis=1)
    return both.reshape((-1,) + placed.shape[1:])


def start_gather(block):
    if not few_devices():
        return lax.all_gather(block, "img", axis=0), None
    outer = lax.axis_size("img") // INNER
    return block, [outer_send(block, k) for k in range(1, outer)]


def end_gather(block, arrived, after=()):
    if arrived is None:
        return block
    return gather_inner(place_outer(block, arrived), after)


def reduce_inner(parts):
    outer = lax.axis_size("img") // INNER
    split = parts.reshape((outer, INNER) + parts.shape[1:])
    me = lax.axis_index("img") % INNER
    send = lax.dynamic_index_in_dim(split, 1 - me, 1, keepdims=False)
    keep = lax.dynamic_index_in_dim(split, me, 1, keepdims=False)
    return keep.astype(F32) + xor_send(send, "img", 1).astype(F32)


def reduce_outer(sums):
    outer = sums.shape[0]
    z = lax.axis_index("img") // INNER
    total = lax.dynamic_index_in_dim(sums, z, 0, keepdims=False)
    for k in range(1, outer):
        send = lax.dynamic_index_in_dim(sums, (z + k) % outer, 0, keepdims=False)
        total = total + outer_send(send.astype(BF16), k).astype(F32)
    return total


def scatter_img(parts):
    return lax.psum_scatter(parts, "img", scatter_dimension=0, tiled=False).astype(F32)


def in_pair_order(own, other, axis):
    first = (lax.axis_index("seq") & 1) == 0
    return jnp.where(
        first, jnp.concatenate([own, other], axis), jnp.concatenate([other, own], axis)
    )


def half_of(block, axis, which):
    size = block.shape[axis] // 2
    return lax.dynamic_slice_in_dim(block, which * size, size, axis)


def over_pieces(total):
    low = total.astype(BF16)
    low = (low.astype(F32) + xor_send(low, "seq", 2).astype(F32)).astype(BF16)
    return low, xor_send(low, "seq", 1)


def local(
    tokens,
    cotangent,
    images_held,
    piece_rows,
    norm_gain,
    norm_shift,
    qkv_weight,
    qkv_bias,
    out_weight,
    out_bias,
    mlp_gain,
    mlp_shift,
    up_weight,
    up_bias,
    down_weight,
    down_bias,
):
    slot_count, piece_size, model_width = tokens.shape
    n_seq = lax.axis_size("seq")
    n_img = lax.axis_size("img")
    me = lax.axis_index("seq")
    pair_me = me & 1
    own_img = lax.axis_index("img")
    row_count = slot_count * piece_size
    heads_here = HEADS // n_seq
    group = 3 * D // n_seq
    group_width = heads_here * HEAD_DIM
    shard = D // n_img
    ff = up_weight.shape[1]
    ff_half = ff // n_img // 2
    blocks = 3 * heads_here

    rows_of = piece_rows[me ^ jnp.arange(n_seq)]
    key_valid = (jnp.arange(piece_size)[None, :] < rows_of[:, None]).reshape(n_seq * piece_size)
    live_slots = jnp.arange(slot_count) < images_held[0]
    valid_rows = (live_slots[:, None] & key_valid[None, :piece_size]).reshape(row_count)
    valid_rows = jnp.pad(valid_rows, (0, round_up(row_count, 16) - row_count))
    valid_rows = valid_rows.astype(F32)[:, None]
    key_mask = jnp.where(
        key_valid[:, None] | (jnp.arange(LANES) != HEAD_DIM)[None, :], 0.0, NEG
    ).astype(F32)

    small = [norm_gain, norm_shift, out_bias, mlp_gain, mlp_shift, down_bias, qkv_bias, up_bias]
    small = [jnp.pad(v[None], ((0, 0), (0, group - v.shape[0]))) for v in small]
    small.append(jnp.zeros((8, group), BF16))
    my_columns = lax.dynamic_slice_in_dim(qkv_weight, me * group, group, 1)
    first_part, first_arrived = start_gather(jnp.concatenate([my_columns] + small, axis=0))

    pair = xor_send(tokens, "seq", 1)
    across = [xor_send(tokens[0], "seq", 2), xor_send(tokens[1:], "seq", 2)]
    diagonal = [xor_send(part, "seq", 1) for part in across]
    slot_tokens = [[(tokens, 0), (pair, 0), (across[0],), (diagonal[0],)]]
    for slot in range(1, slot_count):
        slot_tokens.append(
            [(tokens, slot), (pair, slot), (across[1], slot - 1), (diagonal[1], slot - 1)]
        )

    my_up = lax.dynamic_index_in_dim(
        up_weight.reshape(shard, n_img, 2, ff_half), pair_me, 2, keepdims=False
    ).reshape(shard, -1)
    my_down = once_there(half_of(down_weight, 0, pair_me), tuple(first_arrived or ()))
    down_own = lax.all_gather(my_down, "img", axis=0).reshape(-1, model_width)

    first_set = end_gather(first_part, first_arrived)
    my_second = jnp.concatenate([my_up, half_of(out_weight, 1, pair_me)], axis=1)
    second_part, second_arrived = start_gather(once_there(my_second, (first_set,)))
    qkv_cols = first_set[:, :shard].reshape(model_width, group)
    params = first_set[:, shard:].astype(F32)

    def param(row, width):
        return params[:, row, : width * shard].reshape(-1)

    gain_first, shift_first, bias_out = param(0, 1)[None], param(1, 1)[None], param(2, 1)[None]
    gain_second, shift_second, bias_down = param(3, 1)[None], param(4, 1)[None], param(5, 1)[None]
    pair_bias, bias_up = param(6, 2), param(7, 4).reshape(n_img, 2, ff_half)
    bias_up = jnp.concatenate(
        [
            lax.dynamic_index_in_dim(bias_up, which, 1, keepdims=False).reshape(1, -1)
            for which in (pair_me, 1 - pair_me)
        ],
        axis=1,
    )

    paired = lax.dynamic_slice_in_dim(
        pair_bias.reshape(HEADS, 2, HEAD_DIM), me * heads_here, heads_here, 0
    )
    head_bias = jnp.concatenate(
        [paired[:, :1], jnp.zeros((heads_here, 1, HEAD_DIM), F32), paired[:, 1:]], axis=1
    ).reshape(1, group)

    slot_normed, slot_qkv, slot_attended = [], [], []
    for slot in range(slot_count):
        after = ()
        if slot > 0:
            after = (slot_attended[-1][0],)
        if slot > 1:
            after = after + tuple(slot_attended[-2][1:])
        normed, qkv_rows, *attended = slot_forward(
            slot_tokens[slot], gain_first, shift_first, qkv_cols, head_bias, key_mask, after
        )
        slot_normed.append(normed)
        slot_qkv.append(qkv_rows)
        slot_attended.append(
            [attended[0]] + [xor_send(attended[r], "seq", r) for r in range(1, n_seq)]
        )
    down_own = once_there(down_own, (slot_attended[-1][0],))
    if second_arrived is not None:
        second_arrived = [once_there(part, (slot_attended[1][0],)) for part in second_arrived]
    sent = tuple(part for parts in slot_attended for part in parts[1:])
    second_set = end_gather(second_part, second_arrived, sent).reshape(model_width, -1)
    up_own, out_own = second_set[:, : ff // 2], second_set[:, ff // 2 :]
    up_other = xor_send(up_own, "seq", 1)
    down_other = xor_send(down_own, "seq", 1)
    out_full = in_pair_order(out_own, xor_send(out_own, "seq", 1), 1)
    out_full = out_full.reshape(n_seq, group_width, model_width)
    out_groups = jnp.stack(
        [lax.dynamic_index_in_dim(out_full, me ^ r, 0, keepdims=False) for r in range(n_seq)]
    )
    attended_groups = [[parts[r] for parts in slot_attended] for r in range(n_seq)]

    layer_out, grad_residual, *rest = feed_forward(
        attended_groups,
        tokens,
        cotangent,
        valid_rows,
        out_groups,
        bias_out,
        gain_second,
        shift_second,
        bias_down,
        up_own,
        up_other,
        bias_up,
        down_own,
        down_other,
    )
    grad_first, grad_rest, rest = rest[:n_seq], rest[n_seq : 2 * n_seq], rest[2 * n_seq :]
    grad_out_groups, vectors, grad_up_own, grad_up_other = rest[:4]
    grad_up_bias, grad_down_own, grad_down_other = rest[4:]
    for r in range(1, n_seq):
        grad_first[r] = xor_send(grad_first[r], "seq", r)
        grad_rest[r] = xor_send(grad_rest[r], "seq", r)
    slot_grads = [[(part,) for part in grad_first]]
    for slot in range(1, slot_count):
        slot_grads.append([(part, slot - 1) for part in grad_rest])

    down_sum = grad_down_own.astype(F32) + xor_send(grad_down_other, "seq", 1).astype(F32)
    up_sum = grad_up_own.astype(F32) + xor_send(grad_up_other, "seq", 1).astype(F32)
    grad_out_weight = jnp.concatenate(
        [lax.dynamic_index_in_dim(grad_out_groups, me ^ r, 0, keepdims=False) for r in range(n_seq)],
        axis=0,
    )
    out_sum = half_of(grad_out_weight, 1, pair_me).astype(F32) + xor_send(
        half_of(grad_out_weight, 1, 1 - pair_me), "seq", 1
    ).astype(F32)
    second_grads = jnp.concatenate(
        [up_sum.astype(BF16), out_sum.astype(BF16), down_sum.astype(BF16).reshape(model_width, -1)],
        axis=1,
    ).reshape(n_img, shard, -1)
    own_second = scatter_img(second_grads)

    grad_columns = jnp.zeros((model_width, group), F32)
    bias_sums = jnp.zeros((group,), F32)
    norm_sums = jnp.zeros((8, model_width), F32)
    own_sums, arrivals = [], []
    for slot in range(slot_count):
        after = (second_grads,) if slot == 0 else ()
        if slot > 1:
            after = (arrivals[-2][0],)
        own, across, pairs, grad_columns, slot_norm, slot_bias = slot_backward(
            slot_grads[slot],
            slot_tokens[slot],
            slot_qkv[slot],
            slot_normed[slot],
            qkv_cols,
            grad_columns,
            after,
        )
        norm_sums += slot_norm
        bias_sums += slot_bias[0]
        pairs = xor_send(pairs, "seq", 1)
        across = xor_send((across + pairs[1].astype(F32)).astype(BF16), "seq", 2)
        own_sums.append(own + pairs[0].astype(F32) + across.astype(F32))
        arrivals.append((pairs, across))
    bias_sums = bias_sums.reshape(heads_here, 3, HEAD_DIM)
    grad_pairs = jnp.concatenate([bias_sums[:, :1], bias_sums[:, 2:]], axis=1).reshape(-1)
    grad_pairs = lax.dynamic_update_slice_in_dim(
        jnp.zeros((2 * D,), F32), grad_pairs, me * grad_pairs.shape[0], 0
    )
    up_halves = grad_up_bias.reshape(2, n_img, 1, ff_half)
    grad_up_bias = in_pair_order(up_halves[0], up_halves[1], 1).reshape(-1)
    all_vectors = [
        norm_sums[0],
        norm_sums[1],
        grad_pairs,
        vectors[2],
        vectors[0],
        vectors[1],
        grad_up_bias,
        vectors[3],
    ]
    extra = jnp.concatenate([v.reshape(n_img, -1) for v in all_vectors], axis=1)
    extra_rows = -(-extra.shape[1] // group)
    extra = jnp.pad(extra, ((0, 0), (0, extra_rows * group - extra.shape[1])))
    extra = jnp.pad(
        extra.reshape(n_img, extra_rows, group), ((0, 0), (0, 16 - extra_rows), (0, 0))
    )
    columns = jnp.concatenate([grad_columns.reshape(n_img, shard, group), extra], axis=1)
    columns = once_there(columns.astype(BF16), (arrivals[-2][0],))
    if few_devices():
        own_columns = reduce_outer(once_there(reduce_inner(columns), (pairs,)))
    else:
        own_columns = scatter_img(columns)
    own_columns = own_columns.astype(BF16)

    grad_norm_first = jnp.concatenate(own_sums, axis=0)
    unit, factor = normalize(tokens.reshape(row_count, model_width).astype(F32))
    scaled = grad_norm_first * gain_first
    mean_scaled = jnp.mean(scaled, axis=-1, keepdims=True)
    mean_product = jnp.mean(scaled * unit, axis=-1, keepdims=True)
    grad_inputs = factor * (scaled - mean_scaled - unit * mean_product)
    tokens_grad = grad_residual + grad_inputs.reshape(grad_residual.shape)

    by_sender = jnp.stack(
        [own_columns] + [xor_send(own_columns, "seq", r) for r in range(1, n_seq)]
    )
    by_sender = [
        lax.dynamic_index_in_dim(by_sender, me ^ g, 0, keepdims=False) for g in range(n_seq)
    ]
    share_qkv = jnp.concatenate([part[:shard] for part in by_sender], axis=1).astype(F32)
    mine = sum(part[shard : shard + extra_rows].astype(F32) for part in by_sender).reshape(-1)
    second_low, second_other = over_pieces(own_second)
    cuts = (ff // 2, ff // 2 + model_width // 2)
    up_low, out_low, down_low = jnp.split(second_low, cuts, axis=1)
    up_there, out_there, down_there = jnp.split(second_other, cuts, axis=1)
    up_low = up_low.reshape(shard, n_img, 1, ff_half)
    up_there = up_there.reshape(shard, n_img, 1, ff_half)
    share_up = in_pair_order(up_low, up_there, 2).reshape(shard, ff).astype(F32)
    share_out = in_pair_order(out_low, out_there, 1).astype(F32)
    down_low = down_low.reshape(ff_half, model_width)
    down_there = down_there.reshape(ff_half, model_width)
    share_down = in_pair_order(down_low, down_there, 0).astype(F32)

    shares, at = [], 0
    for v in all_vectors:
        size = v.shape[0] // n_img
        shares.append(mine[at : at + size])
        at += size
    return (
        layer_out,
        tokens_grad,
        shares[0],
        shares[1],
        share_qkv,
        shares[2],
        share_out,
        shares[3],
        shares[4],
        shares[5],
        share_up,
        shares[6],
        share_down,
        shares[7],
    )


def solution(mesh):
    placed = (
        P("img", "seq", None),
        P("img", "seq", None),
        P("img"),
        P(),
        P("img"),
        P("img"),
        P("img", None),
        P("img"),
        P("img", None),
        P("img"),
        P("img"),
        P("img"),
        P("img", None),
        P("img"),
        P("img", None),
        P("img"),
    )
    return jax.shard_map(
        local,
        mesh=mesh,
        in_specs=placed,
        out_specs=(
            P("img", "seq", None),
            P("img", "seq", None),
            P("img"),
            P("img"),
            P("img", None),
            P("img"),
            P("img", None),
            P("img"),
            P("img"),
            P("img"),
            P("img", None),
            P("img"),
            P("img", None),
            P("img"),
        ),
        check_vma=False,
    )
```

```python
from functools import partial

import jax
import jax.numpy as jnp
import numpy as np
from jax import lax
from jax.experimental import pallas as pl
from jax.experimental.pallas import tpu as pltpu
from jax.sharding import PartitionSpec as P

D = 768
HEADS = 12
HEAD_DIM = 64
EPS = 1e-06
NEG = -1e30
LANES = 128
F32 = jnp.float32
BF16 = jnp.bfloat16
VMEM_BYTES = 60 * 1024 * 1024
def cost(giga_flops):
    return pl.CostEstimate(
        flops=giga_flops * 10**9, bytes_accessed=10**7, transcendentals=10**6
    )


def mm(left, right, left_dim=1, right_dim=0):
    return lax.dot_general(
        left, right, (((left_dim,), (right_dim,)), ((), ())), preferred_element_type=F32
    )


def normalize(features):
    row_mean = jnp.mean(features, axis=-1, keepdims=True)
    centred = features - row_mean
    spread = jnp.mean(centred * centred, axis=-1, keepdims=True)
    factor = lax.rsqrt(spread + EPS)
    return centred * factor, factor


def round_up(size, unit):
    return -(-size // unit) * unit


def head_columns(heads, parts):
    place = np.zeros((heads * parts, LANES, heads * parts * HEAD_DIM), np.float32)
    for b in range(heads * parts):
        for d in range(HEAD_DIM):
            place[b, d, b * HEAD_DIM + d] = 1.0
    return jnp.asarray(place, BF16)


def lane_columns(heads):
    pick = np.zeros((3 * heads, LANES, LANES), np.float32)
    ones = np.zeros((3 * heads, 1, LANES), np.float32)
    for b in range(3 * heads):
        start = b * HEAD_DIM % LANES
        for d in range(HEAD_DIM):
            pick[b, start + d, d] = HEAD_DIM**-0.5 if b % 3 == 0 else 1.0
        if b % 3 != 1:
            ones[b, 0, HEAD_DIM] = 1.0
    return jnp.asarray(pick, BF16), jnp.asarray(ones, F32)


def query_block(rows):
    for size in range(min(rows, 400) // 16 * 16, 15, -16):
        if rows % size == 0:
            return size
    return rows


def after_specs(after):
    return [pl.BlockSpec(memory_space=pl.ANY)] * len(after)


def piece_spec(array, *at):
    rest = array.shape[len(at) :]
    return pl.BlockSpec((None,) * len(at) + rest, lambda i: at + (0,) * len(rest))


def piece_specs(pieces):
    return [piece_spec(*piece) for piece in pieces]


def whole_specs(count):
    return [pl.BlockSpec(memory_space=pltpu.VMEM)] * count


def forward_kernel(n_seq, heads, n_after, *refs):
    tokens, refs = refs[:n_seq], refs[n_seq + n_after :]
    gain, shift, weight, bias, key_mask, pick, ones, place = refs[:8]
    normed_out, qkv_out = refs[8:10]
    attended_out, (rows, attended) = refs[10 : 10 + n_seq], refs[10 + n_seq :]
    piece = tokens[0].shape[0]
    total = n_seq * piece
    for r in range(n_seq):
        unit, _ = normalize(tokens[r][...].astype(F32))
        rows[r * piece : (r + 1) * piece, :] = unit * gain[...] + shift[...]
    normed = rows[...].astype(BF16)
    normed_out[...] = normed
    qkv = (mm(normed, weight[...]) + bias[...]).astype(BF16)
    width = qkv.shape[1]
    block = query_block(total)
    pad = qkv_out.shape[1] - total
    parts = []
    for b in range(3 * heads):
        start = b * HEAD_DIM // LANES * LANES
        size = min(LANES, width - start)
        part = mm(qkv[:, start : start + size], pick[b, :size]) + ones[b]
        if b % 3 == 1:
            part = part + key_mask[...]
        part = part.astype(BF16)
        qkv_out[b, :total] = part
        if pad:
            qkv_out[b, total:] = jnp.zeros((pad, LANES), BF16)
        parts.append(part)

    tasks = [(at, h) for at in range(0, total, block) for h in range(heads)]

    def score(task):
        at, h = task
        return mm(parts[3 * h][at : at + block], parts[3 * h + 1], 1, 1)

    scores = score(tasks[0])
    placed = None
    for index, (at, h) in enumerate(tasks):
        following = score(tasks[index + 1]) if index + 1 < len(tasks) else None
        peak = jnp.max(scores, axis=-1, keepdims=True)
        terms = jnp.exp(scores - peak).astype(BF16)
        weighted = mm(terms, parts[3 * h + 2])
        result = (weighted / weighted[:, HEAD_DIM : HEAD_DIM + 1]).astype(BF16)
        here = mm(result, place[h])
        placed = here if h == 0 else placed + here
        if h == heads - 1:
            attended[at : at + block, :] = placed
        scores = following
    for r in range(n_seq):
        attended_out[r][...] = attended[r * piece : (r + 1) * piece, :].astype(BF16)


def slot_forward(pieces, gain, shift, weight, bias, key_mask, after=()):
    n_seq = len(pieces)
    piece, width = pieces[0][0].shape[-2:]
    heads = weight.shape[1] // (3 * HEAD_DIM)
    total = n_seq * piece
    padded = round_up(total, LANES)
    return pl.pallas_call(
        partial(forward_kernel, n_seq, heads, len(after)),
        grid=(1,),
        in_specs=piece_specs(pieces) + after_specs(after) + whole_specs(8),
        out_shape=(
            jax.ShapeDtypeStruct((total, width), BF16),
            jax.ShapeDtypeStruct((3 * heads, padded, LANES), BF16),
            *[jax.ShapeDtypeStruct((piece, heads * HEAD_DIM), BF16)] * n_seq,
        ),
        scratch_shapes=[
            pltpu.VMEM((total, width), F32),
            pltpu.VMEM((total, heads * HEAD_DIM), F32),
        ],
        compiler_params=pltpu.CompilerParams(vmem_limit_bytes=VMEM_BYTES),
        cost_estimate=cost(14),
        name="slot_forward",
    )(
        *[p[0] for p in pieces], *after, gain, shift, weight, bias, key_mask, *lane_columns(heads),
        head_columns(heads, 1),
    )


def backward_kernel(n_seq, heads, n_after, *refs):
    grads, refs = refs[:n_seq], refs[n_seq + n_after :]
    tokens, refs = refs[:n_seq], refs[n_seq:]
    qkv, normed, weight, before, place, spread = refs[:6]
    own, across, pairs, grad_weight, vectors, grad_bias, rows, wide = refs[6:]
    piece = grads[0].shape[0]
    total = n_seq * piece
    padded = qkv.shape[1]
    for r in range(n_seq):
        rows[r * piece : (r + 1) * piece, :] = grads[r][...].astype(F32)
    if padded > total:
        rows[total:, :] = jnp.zeros((padded - total, rows.shape[1]), F32)
    grad_rows = rows[...].astype(BF16)
    grad_heads = [mm(grad_rows, place[h], 1, 1).astype(BF16) for h in range(heads)]
    block = 4 * LANES
    tasks = [(h, at) for h in range(heads) for at in range(0, padded, block)]

    def products(task):
        h, at = task
        end = min(at + block, padded)
        scores = mm(qkv[3 * h + 1, :total], qkv[3 * h, at:end], 1, 1)
        return scores, mm(qkv[3 * h + 2, :total], grad_heads[h][at:end], 1, 1)

    current = products(tasks[0])
    grad_qkv = None
    for index, (h, at) in enumerate(tasks):
        following = products(tasks[index + 1]) if index + 1 < len(tasks) else None
        if at == 0:
            keys_t = jnp.transpose(qkv[3 * h + 1])[:, :total]
            grad_keys = jnp.zeros((total, LANES), F32)
            grad_values = jnp.zeros((total, LANES), F32)
            grad_queries = []
        end = min(at + block, padded)
        scores, grad_probs = current
        peak = jnp.max(scores, axis=0, keepdims=True)
        terms = jnp.exp(scores - peak)
        probs = terms * (1.0 / jnp.sum(terms, axis=0, keepdims=True))
        inner = jnp.sum(probs * grad_probs, axis=0, keepdims=True)
        grad_scores = (probs * (grad_probs - inner)).astype(BF16)
        grad_values = grad_values + mm(probs.astype(BF16), grad_heads[h][at:end])
        grad_keys = grad_keys + mm(grad_scores, qkv[3 * h, at:end])
        grad_queries.append(jnp.transpose(mm(keys_t, grad_scores)))
        if end == padded:
            queries = jnp.concatenate(grad_queries, axis=0)[:total] * (HEAD_DIM**-0.5)
            for t, part in enumerate((queries, grad_keys, grad_values)):
                placed = mm(part.astype(BF16), spread[3 * h + t])
                grad_qkv = placed if grad_qkv is None else grad_qkv + placed
        current = following
    grad_low = grad_qkv.astype(BF16)
    grad_bias[...] = jnp.broadcast_to(
        jnp.sum(grad_low.astype(F32), axis=0, keepdims=True), grad_bias.shape
    )
    grad_weight[...] = before[...] + mm(normed[...], grad_low, 0, 0)
    wide[...] = mm(grad_low, weight[...], 1, 1)
    by_unit = jnp.zeros((1, wide.shape[1]), F32)
    by_one = jnp.zeros((1, wide.shape[1]), F32)
    for r in range(n_seq):
        share = wide[r * piece : (r + 1) * piece, :]
        unit, _ = normalize(tokens[r][...].astype(F32))
        by_unit = by_unit + jnp.sum(share * unit, axis=0, keepdims=True)
        by_one = by_one + jnp.sum(share, axis=0, keepdims=True)
        if r & 1:
            pairs[r // 2] = share.astype(BF16)
        else:
            (own if r == 0 else across)[...] = share
    vectors[...] = jnp.zeros(vectors.shape, F32)
    vectors[0:1, :] = by_unit
    vectors[1:2, :] = by_one


def slot_backward(grads, tokens, qkv, normed, weight, before, after=()):
    n_seq = len(grads)
    piece, width = grads[0][0].shape[-2:]
    heads = qkv.shape[0] // 3
    total = n_seq * piece
    model = normed.shape[1]
    return pl.pallas_call(
        partial(backward_kernel, n_seq, heads, len(after)),
        grid=(1,),
        in_specs=piece_specs(grads) + after_specs(after) + piece_specs(tokens) + whole_specs(6),
        out_shape=(
            jax.ShapeDtypeStruct((piece, model), F32),
            jax.ShapeDtypeStruct((piece, model), F32),
            jax.ShapeDtypeStruct((n_seq // 2, piece, model), BF16),
            jax.ShapeDtypeStruct((model, 3 * width), F32),
            jax.ShapeDtypeStruct((8, model), F32),
            jax.ShapeDtypeStruct((8, 3 * width), F32),
        ),
        scratch_shapes=[
            pltpu.VMEM((qkv.shape[1], width), F32),
            pltpu.VMEM((total, model), F32),
        ],
        compiler_params=pltpu.CompilerParams(vmem_limit_bytes=VMEM_BYTES),
        cost_estimate=cost(0),
        name="slot_backward",
    )(
        *[g[0] for g in grads], *after, *[t[0] for t in tokens], qkv, normed, weight, before,
        head_columns(heads, 1), head_columns(heads, 3),
    )


def gate_kernel(*refs):
    pass


def once_there(array, after):
    if not after:
        return array
    return pl.pallas_call(
        gate_kernel,
        in_specs=after_specs((array,) + tuple(after)),
        out_specs=pl.BlockSpec(memory_space=pl.ANY),
        out_shape=jax.ShapeDtypeStruct(array.shape, array.dtype),
        input_output_aliases={0: 0},
        name="once_there",
    )(array, *after)


def mlp_kernel(slots, groups, *refs):
    attended, refs = refs[: slots * groups], refs[slots * groups :]
    (
        tokens, cotangent, valid, out_weight, bias_out, gain, shift, bias_down, up_own, up_other,
        bias_up, down_own, down_other, layer_out, grad_residual,
    ) = refs[:15]
    grad_first, refs = refs[15 : 15 + groups], refs[15 + groups :]
    grad_rest, refs = refs[:groups], refs[groups:]
    (
        grad_out_weight, vectors, grad_up_own, grad_up_other, grad_up_bias, grad_down_own,
        grad_down_other, staged, residual, output, grad_norm, normed, normed_t, grad_out, heads_in,
    ) = refs
    step = pl.program_id(0)
    piece, width = tokens.shape[1:]
    head_width = attended[0].shape[-1]
    rows = slots * piece
    padded = residual.shape[0]

    def stage(source):
        for s in range(slots):
            staged[s * piece : (s + 1) * piece, : source.shape[-1]] = source[s].astype(F32)

    @pl.when(step == 0)
    def _():
        if padded > rows:
            staged[rows:, :] = jnp.zeros((padded - rows, width), F32)
        for r in range(groups):
            for s in range(slots):
                staged[s * piece : (s + 1) * piece, :head_width] = attended[r * slots + s][
                    ...
                ].astype(F32)
            heads_in[r] = staged[:, :head_width].astype(BF16)
        stage(cotangent)
        grad_out[...] = (staged[...] * valid[...]).astype(BF16)
        stage(tokens)
        total = staged[...] + bias_out[...]
        for r in range(groups):
            total = total + mm(heads_in[r], out_weight[r])
        residual[...] = total
        unit, _ = normalize(total)
        normed_here = (unit * gain[...] + shift[...]).astype(BF16)
        normed[...] = normed_here
        normed_t[...] = jnp.transpose(normed_here)
        output[...] = total + bias_down[...]
        grad_norm[...] = jnp.zeros_like(grad_norm)

    first = step < pl.num_programs(0) // 2
    up = jnp.where(first, up_own[...], up_other[...])
    down = jnp.where(first, down_own[...], down_other[...])
    hidden = mm(normed[...], up) + bias_up[...]
    share = 0.5 * (1.0 + lax.erf(hidden * np.float32(np.sqrt(0.5))))
    density = jnp.exp(-0.5 * hidden * hidden) * np.float32(1.0 / np.sqrt(2.0 * np.pi))
    activated = (hidden * share).astype(BF16)
    grad_hidden = (mm(grad_out[...], down, 1, 1) * (share + hidden * density)).astype(BF16)
    output[...] += mm(activated, down)
    grad_norm[...] += mm(grad_hidden, up, 1, 1)
    grad_up = mm(normed_t[...], grad_hidden).astype(BF16)
    grad_down = mm(activated, grad_out[...], 0, 0).astype(BF16)

    @pl.when(first)
    def _():
        grad_up_own[...] = grad_up
        grad_down_own[...] = grad_down

    @pl.when(jnp.logical_not(first))
    def _():
        grad_up_other[...] = grad_up
        grad_down_other[...] = grad_down

    grad_up_bias[...] = jnp.sum(grad_hidden.astype(F32), axis=0, keepdims=True)

    @pl.when(step == pl.num_programs(0) - 1)
    def _():
        staged[...] = output[...] * valid[...]
        for s in range(slots):
            layer_out[s] = staged[s * piece : (s + 1) * piece, :].astype(BF16)
        grad_low = grad_out[...].astype(F32)
        unit, factor = normalize(residual[...])
        back = grad_norm[...]
        scaled = back * gain[...]
        mean_scaled = jnp.mean(scaled, axis=-1, keepdims=True)
        mean_product = jnp.mean(scaled * unit, axis=-1, keepdims=True)
        total = grad_low + factor * (scaled - mean_scaled - unit * mean_product)
        staged[...] = total
        for s in range(slots):
            grad_residual[s] = staged[s * piece : (s + 1) * piece, :]
        branch = total.astype(BF16)
        vectors[0:1, :] = jnp.sum(back * unit, axis=0, keepdims=True)
        vectors[1:2, :] = jnp.sum(back, axis=0, keepdims=True)
        vectors[2:3, :] = jnp.sum(branch.astype(F32), axis=0, keepdims=True)
        vectors[3:4, :] = jnp.sum(grad_low, axis=0, keepdims=True)
        vectors[4:8, :] = jnp.zeros((4, width), F32)
        for r in range(groups):
            grad_out_weight[r] = mm(heads_in[r], branch, 0, 0).astype(BF16)
            staged[:, :head_width] = mm(branch, out_weight[r], 1, 1)
            grad_first[r][...] = staged[:piece, :head_width].astype(BF16)
            for s in range(1, slots):
                grad_rest[r][s - 1] = staged[s * piece : (s + 1) * piece, :head_width].astype(BF16)


def feed_forward(
    attended, tokens, cotangent, valid, out_weight, bias_out, gain, shift, bias_down, up_own,
    up_other, bias_up, down_own, down_other,
):
    slots, piece, width = tokens.shape
    groups, head_width = len(attended), attended[0][0].shape[-1]
    first = jax.ShapeDtypeStruct((piece, head_width), BF16)
    others = jax.ShapeDtypeStruct((slots - 1, piece, head_width), BF16)
    ff = 2 * up_own.shape[1]
    chunk = 384
    half = ff // 2 // chunk
    padded = round_up(slots * piece, 16)
    whole = lambda shape: pl.BlockSpec(
        shape, lambda i: (0,) * len(shape), pipeline_mode=pl.Buffered(1)
    )
    own = lambda i: jnp.minimum(i, half - 1)
    other = lambda i: jnp.maximum(i - half, 0)
    by_columns = [pl.BlockSpec((width, chunk), lambda i, at=at: (0, at(i))) for at in (own, other)]
    by_rows = [pl.BlockSpec((chunk, width), lambda i, at=at: (at(i), 0)) for at in (own, other)]
    bias_block = pl.BlockSpec((1, chunk), lambda i: (0, i))
    row = whole((1, width))
    return pl.pallas_call(
        partial(mlp_kernel, slots, groups),
        grid=(ff // chunk,),
        in_specs=[
            *[whole(first.shape)] * (groups * slots),
            whole(tokens.shape),
            whole(cotangent.shape),
            whole((padded, 1)),
            whole(out_weight.shape),
            row,
            row,
            row,
            row,
            *by_columns,
            bias_block,
            *by_rows,
        ],
        out_specs=[
            whole(tokens.shape),
            whole(tokens.shape),
            *[whole(first.shape)] * groups,
            *[whole(others.shape)] * groups,
            whole(out_weight.shape),
            whole((8, width)),
            *by_columns,
            bias_block,
            *by_rows,
        ],
        out_shape=[
            jax.ShapeDtypeStruct(tokens.shape, BF16),
            jax.ShapeDtypeStruct(tokens.shape, F32),
            *[first] * groups,
            *[others] * groups,
            jax.ShapeDtypeStruct(out_weight.shape, BF16),
            jax.ShapeDtypeStruct((8, width), F32),
            jax.ShapeDtypeStruct(up_own.shape, BF16),
            jax.ShapeDtypeStruct(up_own.shape, BF16),
            jax.ShapeDtypeStruct((1, ff), F32),
            jax.ShapeDtypeStruct(down_own.shape, BF16),
            jax.ShapeDtypeStruct(down_own.shape, BF16),
        ],
        scratch_shapes=[
            pltpu.VMEM((padded, width), F32),
            pltpu.VMEM((padded, width), F32),
            pltpu.VMEM((padded, width), F32),
            pltpu.VMEM((padded, width), F32),
            pltpu.VMEM((padded, width), BF16),
            pltpu.VMEM((width, padded), BF16),
            pltpu.VMEM((padded, width), BF16),
            pltpu.VMEM((groups, padded, head_width), BF16),
        ],
        compiler_params=pltpu.CompilerParams(
            vmem_limit_bytes=VMEM_BYTES, dimension_semantics=("arbitrary",)
        ),
        cost_estimate=cost(55),
        name="feed_forward",
    )(
        *[part for group in attended for part in group], tokens, cotangent, valid, out_weight, bias_out, gain, shift, bias_down, up_own,
        up_other, bias_up, down_own, down_other,
    )


def xor_send(block, axis, bits):
    n = lax.axis_size(axis)
    return lax.ppermute(block, axis, [(i, i ^ bits) for i in range(n)])


INNER = 2


def outer_send(block, shift):
    outer = lax.axis_size("img") // INNER
    return lax.ppermute(
        block,
        "img",
        [
            (z * INNER + y, ((z + shift) % outer) * INNER + y)
            for z in range(outer)
            for y in range(INNER)
        ],
    )


def few_devices():
    return lax.axis_size("img") <= 16


def place_outer(block, arrived):
    outer = lax.axis_size("img") // INNER
    z = lax.axis_index("img") // INNER
    placed = jnp.zeros((outer,) + block.shape, block.dtype)
    for k, part in enumerate([block] + arrived):
        placed = lax.dynamic_update_slice_in_dim(placed, part[None], (z + outer - k) % outer, 0)
    return placed


def gather_inner(placed, after=()):
    other = once_there(xor_send(placed, "img", 1), after)
    first = (lax.axis_index("img") & 1) == 0
    both = jnp.stack([jnp.where(first, placed, other), jnp.where(first, other, placed)], axis=1)
    return both.reshape((-1,) + placed.shape[1:])


def start_gather(block):
    if not few_devices():
        return lax.all_gather(block, "img", axis=0), None
    outer = lax.axis_size("img") // INNER
    return block, [outer_send(block, k) for k in range(1, outer)]


def end_gather(block, arrived, after=()):
    if arrived is None:
        return block
    return gather_inner(place_outer(block, arrived), after)


def reduce_inner(parts):
    outer = lax.axis_size("img") // INNER
    split = parts.reshape((outer, INNER) + parts.shape[1:])
    me = lax.axis_index("img") % INNER
    send = lax.dynamic_index_in_dim(split, 1 - me, 1, keepdims=False)
    keep = lax.dynamic_index_in_dim(split, me, 1, keepdims=False)
    return keep.astype(F32) + xor_send(send, "img", 1).astype(F32)


def reduce_outer(sums):
    outer = sums.shape[0]
    z = lax.axis_index("img") // INNER
    total = lax.dynamic_index_in_dim(sums, z, 0, keepdims=False)
    for k in range(1, outer):
        send = lax.dynamic_index_in_dim(sums, (z + k) % outer, 0, keepdims=False)
        total = total + outer_send(send.astype(BF16), k).astype(F32)
    return total


def scatter_img(parts):
    return lax.psum_scatter(parts, "img", scatter_dimension=0, tiled=False).astype(F32)


def in_pair_order(own, other, axis):
    first = (lax.axis_index("seq") & 1) == 0
    return jnp.where(
        first, jnp.concatenate([own, other], axis), jnp.concatenate([other, own], axis)
    )


def half_of(block, axis, which):
    size = block.shape[axis] // 2
    return lax.dynamic_slice_in_dim(block, which * size, size, axis)


def over_pieces(total):
    low = total.astype(BF16)
    low = (low.astype(F32) + xor_send(low, "seq", 2).astype(F32)).astype(BF16)
    return low, xor_send(low, "seq", 1)


def local(
    tokens,
    cotangent,
    images_held,
    piece_rows,
    norm_gain,
    norm_shift,
    qkv_weight,
    qkv_bias,
    out_weight,
    out_bias,
    mlp_gain,
    mlp_shift,
    up_weight,
    up_bias,
    down_weight,
    down_bias,
):
    slot_count, piece_size, model_width = tokens.shape
    n_seq = lax.axis_size("seq")
    n_img = lax.axis_size("img")
    me = lax.axis_index("seq")
    pair_me = me & 1
    own_img = lax.axis_index("img")
    row_count = slot_count * piece_size
    heads_here = HEADS // n_seq
    group = 3 * D // n_seq
    group_width = heads_here * HEAD_DIM
    shard = D // n_img
    ff = up_weight.shape[1]
    ff_half = ff // n_img // 2
    blocks = 3 * heads_here

    rows_of = piece_rows[me ^ jnp.arange(n_seq)]
    key_valid = (jnp.arange(piece_size)[None, :] < rows_of[:, None]).reshape(n_seq * piece_size)
    live_slots = jnp.arange(slot_count) < images_held[0]
    valid_rows = (live_slots[:, None] & key_valid[None, :piece_size]).reshape(row_count)
    valid_rows = jnp.pad(valid_rows, (0, round_up(row_count, 16) - row_count))
    valid_rows = valid_rows.astype(F32)[:, None]
    key_mask = jnp.where(
        key_valid[:, None] | (jnp.arange(LANES) != HEAD_DIM)[None, :], 0.0, NEG
    ).astype(F32)

    small = [norm_gain, norm_shift, out_bias, mlp_gain, mlp_shift, down_bias, qkv_bias, up_bias]
    small = [jnp.pad(v[None], ((0, 0), (0, group - v.shape[0]))) for v in small]
    small.append(jnp.zeros((8, group), BF16))
    my_columns = lax.dynamic_slice_in_dim(qkv_weight, me * group, group, 1)
    first_part, first_arrived = start_gather(jnp.concatenate([my_columns] + small, axis=0))

    pair = xor_send(tokens, "seq", 1)
    across = [xor_send(tokens[0], "seq", 2), xor_send(tokens[1:], "seq", 2)]
    diagonal = [xor_send(part, "seq", 1) for part in across]
    slot_tokens = [[(tokens, 0), (pair, 0), (across[0],), (diagonal[0],)]]
    for slot in range(1, slot_count):
        slot_tokens.append(
            [(tokens, slot), (pair, slot), (across[1], slot - 1), (diagonal[1], slot - 1)]
        )

    my_up = lax.dynamic_index_in_dim(
        up_weight.reshape(shard, n_img, 2, ff_half), pair_me, 2, keepdims=False
    ).reshape(shard, -1)
    my_down = once_there(half_of(down_weight, 0, pair_me), tuple(first_arrived or ()))
    down_own = lax.all_gather(my_down, "img", axis=0).reshape(-1, model_width)

    first_set = end_gather(first_part, first_arrived)
    my_second = jnp.concatenate([my_up, half_of(out_weight, 1, pair_me)], axis=1)
    second_part, second_arrived = start_gather(once_there(my_second, (first_set,)))
    qkv_cols = first_set[:, :shard].reshape(model_width, group)
    params = first_set[:, shard:].astype(F32)

    def param(row, width):
        return params[:, row, : width * shard].reshape(-1)

    gain_first, shift_first, bias_out = param(0, 1)[None], param(1, 1)[None], param(2, 1)[None]
    gain_second, shift_second, bias_down = param(3, 1)[None], param(4, 1)[None], param(5, 1)[None]
    pair_bias, bias_up = param(6, 2), param(7, 4).reshape(n_img, 2, ff_half)
    bias_up = jnp.concatenate(
        [
            lax.dynamic_index_in_dim(bias_up, which, 1, keepdims=False).reshape(1, -1)
            for which in (pair_me, 1 - pair_me)
        ],
        axis=1,
    )

    paired = lax.dynamic_slice_in_dim(
        pair_bias.reshape(HEADS, 2, HEAD_DIM), me * heads_here, heads_here, 0
    )
    head_bias = jnp.concatenate(
        [paired[:, :1], jnp.zeros((heads_here, 1, HEAD_DIM), F32), paired[:, 1:]], axis=1
    ).reshape(1, group)

    slot_normed, slot_qkv, slot_attended = [], [], []
    for slot in range(slot_count):
        after = ()
        if slot > 0:
            after = (slot_attended[-1][0],)
        if slot > 1:
            after = after + tuple(slot_attended[-2][1:])
        normed, qkv_rows, *attended = slot_forward(
            slot_tokens[slot], gain_first, shift_first, qkv_cols, head_bias, key_mask, after
        )
        slot_normed.append(normed)
        slot_qkv.append(qkv_rows)
        slot_attended.append(
            [attended[0]] + [xor_send(attended[r], "seq", r) for r in range(1, n_seq)]
        )
    down_own = once_there(down_own, (slot_attended[-1][0],))
    if second_arrived is not None:
        second_arrived = [once_there(part, (slot_attended[1][0],)) for part in second_arrived]
    sent = tuple(part for parts in slot_attended for part in parts[1:])
    second_set = end_gather(second_part, second_arrived, sent).reshape(model_width, -1)
    up_own, out_own = second_set[:, : ff // 2], second_set[:, ff // 2 :]
    up_other = xor_send(up_own, "seq", 1)
    down_other = xor_send(down_own, "seq", 1)
    out_full = in_pair_order(out_own, xor_send(out_own, "seq", 1), 1)
    out_full = out_full.reshape(n_seq, group_width, model_width)
    out_groups = jnp.stack(
        [lax.dynamic_index_in_dim(out_full, me ^ r, 0, keepdims=False) for r in range(n_seq)]
    )
    attended_groups = [[parts[r] for parts in slot_attended] for r in range(n_seq)]

    layer_out, grad_residual, *rest = feed_forward(
        attended_groups,
        tokens,
        cotangent,
        valid_rows,
        out_groups,
        bias_out,
        gain_second,
        shift_second,
        bias_down,
        up_own,
        up_other,
        bias_up,
        down_own,
        down_other,
    )
    grad_first, grad_rest, rest = rest[:n_seq], rest[n_seq : 2 * n_seq], rest[2 * n_seq :]
    grad_out_groups, vectors, grad_up_own, grad_up_other = rest[:4]
    grad_up_bias, grad_down_own, grad_down_other = rest[4:]
    for r in range(1, n_seq):
        grad_first[r] = xor_send(grad_first[r], "seq", r)
        grad_rest[r] = xor_send(grad_rest[r], "seq", r)
    slot_grads = [[(part,) for part in grad_first]]
    for slot in range(1, slot_count):
        slot_grads.append([(part, slot - 1) for part in grad_rest])

    sent = tuple(grad_first[1:])
    down_sum = once_there(xor_send(grad_down_other, "seq", 1), sent).astype(F32)
    down_sum = grad_down_own.astype(F32) + down_sum
    up_sum = once_there(xor_send(grad_up_other, "seq", 1), sent).astype(F32)
    up_sum = grad_up_own.astype(F32) + up_sum
    grad_out_weight = jnp.concatenate(
        [lax.dynamic_index_in_dim(grad_out_groups, me ^ r, 0, keepdims=False) for r in range(n_seq)],
        axis=0,
    )
    out_sum = half_of(grad_out_weight, 1, pair_me).astype(F32) + xor_send(
        half_of(grad_out_weight, 1, 1 - pair_me), "seq", 1
    ).astype(F32)
    second_grads = jnp.concatenate(
        [up_sum.astype(BF16), out_sum.astype(BF16), down_sum.astype(BF16).reshape(model_width, -1)],
        axis=1,
    ).reshape(n_img, shard, -1)
    own_second = scatter_img(second_grads)

    grad_columns = jnp.zeros((model_width, group), F32)
    bias_sums = jnp.zeros((group,), F32)
    norm_sums = jnp.zeros((8, model_width), F32)
    own_sums, arrivals = [], []
    for slot in range(slot_count):
        after = (second_grads,) if slot == 0 else ()
        if slot > 1:
            after = (arrivals[-2][1],)
        own, across, pairs, grad_columns, slot_norm, slot_bias = slot_backward(
            slot_grads[slot],
            slot_tokens[slot],
            slot_qkv[slot],
            slot_normed[slot],
            qkv_cols,
            grad_columns,
            after,
        )
        norm_sums += slot_norm
        bias_sums += slot_bias[0]
        pairs = xor_send(pairs, "seq", 1)
        across = xor_send((across + pairs[1].astype(F32)).astype(BF16), "seq", 2)
        own_sums.append(own + pairs[0].astype(F32) + across.astype(F32))
        arrivals.append((pairs, across))
    bias_sums = bias_sums.reshape(heads_here, 3, HEAD_DIM)
    grad_pairs = jnp.concatenate([bias_sums[:, :1], bias_sums[:, 2:]], axis=1).reshape(-1)
    grad_pairs = lax.dynamic_update_slice_in_dim(
        jnp.zeros((2 * D,), F32), grad_pairs, me * grad_pairs.shape[0], 0
    )
    up_halves = grad_up_bias.reshape(2, n_img, 1, ff_half)
    grad_up_bias = in_pair_order(up_halves[0], up_halves[1], 1).reshape(-1)
    all_vectors = [
        norm_sums[0],
        norm_sums[1],
        grad_pairs,
        vectors[2],
        vectors[0],
        vectors[1],
        grad_up_bias,
        vectors[3],
    ]
    extra = jnp.concatenate([v.reshape(n_img, -1) for v in all_vectors], axis=1)
    extra_rows = -(-extra.shape[1] // group)
    extra = jnp.pad(extra, ((0, 0), (0, extra_rows * group - extra.shape[1])))
    extra = jnp.pad(
        extra.reshape(n_img, extra_rows, group), ((0, 0), (0, 16 - extra_rows), (0, 0))
    )
    columns = jnp.concatenate([grad_columns.reshape(n_img, shard, group), extra], axis=1)
    columns = once_there(columns.astype(BF16), (arrivals[-2][0],))
    if few_devices():
        own_columns = reduce_outer(once_there(reduce_inner(columns), (own_second, pairs)))
    else:
        own_columns = scatter_img(columns)
    own_columns = own_columns.astype(BF16)

    grad_norm_first = jnp.concatenate(own_sums, axis=0)
    unit, factor = normalize(tokens.reshape(row_count, model_width).astype(F32))
    scaled = grad_norm_first * gain_first
    mean_scaled = jnp.mean(scaled, axis=-1, keepdims=True)
    mean_product = jnp.mean(scaled * unit, axis=-1, keepdims=True)
    grad_inputs = factor * (scaled - mean_scaled - unit * mean_product)
    tokens_grad = grad_residual + grad_inputs.reshape(grad_residual.shape)

    by_sender = jnp.stack(
        [own_columns] + [xor_send(own_columns, "seq", r) for r in range(1, n_seq)]
    )
    by_sender = [
        lax.dynamic_index_in_dim(by_sender, me ^ g, 0, keepdims=False) for g in range(n_seq)
    ]
    share_qkv = jnp.concatenate([part[:shard] for part in by_sender], axis=1).astype(F32)
    mine = sum(part[shard : shard + extra_rows].astype(F32) for part in by_sender).reshape(-1)
    second_low, second_other = over_pieces(own_second)
    cuts = (ff // 2, ff // 2 + model_width // 2)
    up_low, out_low, down_low = jnp.split(second_low, cuts, axis=1)
    up_there, out_there, down_there = jnp.split(second_other, cuts, axis=1)
    up_low = up_low.reshape(shard, n_img, 1, ff_half)
    up_there = up_there.reshape(shard, n_img, 1, ff_half)
    share_up = in_pair_order(up_low, up_there, 2).reshape(shard, ff).astype(F32)
    share_out = in_pair_order(out_low, out_there, 1).astype(F32)
    down_low = down_low.reshape(ff_half, model_width)
    down_there = down_there.reshape(ff_half, model_width)
    share_down = in_pair_order(down_low, down_there, 0).astype(F32)

    shares, at = [], 0
    for v in all_vectors:
        size = v.shape[0] // n_img
        shares.append(mine[at : at + size])
        at += size
    return (
        layer_out,
        tokens_grad,
        shares[0],
        shares[1],
        share_qkv,
        shares[2],
        share_out,
        shares[3],
        shares[4],
        shares[5],
        share_up,
        shares[6],
        share_down,
        shares[7],
    )


def solution(mesh):
    placed = (
        P("img", "seq", None),
        P("img", "seq", None),
        P("img"),
        P(),
        P("img"),
        P("img"),
        P("img", None),
        P("img"),
        P("img", None),
        P("img"),
        P("img"),
        P("img"),
        P("img", None),
        P("img"),
        P("img", None),
        P("img"),
    )
    return jax.shard_map(
        local,
        mesh=mesh,
        in_specs=placed,
        out_specs=(
            P("img", "seq", None),
            P("img", "seq", None),
            P("img"),
            P("img"),
            P("img", None),
            P("img"),
            P("img", None),
            P("img"),
            P("img"),
            P("img"),
            P("img", None),
            P("img"),
            P("img", None),
            P("img"),
        ),
        check_vma=False,
    )
```

```python
from functools import partial

import jax
import jax.numpy as jnp
import numpy as np
from jax import lax
from jax.experimental import pallas as pl
from jax.experimental.pallas import tpu as pltpu
from jax.sharding import PartitionSpec as P

D = 768
HEADS = 12
HEAD_DIM = 64
EPS = 1e-06
NEG = -1e30
LANES = 128
F32 = jnp.float32
BF16 = jnp.bfloat16
VMEM_BYTES = 60 * 1024 * 1024
def cost(giga_flops):
    return pl.CostEstimate(
        flops=giga_flops * 10**9, bytes_accessed=10**7, transcendentals=10**6
    )


def mm(left, right, left_dim=1, right_dim=0):
    return lax.dot_general(
        left, right, (((left_dim,), (right_dim,)), ((), ())), preferred_element_type=F32
    )


def normalize(features):
    row_mean = jnp.mean(features, axis=-1, keepdims=True)
    centred = features - row_mean
    spread = jnp.mean(centred * centred, axis=-1, keepdims=True)
    factor = lax.rsqrt(spread + EPS)
    return centred * factor, factor


def round_up(size, unit):
    return -(-size // unit) * unit


def head_columns(heads, parts):
    place = np.zeros((heads * parts, LANES, heads * parts * HEAD_DIM), np.float32)
    for b in range(heads * parts):
        for d in range(HEAD_DIM):
            place[b, d, b * HEAD_DIM + d] = 1.0
    return jnp.asarray(place, BF16)


def lane_columns(heads):
    pick = np.zeros((3 * heads, LANES, LANES), np.float32)
    ones = np.zeros((3 * heads, 1, LANES), np.float32)
    for b in range(3 * heads):
        start = b * HEAD_DIM % LANES
        for d in range(HEAD_DIM):
            pick[b, start + d, d] = HEAD_DIM**-0.5 if b % 3 == 0 else 1.0
        if b % 3 != 1:
            ones[b, 0, HEAD_DIM] = 1.0
    return jnp.asarray(pick, BF16), jnp.asarray(ones, F32)


def query_block(rows):
    for size in range(min(rows, 400) // 16 * 16, 15, -16):
        if rows % size == 0:
            return size
    return rows


def after_specs(after):
    return [pl.BlockSpec(memory_space=pl.ANY)] * len(after)


def piece_spec(array, *at):
    rest = array.shape[len(at) :]
    return pl.BlockSpec((None,) * len(at) + rest, lambda i: at + (0,) * len(rest))


def piece_specs(pieces):
    return [piece_spec(*piece) for piece in pieces]


def whole_specs(count):
    return [pl.BlockSpec(memory_space=pltpu.VMEM)] * count


def forward_kernel(n_seq, heads, n_after, *refs):
    tokens, refs = refs[:n_seq], refs[n_seq + n_after :]
    gain, shift, weight, bias, key_mask, pick, ones, place = refs[:8]
    normed_out, qkv_out = refs[8:10]
    attended_out, (rows, attended) = refs[10 : 10 + n_seq], refs[10 + n_seq :]
    piece = tokens[0].shape[0]
    total = n_seq * piece
    for r in range(n_seq):
        unit, _ = normalize(tokens[r][...].astype(F32))
        rows[r * piece : (r + 1) * piece, :] = unit * gain[...] + shift[...]
    normed = rows[...].astype(BF16)
    normed_out[...] = normed
    qkv = (mm(normed, weight[...]) + bias[...]).astype(BF16)
    width = qkv.shape[1]
    block = query_block(total)
    pad = qkv_out.shape[1] - total
    parts = []
    for b in range(3 * heads):
        start = b * HEAD_DIM // LANES * LANES
        size = min(LANES, width - start)
        part = mm(qkv[:, start : start + size], pick[b, :size]) + ones[b]
        if b % 3 == 1:
            part = part + key_mask[...]
        part = part.astype(BF16)
        qkv_out[b, :total] = part
        if pad:
            qkv_out[b, total:] = jnp.zeros((pad, LANES), BF16)
        parts.append(part)

    tasks = [(at, h) for at in range(0, total, block) for h in range(heads)]

    def score(task):
        at, h = task
        return mm(parts[3 * h][at : at + block], parts[3 * h + 1], 1, 1)

    scores = score(tasks[0])
    placed = None
    for index, (at, h) in enumerate(tasks):
        following = score(tasks[index + 1]) if index + 1 < len(tasks) else None
        peak = jnp.max(scores, axis=-1, keepdims=True)
        terms = jnp.exp(scores - peak).astype(BF16)
        weighted = mm(terms, parts[3 * h + 2])
        result = (weighted / weighted[:, HEAD_DIM : HEAD_DIM + 1]).astype(BF16)
        here = mm(result, place[h])
        placed = here if h == 0 else placed + here
        if h == heads - 1:
            attended[at : at + block, :] = placed
        scores = following
    for r in range(n_seq):
        attended_out[r][...] = attended[r * piece : (r + 1) * piece, :].astype(BF16)


def slot_forward(pieces, gain, shift, weight, bias, key_mask, after=()):
    n_seq = len(pieces)
    piece, width = pieces[0][0].shape[-2:]
    heads = weight.shape[1] // (3 * HEAD_DIM)
    total = n_seq * piece
    padded = round_up(total, LANES)
    return pl.pallas_call(
        partial(forward_kernel, n_seq, heads, len(after)),
        grid=(1,),
        in_specs=piece_specs(pieces) + after_specs(after) + whole_specs(8),
        out_shape=(
            jax.ShapeDtypeStruct((total, width), BF16),
            jax.ShapeDtypeStruct((3 * heads, padded, LANES), BF16),
            *[jax.ShapeDtypeStruct((piece, heads * HEAD_DIM), BF16)] * n_seq,
        ),
        scratch_shapes=[
            pltpu.VMEM((total, width), F32),
            pltpu.VMEM((total, heads * HEAD_DIM), F32),
        ],
        compiler_params=pltpu.CompilerParams(vmem_limit_bytes=36 * 1024 * 1024),
        cost_estimate=cost(14),
        name="slot_forward",
    )(
        *[p[0] for p in pieces], *after, gain, shift, weight, bias, key_mask, *lane_columns(heads),
        head_columns(heads, 1),
    )


def backward_kernel(n_seq, heads, n_after, *refs):
    grads, refs = refs[:n_seq], refs[n_seq + n_after :]
    tokens, refs = refs[:n_seq], refs[n_seq:]
    qkv, normed, weight, before, place, spread = refs[:6]
    own, across, pairs, grad_weight, vectors, grad_bias, rows, wide = refs[6:]
    piece = grads[0].shape[0]
    total = n_seq * piece
    padded = qkv.shape[1]
    for r in range(n_seq):
        rows[r * piece : (r + 1) * piece, :] = grads[r][...].astype(F32)
    if padded > total:
        rows[total:, :] = jnp.zeros((padded - total, rows.shape[1]), F32)
    grad_rows = rows[...].astype(BF16)
    grad_heads = [mm(grad_rows, place[h], 1, 1).astype(BF16) for h in range(heads)]
    block = 4 * LANES
    tasks = [(h, at) for h in range(heads) for at in range(0, padded, block)]

    def products(task):
        h, at = task
        end = min(at + block, padded)
        scores = mm(qkv[3 * h + 1, :total], qkv[3 * h, at:end], 1, 1)
        return scores, mm(qkv[3 * h + 2, :total], grad_heads[h][at:end], 1, 1)

    current = products(tasks[0])
    grad_qkv = None
    for index, (h, at) in enumerate(tasks):
        following = products(tasks[index + 1]) if index + 1 < len(tasks) else None
        if at == 0:
            keys_t = jnp.transpose(qkv[3 * h + 1])[:, :total]
            grad_keys = jnp.zeros((total, LANES), F32)
            grad_values = jnp.zeros((total, LANES), F32)
            grad_queries = []
        end = min(at + block, padded)
        scores, grad_probs = current
        peak = jnp.max(scores, axis=0, keepdims=True)
        terms = jnp.exp(scores - peak)
        probs = terms * (1.0 / jnp.sum(terms, axis=0, keepdims=True))
        inner = jnp.sum(probs * grad_probs, axis=0, keepdims=True)
        grad_scores = (probs * (grad_probs - inner)).astype(BF16)
        grad_values = grad_values + mm(probs.astype(BF16), grad_heads[h][at:end])
        grad_keys = grad_keys + mm(grad_scores, qkv[3 * h, at:end])
        grad_queries.append(jnp.transpose(mm(keys_t, grad_scores)))
        if end == padded:
            queries = jnp.concatenate(grad_queries, axis=0)[:total] * (HEAD_DIM**-0.5)
            for t, part in enumerate((queries, grad_keys, grad_values)):
                placed = mm(part.astype(BF16), spread[3 * h + t])
                grad_qkv = placed if grad_qkv is None else grad_qkv + placed
        current = following
    grad_low = grad_qkv.astype(BF16)
    grad_bias[...] = jnp.broadcast_to(
        jnp.sum(grad_low.astype(F32), axis=0, keepdims=True), grad_bias.shape
    )
    grad_weight[...] = before[...] + mm(normed[...], grad_low, 0, 0)
    wide[...] = mm(grad_low, weight[...], 1, 1)
    by_unit = jnp.zeros((1, wide.shape[1]), F32)
    by_one = jnp.zeros((1, wide.shape[1]), F32)
    for r in range(n_seq):
        share = wide[r * piece : (r + 1) * piece, :]
        unit, _ = normalize(tokens[r][...].astype(F32))
        by_unit = by_unit + jnp.sum(share * unit, axis=0, keepdims=True)
        by_one = by_one + jnp.sum(share, axis=0, keepdims=True)
        if r & 1:
            pairs[r // 2] = share.astype(BF16)
        else:
            (own if r == 0 else across)[...] = share
    vectors[...] = jnp.zeros(vectors.shape, F32)
    vectors[0:1, :] = by_unit
    vectors[1:2, :] = by_one


def slot_backward(grads, tokens, qkv, normed, weight, before, after=()):
    n_seq = len(grads)
    piece, width = grads[0][0].shape[-2:]
    heads = qkv.shape[0] // 3
    total = n_seq * piece
    model = normed.shape[1]
    return pl.pallas_call(
        partial(backward_kernel, n_seq, heads, len(after)),
        grid=(1,),
        in_specs=piece_specs(grads) + after_specs(after) + piece_specs(tokens) + whole_specs(6),
        out_shape=(
            jax.ShapeDtypeStruct((piece, model), F32),
            jax.ShapeDtypeStruct((piece, model), F32),
            jax.ShapeDtypeStruct((n_seq // 2, piece, model), BF16),
            jax.ShapeDtypeStruct((model, 3 * width), F32),
            jax.ShapeDtypeStruct((8, model), F32),
            jax.ShapeDtypeStruct((8, 3 * width), F32),
        ),
        scratch_shapes=[
            pltpu.VMEM((qkv.shape[1], width), F32),
            pltpu.VMEM((total, model), F32),
        ],
        compiler_params=pltpu.CompilerParams(vmem_limit_bytes=VMEM_BYTES),
        cost_estimate=cost(0),
        name="slot_backward",
    )(
        *[g[0] for g in grads], *after, *[t[0] for t in tokens], qkv, normed, weight, before,
        head_columns(heads, 1), head_columns(heads, 3),
    )


def gate_kernel(*refs):
    pass


def once_there(array, after):
    if not after:
        return array
    return pl.pallas_call(
        gate_kernel,
        in_specs=after_specs((array,) + tuple(after)),
        out_specs=pl.BlockSpec(memory_space=pl.ANY),
        out_shape=jax.ShapeDtypeStruct(array.shape, array.dtype),
        input_output_aliases={0: 0},
        name="once_there",
    )(array, *after)


def mlp_kernel(slots, groups, *refs):
    attended, refs = refs[: slots * groups], refs[slots * groups :]
    (
        tokens, cotangent, valid, out_weight, bias_out, gain, shift, bias_down, up_own, up_other,
        bias_up, down_own, down_other, layer_out, grad_residual,
    ) = refs[:15]
    grad_first, refs = refs[15 : 15 + groups], refs[15 + groups :]
    grad_rest, refs = refs[:groups], refs[groups:]
    (
        grad_out_weight, vectors, grad_up_own, grad_up_other, grad_up_bias, grad_down_own,
        grad_down_other, staged, residual, output, grad_norm, normed, normed_t, grad_out, heads_in,
    ) = refs
    step = pl.program_id(0)
    piece, width = tokens.shape[1:]
    head_width = attended[0].shape[-1]
    rows = slots * piece
    padded = residual.shape[0]

    def stage(source):
        for s in range(slots):
            staged[s * piece : (s + 1) * piece, : source.shape[-1]] = source[s].astype(F32)

    @pl.when(step == 0)
    def _():
        if padded > rows:
            staged[rows:, :] = jnp.zeros((padded - rows, width), F32)
        for r in range(groups):
            for s in range(slots):
                staged[s * piece : (s + 1) * piece, :head_width] = attended[r * slots + s][
                    ...
                ].astype(F32)
            heads_in[r] = staged[:, :head_width].astype(BF16)
        stage(cotangent)
        grad_out[...] = (staged[...] * valid[...]).astype(BF16)
        stage(tokens)
        total = staged[...] + bias_out[...]
        for r in range(groups):
            total = total + mm(heads_in[r], out_weight[r])
        residual[...] = total
        unit, _ = normalize(total)
        normed_here = (unit * gain[...] + shift[...]).astype(BF16)
        normed[...] = normed_here
        normed_t[...] = jnp.transpose(normed_here)
        output[...] = total + bias_down[...]
        grad_norm[...] = jnp.zeros_like(grad_norm)

    first = step < pl.num_programs(0) // 2
    up = jnp.where(first, up_own[...], up_other[...])
    down = jnp.where(first, down_own[...], down_other[...])
    hidden = mm(normed[...], up) + bias_up[...]
    share = 0.5 * (1.0 + lax.erf(hidden * np.float32(np.sqrt(0.5))))
    density = jnp.exp(-0.5 * hidden * hidden) * np.float32(1.0 / np.sqrt(2.0 * np.pi))
    activated = (hidden * share).astype(BF16)
    grad_hidden = (mm(grad_out[...], down, 1, 1) * (share + hidden * density)).astype(BF16)
    output[...] += mm(activated, down)
    grad_norm[...] += mm(grad_hidden, up, 1, 1)
    grad_up = mm(normed_t[...], grad_hidden).astype(BF16)
    grad_down = mm(activated, grad_out[...], 0, 0).astype(BF16)

    @pl.when(first)
    def _():
        grad_up_own[...] = grad_up
        grad_down_own[...] = grad_down

    @pl.when(jnp.logical_not(first))
    def _():
        grad_up_other[...] = grad_up
        grad_down_other[...] = grad_down

    grad_up_bias[...] = jnp.sum(grad_hidden.astype(F32), axis=0, keepdims=True)

    @pl.when(step == pl.num_programs(0) - 1)
    def _():
        staged[...] = output[...] * valid[...]
        for s in range(slots):
            layer_out[s] = staged[s * piece : (s + 1) * piece, :].astype(BF16)
        grad_low = grad_out[...].astype(F32)
        unit, factor = normalize(residual[...])
        back = grad_norm[...]
        scaled = back * gain[...]
        mean_scaled = jnp.mean(scaled, axis=-1, keepdims=True)
        mean_product = jnp.mean(scaled * unit, axis=-1, keepdims=True)
        total = grad_low + factor * (scaled - mean_scaled - unit * mean_product)
        staged[...] = total
        for s in range(slots):
            grad_residual[s] = staged[s * piece : (s + 1) * piece, :]
        branch = total.astype(BF16)
        vectors[0:1, :] = jnp.sum(back * unit, axis=0, keepdims=True)
        vectors[1:2, :] = jnp.sum(back, axis=0, keepdims=True)
        vectors[2:3, :] = jnp.sum(branch.astype(F32), axis=0, keepdims=True)
        vectors[3:4, :] = jnp.sum(grad_low, axis=0, keepdims=True)
        vectors[4:8, :] = jnp.zeros((4, width), F32)
        for r in range(groups):
            grad_out_weight[r] = mm(heads_in[r], branch, 0, 0).astype(BF16)
            staged[:, :head_width] = mm(branch, out_weight[r], 1, 1)
            grad_first[r][...] = staged[:piece, :head_width].astype(BF16)
            for s in range(1, slots):
                grad_rest[r][s - 1] = staged[s * piece : (s + 1) * piece, :head_width].astype(BF16)


def feed_forward(
    attended, tokens, cotangent, valid, out_weight, bias_out, gain, shift, bias_down, up_own,
    up_other, bias_up, down_own, down_other,
):
    slots, piece, width = tokens.shape
    groups, head_width = len(attended), attended[0][0].shape[-1]
    first = jax.ShapeDtypeStruct((piece, head_width), BF16)
    others = jax.ShapeDtypeStruct((slots - 1, piece, head_width), BF16)
    ff = 2 * up_own.shape[1]
    chunk = 384
    half = ff // 2 // chunk
    padded = round_up(slots * piece, 16)
    whole = lambda shape: pl.BlockSpec(
        shape, lambda i: (0,) * len(shape), pipeline_mode=pl.Buffered(1)
    )
    own = lambda i: jnp.minimum(i, half - 1)
    other = lambda i: jnp.maximum(i - half, 0)
    by_columns = [pl.BlockSpec((width, chunk), lambda i, at=at: (0, at(i))) for at in (own, other)]
    by_rows = [pl.BlockSpec((chunk, width), lambda i, at=at: (at(i), 0)) for at in (own, other)]
    bias_block = pl.BlockSpec((1, chunk), lambda i: (0, i))
    row = whole((1, width))
    return pl.pallas_call(
        partial(mlp_kernel, slots, groups),
        grid=(ff // chunk,),
        in_specs=[
            *[whole(first.shape)] * (groups * slots),
            whole(tokens.shape),
            whole(cotangent.shape),
            whole((padded, 1)),
            whole(out_weight.shape),
            row,
            row,
            row,
            row,
            *by_columns,
            bias_block,
            *by_rows,
        ],
        out_specs=[
            whole(tokens.shape),
            whole(tokens.shape),
            *[whole(first.shape)] * groups,
            *[whole(others.shape)] * groups,
            whole(out_weight.shape),
            whole((8, width)),
            *by_columns,
            bias_block,
            *by_rows,
        ],
        out_shape=[
            jax.ShapeDtypeStruct(tokens.shape, BF16),
            jax.ShapeDtypeStruct(tokens.shape, F32),
            *[first] * groups,
            *[others] * groups,
            jax.ShapeDtypeStruct(out_weight.shape, BF16),
            jax.ShapeDtypeStruct((8, width), F32),
            jax.ShapeDtypeStruct(up_own.shape, BF16),
            jax.ShapeDtypeStruct(up_own.shape, BF16),
            jax.ShapeDtypeStruct((1, ff), F32),
            jax.ShapeDtypeStruct(down_own.shape, BF16),
            jax.ShapeDtypeStruct(down_own.shape, BF16),
        ],
        scratch_shapes=[
            pltpu.VMEM((padded, width), F32),
            pltpu.VMEM((padded, width), F32),
            pltpu.VMEM((padded, width), F32),
            pltpu.VMEM((padded, width), F32),
            pltpu.VMEM((padded, width), BF16),
            pltpu.VMEM((width, padded), BF16),
            pltpu.VMEM((padded, width), BF16),
            pltpu.VMEM((groups, padded, head_width), BF16),
        ],
        compiler_params=pltpu.CompilerParams(
            vmem_limit_bytes=VMEM_BYTES, dimension_semantics=("arbitrary",)
        ),
        cost_estimate=cost(55),
        name="feed_forward",
    )(
        *[part for group in attended for part in group], tokens, cotangent, valid, out_weight, bias_out, gain, shift, bias_down, up_own,
        up_other, bias_up, down_own, down_other,
    )


def xor_send(block, axis, bits):
    n = lax.axis_size(axis)
    return lax.ppermute(block, axis, [(i, i ^ bits) for i in range(n)])


INNER = 2


def outer_send(block, shift):
    outer = lax.axis_size("img") // INNER
    return lax.ppermute(
        block,
        "img",
        [
            (z * INNER + y, ((z + shift) % outer) * INNER + y)
            for z in range(outer)
            for y in range(INNER)
        ],
    )


def few_devices():
    return lax.axis_size("img") <= 16


def place_outer(block, arrived):
    outer = lax.axis_size("img") // INNER
    z = lax.axis_index("img") // INNER
    placed = jnp.zeros((outer,) + block.shape, block.dtype)
    for k, part in enumerate([block] + arrived):
        placed = lax.dynamic_update_slice_in_dim(placed, part[None], (z + outer - k) % outer, 0)
    return placed


def gather_inner(placed, after=()):
    other = once_there(xor_send(placed, "img", 1), after)
    first = (lax.axis_index("img") & 1) == 0
    both = jnp.stack([jnp.where(first, placed, other), jnp.where(first, other, placed)], axis=1)
    return both.reshape((-1,) + placed.shape[1:])


def start_gather(block):
    if not few_devices():
        return lax.all_gather(block, "img", axis=0), None
    outer = lax.axis_size("img") // INNER
    return block, [outer_send(block, k) for k in range(1, outer)]


def end_gather(block, arrived, after=()):
    if arrived is None:
        return block
    return gather_inner(place_outer(block, arrived), after)


def reduce_inner(parts):
    outer = lax.axis_size("img") // INNER
    split = parts.reshape((outer, INNER) + parts.shape[1:])
    me = lax.axis_index("img") % INNER
    send = lax.dynamic_index_in_dim(split, 1 - me, 1, keepdims=False)
    keep = lax.dynamic_index_in_dim(split, me, 1, keepdims=False)
    return keep.astype(F32) + xor_send(send, "img", 1).astype(F32)


def reduce_outer(sums):
    outer = sums.shape[0]
    z = lax.axis_index("img") // INNER
    total = lax.dynamic_index_in_dim(sums, z, 0, keepdims=False)
    for k in range(1, outer):
        send = lax.dynamic_index_in_dim(sums, (z + k) % outer, 0, keepdims=False)
        total = total + outer_send(send.astype(BF16), k).astype(F32)
    return total


def scatter_img(parts):
    return lax.psum_scatter(parts, "img", scatter_dimension=0, tiled=False).astype(F32)


def in_pair_order(own, other, axis):
    first = (lax.axis_index("seq") & 1) == 0
    return jnp.where(
        first, jnp.concatenate([own, other], axis), jnp.concatenate([other, own], axis)
    )


def half_of(block, axis, which):
    size = block.shape[axis] // 2
    return lax.dynamic_slice_in_dim(block, which * size, size, axis)


def over_pieces(total):
    low = total.astype(BF16)
    low = (low.astype(F32) + xor_send(low, "seq", 2).astype(F32)).astype(BF16)
    return low, xor_send(low, "seq", 1)


def local(
    tokens,
    cotangent,
    images_held,
    piece_rows,
    norm_gain,
    norm_shift,
    qkv_weight,
    qkv_bias,
    out_weight,
    out_bias,
    mlp_gain,
    mlp_shift,
    up_weight,
    up_bias,
    down_weight,
    down_bias,
):
    slot_count, piece_size, model_width = tokens.shape
    n_seq = lax.axis_size("seq")
    n_img = lax.axis_size("img")
    me = lax.axis_index("seq")
    pair_me = me & 1
    own_img = lax.axis_index("img")
    row_count = slot_count * piece_size
    heads_here = HEADS // n_seq
    group = 3 * D // n_seq
    group_width = heads_here * HEAD_DIM
    shard = D // n_img
    ff = up_weight.shape[1]
    ff_half = ff // n_img // 2
    blocks = 3 * heads_here

    rows_of = piece_rows[me ^ jnp.arange(n_seq)]
    key_valid = (jnp.arange(piece_size)[None, :] < rows_of[:, None]).reshape(n_seq * piece_size)
    live_slots = jnp.arange(slot_count) < images_held[0]
    valid_rows = (live_slots[:, None] & key_valid[None, :piece_size]).reshape(row_count)
    valid_rows = jnp.pad(valid_rows, (0, round_up(row_count, 16) - row_count))
    valid_rows = valid_rows.astype(F32)[:, None]
    key_mask = jnp.where(
        key_valid[:, None] | (jnp.arange(LANES) != HEAD_DIM)[None, :], 0.0, NEG
    ).astype(F32)

    small = [norm_gain, norm_shift, out_bias, mlp_gain, mlp_shift, down_bias, qkv_bias, up_bias]
    small = [jnp.pad(v[None], ((0, 0), (0, group - v.shape[0]))) for v in small]
    small.append(jnp.zeros((8, group), BF16))
    my_columns = lax.dynamic_slice_in_dim(qkv_weight, me * group, group, 1)
    first_part, first_arrived = start_gather(jnp.concatenate([my_columns] + small, axis=0))

    pair = xor_send(tokens, "seq", 1)
    across = [xor_send(tokens[0], "seq", 2), xor_send(tokens[1:], "seq", 2)]
    diagonal = [xor_send(part, "seq", 1) for part in across]
    slot_tokens = [[(tokens, 0), (pair, 0), (across[0],), (diagonal[0],)]]
    for slot in range(1, slot_count):
        slot_tokens.append(
            [(tokens, slot), (pair, slot), (across[1], slot - 1), (diagonal[1], slot - 1)]
        )

    my_up = lax.dynamic_index_in_dim(
        up_weight.reshape(shard, n_img, 2, ff_half), pair_me, 2, keepdims=False
    ).reshape(shard, -1)
    my_down = once_there(half_of(down_weight, 0, pair_me), tuple(first_arrived or ()))
    down_own = lax.all_gather(my_down, "img", axis=0).reshape(-1, model_width)

    first_set = end_gather(first_part, first_arrived)
    my_second = jnp.concatenate([my_up, half_of(out_weight, 1, pair_me)], axis=1)
    second_part, second_arrived = start_gather(once_there(my_second, (first_set,)))
    qkv_cols = first_set[:, :shard].reshape(model_width, group)
    params = first_set[:, shard:].astype(F32)

    def param(row, width):
        return params[:, row, : width * shard].reshape(-1)

    gain_first, shift_first, bias_out = param(0, 1)[None], param(1, 1)[None], param(2, 1)[None]
    gain_second, shift_second, bias_down = param(3, 1)[None], param(4, 1)[None], param(5, 1)[None]
    pair_bias, bias_up = param(6, 2), param(7, 4).reshape(n_img, 2, ff_half)
    bias_up = jnp.concatenate(
        [
            lax.dynamic_index_in_dim(bias_up, which, 1, keepdims=False).reshape(1, -1)
            for which in (pair_me, 1 - pair_me)
        ],
        axis=1,
    )

    paired = lax.dynamic_slice_in_dim(
        pair_bias.reshape(HEADS, 2, HEAD_DIM), me * heads_here, heads_here, 0
    )
    head_bias = jnp.concatenate(
        [paired[:, :1], jnp.zeros((heads_here, 1, HEAD_DIM), F32), paired[:, 1:]], axis=1
    ).reshape(1, group)

    slot_normed, slot_qkv, slot_attended = [], [], []
    for slot in range(slot_count):
        after = ()
        if slot > 0:
            after = (slot_attended[-1][0],)
        if slot > 1:
            after = after + tuple(slot_attended[-2][1:])
        normed, qkv_rows, *attended = slot_forward(
            slot_tokens[slot], gain_first, shift_first, qkv_cols, head_bias, key_mask, after
        )
        slot_normed.append(normed)
        slot_qkv.append(qkv_rows)
        slot_attended.append(
            [attended[0]] + [xor_send(attended[r], "seq", r) for r in range(1, n_seq)]
        )
    down_own = once_there(down_own, (slot_attended[-1][0],))
    if second_arrived is not None:
        second_arrived = [once_there(part, (slot_attended[1][0],)) for part in second_arrived]
    sent = tuple(part for parts in slot_attended for part in parts[1:])
    second_set = end_gather(second_part, second_arrived, sent).reshape(model_width, -1)
    up_own, out_own = second_set[:, : ff // 2], second_set[:, ff // 2 :]
    up_other = xor_send(up_own, "seq", 1)
    down_other = xor_send(down_own, "seq", 1)
    out_full = in_pair_order(out_own, xor_send(out_own, "seq", 1), 1)
    out_full = out_full.reshape(n_seq, group_width, model_width)
    out_groups = jnp.stack(
        [lax.dynamic_index_in_dim(out_full, me ^ r, 0, keepdims=False) for r in range(n_seq)]
    )
    attended_groups = [[parts[r] for parts in slot_attended] for r in range(n_seq)]

    layer_out, grad_residual, *rest = feed_forward(
        attended_groups,
        tokens,
        cotangent,
        valid_rows,
        out_groups,
        bias_out,
        gain_second,
        shift_second,
        bias_down,
        up_own,
        up_other,
        bias_up,
        down_own,
        down_other,
    )
    grad_first, grad_rest, rest = rest[:n_seq], rest[n_seq : 2 * n_seq], rest[2 * n_seq :]
    grad_out_groups, vectors, grad_up_own, grad_up_other = rest[:4]
    grad_up_bias, grad_down_own, grad_down_other = rest[4:]
    for r in range(1, n_seq):
        grad_first[r] = xor_send(grad_first[r], "seq", r)
        grad_rest[r] = xor_send(grad_rest[r], "seq", r)
    slot_grads = [[(part,) for part in grad_first]]
    for slot in range(1, slot_count):
        slot_grads.append([(part, slot - 1) for part in grad_rest])

    sent = tuple(grad_first[1:])
    down_sum = once_there(xor_send(grad_down_other, "seq", 1), sent).astype(F32)
    down_sum = grad_down_own.astype(F32) + down_sum
    up_sum = once_there(xor_send(grad_up_other, "seq", 1), sent).astype(F32)
    up_sum = grad_up_own.astype(F32) + up_sum
    grad_out_weight = jnp.concatenate(
        [lax.dynamic_index_in_dim(grad_out_groups, me ^ r, 0, keepdims=False) for r in range(n_seq)],
        axis=0,
    )
    out_sum = half_of(grad_out_weight, 1, pair_me).astype(F32) + xor_send(
        half_of(grad_out_weight, 1, 1 - pair_me), "seq", 1
    ).astype(F32)
    down_sum = down_sum.astype(BF16).reshape(n_img, -1, shard, model_width)
    down_blocks = down_sum.shape[1]
    second_grads = jnp.concatenate(
        [part.astype(BF16).reshape(n_img, shard, -1) for part in (up_sum, out_sum)]
        + [down_sum[:, p] for p in range(down_blocks)],
        axis=2,
    )
    own_second = scatter_img(second_grads)

    grad_columns = jnp.zeros((model_width, group), F32)
    bias_sums = jnp.zeros((group,), F32)
    norm_sums = jnp.zeros((8, model_width), F32)
    own_sums, arrivals = [], []
    for slot in range(slot_count):
        after = (second_grads,) if slot == 0 else ()
        if slot > 1:
            after = (arrivals[-2][1],)
        own, across, pairs, grad_columns, slot_norm, slot_bias = slot_backward(
            slot_grads[slot],
            slot_tokens[slot],
            slot_qkv[slot],
            slot_normed[slot],
            qkv_cols,
            grad_columns,
            after,
        )
        norm_sums += slot_norm
        bias_sums += slot_bias[0]
        pairs = xor_send(pairs, "seq", 1)
        across = (across + pairs[1].astype(F32)).astype(BF16)
        own_sums.append(own + pairs[0].astype(F32))
        if slot < slot_count - 1:
            across = xor_send(across, "seq", 2)
            own_sums[-1] = own_sums[-1] + across.astype(F32)
        arrivals.append((pairs, across))
    bias_sums = bias_sums.reshape(heads_here, 3, HEAD_DIM)
    grad_pairs = jnp.concatenate([bias_sums[:, :1], bias_sums[:, 2:]], axis=1).reshape(-1)
    grad_pairs = lax.dynamic_update_slice_in_dim(
        jnp.zeros((2 * D,), F32), grad_pairs, me * grad_pairs.shape[0], 0
    )
    up_halves = grad_up_bias.reshape(2, n_img, 1, ff_half)
    grad_up_bias = in_pair_order(up_halves[0], up_halves[1], 1).reshape(-1)
    all_vectors = [
        norm_sums[0],
        norm_sums[1],
        grad_pairs,
        vectors[2],
        vectors[0],
        vectors[1],
        grad_up_bias,
        vectors[3],
    ]
    extra = jnp.concatenate([v.reshape(n_img, -1) for v in all_vectors], axis=1)
    extra_rows = -(-extra.shape[1] // group)
    extra = jnp.pad(extra, ((0, 0), (0, extra_rows * group - extra.shape[1])))
    extra = jnp.pad(
        extra.reshape(n_img, extra_rows, group), ((0, 0), (0, 16 - extra_rows), (0, 0))
    )
    columns = jnp.concatenate([grad_columns.reshape(n_img, shard, group), extra], axis=1)
    columns = once_there(columns.astype(BF16), (own_second, arrivals[-2][0]))
    if few_devices():
        own_columns = reduce_outer(reduce_inner(columns))
    else:
        own_columns = scatter_img(columns)
    own_columns = own_columns.astype(BF16)

    across = xor_send(once_there(arrivals[-1][1], (columns,)), "seq", 2)
    own_sums[-1] = own_sums[-1] + once_there(across, (own_columns,)).astype(F32)

    grad_norm_first = jnp.concatenate(own_sums, axis=0)
    unit, factor = normalize(tokens.reshape(row_count, model_width).astype(F32))
    scaled = grad_norm_first * gain_first
    mean_scaled = jnp.mean(scaled, axis=-1, keepdims=True)
    mean_product = jnp.mean(scaled * unit, axis=-1, keepdims=True)
    grad_inputs = factor * (scaled - mean_scaled - unit * mean_product)
    tokens_grad = grad_residual + grad_inputs.reshape(grad_residual.shape)

    by_sender = jnp.stack(
        [own_columns] + [xor_send(own_columns, "seq", r) for r in range(1, n_seq)]
    )
    by_sender = [
        lax.dynamic_index_in_dim(by_sender, me ^ g, 0, keepdims=False) for g in range(n_seq)
    ]
    share_qkv = jnp.concatenate([part[:shard] for part in by_sender], axis=1).astype(F32)
    mine = sum(part[shard : shard + extra_rows].astype(F32) for part in by_sender).reshape(-1)
    second_low, second_other = over_pieces(own_second)
    cuts = (ff // 2, ff // 2 + model_width // 2)
    up_low, out_low, down_low = jnp.split(second_low, cuts, axis=1)
    up_there, out_there, down_there = jnp.split(second_other, cuts, axis=1)
    up_low = up_low.reshape(shard, n_img, 1, ff_half)
    up_there = up_there.reshape(shard, n_img, 1, ff_half)
    share_up = in_pair_order(up_low, up_there, 2).reshape(shard, ff).astype(F32)
    share_out = in_pair_order(out_low, out_there, 1).astype(F32)
    down_low, down_there = (
        jnp.concatenate(jnp.split(part, down_blocks, axis=1), axis=0)
        for part in (down_low, down_there)
    )
    share_down = in_pair_order(down_low, down_there, 0).astype(F32)

    shares, at = [], 0
    for v in all_vectors:
        size = v.shape[0] // n_img
        shares.append(mine[at : at + size])
        at += size
    return (
        layer_out,
        tokens_grad,
        shares[0],
        shares[1],
        share_qkv,
        shares[2],
        share_out,
        shares[3],
        shares[4],
        shares[5],
        share_up,
        shares[6],
        share_down,
        shares[7],
    )


def solution(mesh):
    placed = (
        P("img", "seq", None),
        P("img", "seq", None),
        P("img"),
        P(),
        P("img"),
        P("img"),
        P("img", None),
        P("img"),
        P("img", None),
        P("img"),
        P("img"),
        P("img"),
        P("img", None),
        P("img"),
        P("img", None),
        P("img"),
    )
    return jax.shard_map(
        local,
        mesh=mesh,
        in_specs=placed,
        out_specs=(
            P("img", "seq", None),
            P("img", "seq", None),
            P("img"),
            P("img"),
            P("img", None),
            P("img"),
            P("img", None),
            P("img"),
            P("img"),
            P("img"),
            P("img", None),
            P("img"),
            P("img", None),
            P("img"),
        ),
        check_vma=False,
    )
```
